512 devices in a mesh: body: 2 (over core), gx: 16 (over z), gy: 16 (over x, y).
Axes of the slice: x: 4, y: 4, z: 16, core: 2. Of those that a mesh axis runs over, the one named last changes fastest.
Arguments:
- disp: float32 [2, 3, 128, 512, 128], P('body', None, 'gx', 'gy'), may hold values from -4 to 4
- force: float32 [2, 3, 128, 512, 128], P('body', None, 'gx', 'gy'), may hold values from -12 to 12
- kappa: float32 [2, 128, 512, 128], P('body', 'gx', 'gy'), may hold values from 0.05 to 0.5
- sigma: float32 [2, 128, 512, 128], P('body', 'gx', 'gy'), may hold values from 0.2 to 1
- gap0: float32 [512, 128], P(('gx', 'gy')), may hold values from -3 to 3
- pressure: float32 [512, 128], P(('gx', 'gy')), may hold values from 0 to 1
- mortar: float32 [512, 128, 128], P(('gx', 'gy')), may hold values from -0.5 to 0.5
- partner: int32 [512], P(('gx', 'gy')), may hold values from 0 to 31
- active: int32 [512], P(('gx', 'gy')), may hold values 0 or 1
Outputs:
- increment: float32 [2, 3, 128, 512, 128], P('body', None, 'gx', 'gy')
- new_pressure: float32 [512, 128], P(('gx', 'gy'))
The draws below stay inside these ranges and needn't reach their ends.
Inputs may be any that keep to these rules, and one draw needn't show every extreme that they name: partner numbers a master block of the same gy index: gx index times 2 plus the local block. 1 marks a block of the active contact set.
All inputs are finite; a program needn't handle non-finite values.
Results may differ from the reference program's by a relative error of at most 0.00015.
Values sent between devices are 32-bit elements; how exact they have to be, the bound alone decides.
No kernel may reach another device: no remote copies, remote signals or barrier semaphores. Data moves between devices by JAX's collectives and lax.ppermute only.
A program may use at most 64 MiB of HBM per device.

```python
import math
import jax
import jax.numpy as jnp
from jax import lax

CX = 8
CY = 32
NZ = 128
SBLK = 128
COMP = 3
CG_ITERS = 2
BLK_DEV = 2
ROWBLK = 32
NBLK = 512
NX = 128
NY = 512
N_GX = 16
N_GY = 16


def plant(values, rng, low, top_value):
    longest = values.shape.index(max(values.shape))
    spots = []
    for shift in (0, 1):
        where = [jax.random.randint(jax.random.fold_in(rng, axis), (), 0, length) for axis, length in enumerate(values.shape)]
        where[longest] = (where[longest] + shift) % values.shape[longest]
        spots.append(tuple(where))
    return values.at[spots[0]].set(low).at[spots[1]].set(top_value)


def level_of(own_key, extent, pieces, low, top_value):
    factor_of = 1.0
    for axis_at, parts in pieces:
        draws = jax.random.uniform(jax.random.fold_in(jax.random.fold_in(own_key, 6), axis_at), (parts,), jnp.float32, low / len(pieces), top_value / len(pieces))
        factor_of = factor_of * jnp.repeat(jnp.exp(draws), extent[axis_at] // parts).reshape((-1,) + (1,) * (len(extent) - 1 - axis_at))
    return factor_of


def scatter_about(stream_key, dims, scale, most, cuts=(), kind=jnp.bfloat16):
    entries = jax.random.normal(stream_key, dims, jnp.float32) * scale
    if len(cuts) > 0:
        entries = level_of(stream_key, dims, cuts, -0.22, 0.18) * entries
    return jnp.clip(entries, min=-most, max=most).astype(kind)


def setup_inputs(seed: int = 0) -> dict:
    streams_of = jax.random.split(jax.random.key(seed), 10)
    return {
        "disp": scatter_about(streams_of[0], (2, COMP, NX, NY, NZ), 0.5, 4.0, ((0, 2), (2, 16), (3, 16)), jnp.float32),
        "force": scatter_about(streams_of[1], (2, COMP, NX, NY, NZ), 2.0, 12.0, ((0, 2), (2, 16), (3, 16)), jnp.float32),
        "kappa": jnp.clip(jnp.exp(math.log(0.5) - 2.3025851 * jax.random.uniform(streams_of[2], (2, NX, NY, NZ), jnp.float32) ** level_of(streams_of[2], (2, NX, NY, NZ), ((0, 2), (1, 16), (2, 16)), -0.2, 0.2)), 0.05, 0.5),
        "sigma": jnp.clip(jnp.exp(math.log(1.0) - 1.609438 * jax.random.uniform(streams_of[3], (2, NX, NY, NZ), jnp.float32) ** level_of(streams_of[3], (2, NX, NY, NZ), ((0, 2), (1, 16), (2, 16)), -0.2, 0.2)), 0.2, 1.0),
        "gap0": scatter_about(streams_of[4], (NBLK, SBLK), 0.5, 3.0, ((0, 256),), jnp.float32),
        "pressure": jnp.clip(1.0 * jax.random.uniform(streams_of[5], (NBLK, SBLK), jnp.float32) ** level_of(streams_of[5], (NBLK, SBLK), ((0, 256),), -0.2, 0.2), 0.0, 1.0),
        "mortar": scatter_about(streams_of[6], (NBLK, SBLK, SBLK), SBLK ** -0.5, 0.5, ((0, 256),), jnp.float32),
        "partner": plant(jax.random.randint(streams_of[7], (NBLK,), 0, ROWBLK), jax.random.fold_in(streams_of[7], 1), 0, ROWBLK - 1).astype(jnp.int32),
        "active": plant((jax.random.randint(streams_of[8], (NBLK,), 0, 2) < 1).astype(jnp.int32), jax.random.fold_in(streams_of[8], 1), 0, 1),
    }


def neighbours():
    result = []
    for first in (-1, 0, 1):
        for second in (-1, 0, 1):
            for third in (-1, 0, 1):
                if first != 0 or second != 0 or third != 0:
                    result.append((first, second, third))
    return result

def apply_stencil(field, padded, kappa, kappa_rim, sigma):
    sizes = field.shape[2:]
    total = sigma[:, None] * field
    for offset in neighbours():
        weight = 0.5 ** (abs(offset[0]) + abs(offset[1]) + abs(offset[2]) - 1)
        lower = [1 + offset[0], 1 + offset[1], 1 + offset[2]]
        bond = 0.5 * (kappa + kappa_rim[:, lower[0]:lower[0] + sizes[0], lower[1]:lower[1] + sizes[1], lower[2]:lower[2] + sizes[2]])
        near = padded[:, :, lower[0]:lower[0] + sizes[0], lower[1]:lower[1] + sizes[1], lower[2]:lower[2] + sizes[2]]
        total = total + weight * bond[:, None] * (field - near)
    return total

def stencil(field, kappa, sigma):
    padded = jnp.pad(field, ((0, 0), (0, 0), (1, 1), (1, 1), (1, 1)))
    kappa_rim = jnp.pad(kappa, ((0, 0), (1, 1), (1, 1), (1, 1)))
    return apply_stencil(field, padded, kappa, kappa_rim, sigma)

def blocks_of(field):
    surface = field[:, 2, :, :, 0]
    surface = surface.reshape(2, N_GX, CX, N_GY, CY).transpose(0, 1, 3, 2, 4)
    return surface.reshape(2, N_GX, N_GY, BLK_DEV, SBLK)

def gap_of(field, partner_grid, mortar_grid):
    surfaces = blocks_of(field)
    master_row = surfaces[1].transpose(1, 0, 2, 3).reshape(N_GY, N_GX * BLK_DEV, SBLK)
    row_index = jnp.arange(N_GY, dtype=jnp.int32)[None, :, None]
    picked = master_row[row_index, partner_grid]
    pulled = jnp.einsum('abcij,abcj->abci', mortar_grid, picked, precision=lax.Precision.HIGHEST)
    return -surfaces[0] - pulled

def spread(traction, partner_grid, mortar_grid):
    pulled = jnp.einsum('abcij,abci->abcj', mortar_grid, traction, precision=lax.Precision.HIGHEST)
    row_index = jnp.arange(N_GY, dtype=jnp.int32)[None, :, None]
    master_row = jnp.zeros((N_GY, N_GX * BLK_DEV, SBLK), jnp.float32).at[row_index, partner_grid].add(-pulled)
    master = master_row.reshape(N_GY, N_GX, BLK_DEV, SBLK).transpose(1, 0, 2, 3)
    both = jnp.stack([-traction, master])
    both = both.reshape(2, N_GX, N_GY, CX, CY).transpose(0, 1, 3, 2, 4)
    return both.reshape(2, NX, NY)

def reference(disp, force, kappa, sigma, gap0, pressure, mortar, partner, active):
    mortar_grid = mortar.reshape(N_GX, N_GY, BLK_DEV, SBLK, SBLK)
    partner_grid = partner.reshape(N_GX, N_GY, BLK_DEV).astype(jnp.int32)
    press = pressure.reshape(N_GX, N_GY, BLK_DEV, SBLK)
    flags = active.reshape(N_GX, N_GY, BLK_DEV, 1).astype(jnp.float32)
    gap = gap0.reshape(N_GX, N_GY, BLK_DEV, SBLK) + gap_of(disp, partner_grid, mortar_grid)
    radius = jnp.sqrt(gap * gap + press * press + 0.01)
    complement = gap + press - radius
    slope_gap = 1.0 - gap / radius
    slope_press = 1.0 - press / radius
    divisor = slope_press + 0.5
    stiffness = flags * slope_gap / divisor
    excess = flags * complement / divisor
    rhs = force - stencil(disp, kappa, sigma)
    rhs = rhs.at[:, 2, :, :, 0].add(spread(flags * press - excess, partner_grid, mortar_grid))

    def operate(field):
        image = stencil(field, kappa, sigma)
        return image.at[:, 2, :, :, 0].add(spread(stiffness * gap_of(field, partner_grid, mortar_grid), partner_grid, mortar_grid))
    increment = jnp.zeros_like(rhs)
    residual, direction = (rhs, rhs)
    norm_now = jnp.sum(residual * residual)
    for step in range(CG_ITERS):
        image = operate(direction)
        alpha = norm_now / jnp.sum(direction * image)
        increment = increment + alpha * direction
        residual = residual - alpha * image
        norm_next = jnp.sum(residual * residual)
        direction = residual + norm_next / norm_now * direction
        norm_now = norm_next
    change = gap_of(increment, partner_grid, mortar_grid)
    new_press = flags * (press - (complement + slope_gap * change) / divisor)
    return (increment, new_press.reshape(NBLK, SBLK))
```

```python
import jax
import jax.numpy as jnp
from jax import lax
from jax.sharding import PartitionSpec as P

HIGH = lax.Precision.HIGHEST
SBLK = 128
WIDE = 3


def shifted(block, axis, step):
    count = lax.axis_size(axis)
    pairs = [(i, i + step) for i in range(count) if 0 <= i + step < count]
    return lax.ppermute(block, axis, pairs)


def halo(fields, axis, dim):
    low_parts, high_parts = [], []
    for array, width in fields:
        size = array.shape[dim]
        low_parts.append(lax.slice_in_dim(array, size - width, size, axis=dim).reshape(-1, 128))
        high_parts.append(lax.slice_in_dim(array, 0, width, axis=dim).reshape(-1, 128))
    low = shifted(jnp.concatenate(low_parts), axis, 1)
    high = shifted(jnp.concatenate(high_parts), axis, -1)
    result, at = [], 0
    for (array, width), part in zip(fields, low_parts):
        rows = part.shape[0]
        shape = array.shape[:dim] + (width,) + array.shape[dim + 1 :]
        result.append(
            jnp.concatenate(
                [low[at : at + rows].reshape(shape), array, high[at : at + rows].reshape(shape)],
                axis=dim,
            )
        )
        at += rows
    return result


def smooth(field):
    zero = jnp.zeros_like(field[..., :1])
    field = field + 0.5 * (
        jnp.concatenate([zero, field[..., :-1]], -1) + jnp.concatenate([field[..., 1:], zero], -1)
    )
    field = field[..., 1:-1, :] + 0.5 * (field[..., :-2, :] + field[..., 2:, :])
    return field[..., 1:-1, :, :] + 0.5 * (field[..., :-2, :, :] + field[..., 2:, :, :])


def inner(field):
    return field[..., 1:-1, 1:-1, :]


def apply_k(field, kappa, diagonal):
    return diagonal * inner(field) - inner(kappa) * smooth(field) - smooth(kappa * field)


def inside(axis, width, size):
    place = lax.axis_index(axis) * size + jnp.arange(-width, size + width)
    return ((place >= 0) & (place < lax.axis_size(axis) * size)).astype(jnp.float32)


def rim_mask(width, sizes):
    return inside("gx", width, sizes[0])[:, None, None] * inside("gy", width, sizes[1])[:, None]


def base(disp, force, kappa, sigma):
    sizes = disp.shape[1:3]
    disp_x, kappa_x, force_x, sigma_x = halo(
        ((disp, 3), (kappa[None], 3), (force, 2), (sigma[None], 2)), "gx", 1
    )
    disp_e, kappa_e, force_e, sigma_e = halo(
        ((disp_x, 3), (kappa_x, 3), (force_x, 2), (sigma_x, 2)), "gy", 2
    )
    diagonal = sigma_e + 8.0 * inner(kappa_e) + smooth(kappa_e)
    res = (force_e - apply_k(disp_e, kappa_e, diagonal)) * rim_mask(2, sizes)
    image = apply_k(res, inner(kappa_e), inner(diagonal)) * rim_mask(1, sizes)
    second = apply_k(image, inner(inner(kappa_e)), inner(inner(diagonal)))
    res, image = inner(inner(res)), inner(image)
    moments = jnp.stack(
        [jnp.sum(res * res), jnp.sum(res * image), jnp.sum(image * image), jnp.sum(image * second)]
    )
    diag = inner(inner(diagonal))[0]
    strips = jnp.stack(
        [
            disp[2, :, :, 0],
            res[2, :, :, 0],
            image[2, :, :, 0],
            image[2, :, :, 1],
            second[2, :, :, 0],
            second[2, :, :, 1],
            kappa[:, :, 0],
            kappa[:, :, 1],
            diag[:, :, 0],
            diag[:, :, 1],
        ]
    )
    return res, image, moments, strips


def smooth_row(grid, low=None, high=None):
    zero = jnp.zeros_like(grid[..., :1])
    low = zero if low is None else low[..., None]
    high = zero if high is None else high[..., None]
    wide = jnp.concatenate([low, grid, high], -1)
    wide = wide[..., 1:-1] + 0.5 * (wide[..., :-2] + wide[..., 2:])
    return smooth_line(wide, -2)


def smooth_line(wide, dim):
    zero = jnp.zeros_like(lax.slice_in_dim(wide, 0, 1, axis=dim))
    size = wide.shape[dim]
    before = jnp.concatenate([zero, lax.slice_in_dim(wide, 0, size - 1, axis=dim)], dim)
    after = jnp.concatenate([lax.slice_in_dim(wide, 1, size, axis=dim), zero], dim)
    return wide + 0.5 * (before + after)


def on_device(disp, force, kappa, sigma, gap0, pressure, mortar, partner, active):
    body, gx = lax.axis_index("body"), lax.axis_index("gx")
    row = lax.axis_size("gx")
    tile = disp.shape[2:4]
    res, image, moments, strips = base(disp[0], force[0], kappa[0], sigma[0])
    extra = jnp.zeros((8, 128), jnp.float32)
    extra = extra.at[0, :4].set(moments)
    extra = extra.at[1, :2].set(partner.astype(jnp.float32))
    extra = extra.at[2, :2].set(active.astype(jnp.float32))
    own_mortar = lax.dynamic_index_in_dim(mortar, body, 0, keepdims=False)
    package = jnp.concatenate([own_mortar, strips.reshape(20, 128), gap0, pressure, extra])
    gathered = lax.all_gather(lax.all_gather(package, "gx"), "body")
    blocks = gathered[:, :, :128].reshape(2 * row, SBLK, SBLK)

    def ordered(rows):
        return rows.transpose(1, 0, 2).reshape(2 * row, SBLK)

    gap0_row = ordered(gathered[0, :, 148:150])
    press = ordered(gathered[0, :, 150:152])
    sums = jnp.sum(gathered[:, :, 152, :4], axis=(0, 1))
    pair = gathered[0, :, 153, :2].T.reshape(-1).astype(jnp.int32)
    flags = gathered[0, :, 154, :2].T.reshape(-1, 1)
    place = (pair % 2) * row + pair // 2
    selector = (place[:, None] == jnp.arange(2 * row, dtype=jnp.int32)[None, :]).astype(jnp.float32)
    surface = (
        gathered[:, :, 128:148]
        .reshape(2, row, 10, tile[0], tile[1])
        .transpose(2, 0, 1, 3, 4)
        .reshape(10, 2, row * tile[0], tile[1])
    )
    s_disp, s_res, s_im0, s_im1, s_sec0, s_sec1, kap0, kap1, dia0, dia1 = surface

    def to_blocks(grid):
        return ordered(grid.reshape(row, 2, SBLK))

    def to_grid(rows):
        return rows.reshape(2, row, SBLK).transpose(1, 0, 2).reshape(row * tile[0], tile[1])

    def gap_of(grids):
        picked = jnp.dot(selector, to_blocks(grids[1]), precision=HIGH)
        return -to_blocks(grids[0]) - jnp.einsum("bij,bj->bi", blocks, picked, precision=HIGH)

    def spread(traction):
        pulled = jnp.einsum("bij,bi->bj", blocks, traction, precision=HIGH)
        master = -jnp.dot(selector.T, pulled, precision=HIGH)
        return jnp.stack([to_grid(-traction), to_grid(master)])

    gap = gap0_row + gap_of(s_disp)
    radius = jnp.sqrt(gap * gap + press * press + 0.01)
    complement = gap + press - radius
    slope_gap = 1.0 - gap / radius
    slope_press = 1.0 - press / radius
    divisor = slope_press + 0.5
    stiffness = flags * slope_gap / divisor
    excess = flags * complement / divisor
    first = spread(flags * press - excess)
    weighted = kap0 * first
    edges = jnp.stack([first, weighted])
    low = shifted(edges[..., -1], "gy", 1)
    high = shifted(edges[..., 0], "gy", -1)
    gap_res = gap_of(s_res + first)
    push = stiffness * gap_res
    second = spread(push)
    smooth_first = smooth_row(first, low[0], high[0])
    smooth_weighted = smooth_row(weighted, low[1], high[1])
    k_first = dia0 * first - kap0 * smooth_first - smooth_weighted
    b0 = k_first + second
    b1 = -0.5 * (kap1 * smooth_first + smooth_weighted)
    gap_im = gap_of(s_im0 + b0)
    mu0 = sums[0] + jnp.sum(2.0 * s_res * first + first * first)
    mu1 = sums[1] + jnp.sum(2.0 * s_im0 * first + first * k_first) + jnp.sum(gap_res * push)
    mu2 = sums[2] + jnp.sum(2.0 * (s_im0 * b0 + s_im1 * b1) + b0 * b0 + b1 * b1)
    mu3 = sums[3] + jnp.sum(
        2.0 * (s_sec0 * b0 + s_sec1 * b1)
        + dia0 * b0 * b0
        + dia1 * b1 * b1
        - 2.0
        * (
            kap0 * b0 * smooth_row(b0 + 0.5 * b1)
            + kap1 * b1 * smooth_row(0.5 * b0 + b1)
        )
    )
    mu3 = mu3 + jnp.sum(stiffness * gap_im * gap_im)
    rims = jnp.stack([b0, b1, kap0 * b0, kap1 * b1])
    rims = jnp.stack([rims[..., 0], rims[..., -1]])
    length = row * tile[0]
    send = jnp.concatenate([rims.reshape(16, length), jnp.zeros((8, length), jnp.float32)])
    send = send.at[16, :4].set(jnp.stack([mu0, mu1, mu2, mu3]))
    columns = lax.axis_size("gy")
    rows = lax.all_to_all(
        jnp.broadcast_to(send[None], (columns,) + send.shape), "gy", 0, 0, tiled=True
    )
    total = jnp.sum(rows[:, 16, :4], axis=0)
    rims = rows[:, :16].reshape(columns, 2, 4, 2, length)
    upper = rims[:-1, 1]
    lower = rims[1:, 0]
    mixed = smooth_line(
        jnp.stack(
            [
                lower[:, 0] + 0.5 * lower[:, 1],
                0.5 * lower[:, 0] + lower[:, 1],
                lower[:, 2] + 0.5 * lower[:, 3],
                0.5 * lower[:, 2] + lower[:, 3],
            ],
            axis=1,
        ),
        -1,
    )
    across = jnp.sum(
        upper[:, 2] * mixed[:, 0]
        + upper[:, 3] * mixed[:, 1]
        + upper[:, 0] * mixed[:, 2]
        + upper[:, 1] * mixed[:, 3]
    )
    m0, m1, m2 = total[0], total[1], total[2]
    m3 = total[3] - across
    alpha = m0 / m1
    left = alpha * alpha * m2 - m0
    beta = left / m0
    energy = (m1 - 2.0 * alpha * m2 + alpha * alpha * m3) - beta * left / alpha
    step = left / energy
    c_res = alpha + step * (1.0 + beta)
    c_im = -step * alpha
    change = c_res * gap_res + c_im * gap_im
    new_press = flags * (press - (complement + slope_gap * change) / divisor)
    new_press = lax.dynamic_index_in_dim(
        new_press.reshape(2, row, SBLK), gx, 1, keepdims=False
    )

    def own(grids):
        grid = lax.dynamic_index_in_dim(grids, body, 0, keepdims=False)
        return lax.dynamic_slice_in_dim(grid, gx * tile[0], tile[0], 0)

    increment = c_res * res + c_im * image
    increment = increment.at[2, :, :, 0].add(own(c_res * first + c_im * b0))
    increment = increment.at[2, :, :, 1].add(own(c_im * b1))
    return (increment[None], new_press)


def solution(mesh):
    placed = (
        P("body", None, "gx", "gy", None),
        P("body", None, "gx", "gy", None),
        P("body", "gx", "gy", None),
        P("body", "gx", "gy", None),
        P(("gx", "gy"), None),
        P(("gx", "gy"), None),
        P(("gx", "gy"), None, None),
        P(("gx", "gy")),
        P(("gx", "gy")),
    )
    return jax.shard_map(
        on_device,
        mesh=mesh,
        in_specs=placed,
        out_specs=(P("body", None, "gx", "gy", None), P(("gx", "gy"), None)),
        check_vma=False,
    )
```

```python
import jax
import jax.numpy as jnp
from jax import lax
from jax.experimental import pallas as pl
from jax.experimental.pallas import tpu as pltpu
from jax.sharding import PartitionSpec as P

HIGH = lax.Precision.HIGHEST
F32 = jnp.float32
LANES = 128
DEPTHS = (3, 3, 3, 3, 2, 2, 2, 2)
STARTS = (0, 3, 6, 9, 12, 14, 16, 18)
SLABS = 20
LINES = 14
ROWS = 48
KAP0, KAP1, DIA0, DIA1, RES0, IM0, IM1, SEC0, SEC1 = 0, 1, 2, 3, 4, 6, 7, 8, 9


def roll(value, step, axis):
    return pltpu.roll(value, step % value.shape[axis], axis)


def iota(shape, axis):
    return lax.broadcasted_iota(jnp.int32, shape, axis)


def call(body, outs, args, smem=(), scratch=()):
    specs = [
        pl.BlockSpec(memory_space=pltpu.SMEM if i in smem else pltpu.VMEM)
        for i in range(len(args))
    ]
    many = isinstance(outs, list)
    shapes = [jax.ShapeDtypeStruct(s, F32) for s in (outs if many else [outs])]
    vmem = pl.BlockSpec(memory_space=pltpu.VMEM)
    return pl.pallas_call(
        body,
        out_shape=shapes if many else shapes[0],
        in_specs=specs,
        out_specs=[vmem] * len(shapes) if many else vmem,
        scratch_shapes=[pltpu.VMEM(s, F32) for s in scratch],
        compiler_params=pltpu.CompilerParams(vmem_limit_bytes=40 * 1024 * 1024),
    )(*args)


def fill(out, block):
    for at in range(0, out.shape[0], 8):
        out[at : at + 8, :] = block


def stack_rows(pieces):
    return jnp.concatenate(pieces, axis=0)


def tile_lines(disp, force, kappa, sigma):
    return (
        lambda x: disp[0, 0, x],
        lambda x: disp[0, 1, x],
        lambda x: disp[0, 2, x],
        lambda x: kappa[0, x],
        lambda x: force[0, 0, x],
        lambda x: force[0, 1, x],
        lambda x: force[0, 2, x],
        lambda x: sigma[0, x],
    )


def pack_x(partner, disp, force, kappa, sigma, up, down, package):
    for line, depth, start in zip(tile_lines(disp, force, kappa, sigma), DEPTHS, STARTS):
        for k in range(depth):
            up[start + k] = line(8 - depth + k)
            down[start + k] = line(k)
    first = disp[0, 2, 0:4].reshape(LANES, LANES).T[0:1]
    second = disp[0, 2, 4:8].reshape(LANES, LANES).T[0:1]
    lane = iota((1, LANES), 1)
    hot = []
    for k in range(2):
        q = partner[k]
        hot.append(jnp.where(lane == 4 * (q // 2) + q % 2, 1.0, 0.0).astype(F32))
    four = stack_rows([first, second, hot[0], hot[1]])
    fill(package, stack_rows([four, four]))


def ext_line(line, low, high, field, x):
    depth, start = DEPTHS[field], STARTS[field]
    if x < 3:
        k = x - (3 - depth)
        return None if k < 0 else low[start + k]
    if x < 11:
        return line(x - 3)
    k = x - 11
    return None if k >= depth else high[start + k]


def pack_y(disp, force, kappa, sigma, low, high, up, down):
    lines = tile_lines(disp, force, kappa, sigma)
    sub = iota((8, LANES), 0)
    zero = jnp.zeros((8, LANES), F32)
    for x in range(LINES):
        last, first = [], []
        for field in range(8):
            value = ext_line(lines[field], low, high, field, x)
            last.append(zero if value is None else value[24:32])
            first.append(zero if value is None else value[0:8])
        for k, (a, b, c) in enumerate(((0, 1, 4), (2, 3, 5))):
            up[x, 8 * k : 8 * k + 8] = jnp.where(
                sub >= 5, last[a], jnp.where(sub >= 2, roll(last[b], -3, 0), roll(last[c], -6, 0))
            )
            down[x, 8 * k : 8 * k + 8] = jnp.where(
                sub < 3, first[a], jnp.where(sub < 6, roll(first[b], 3, 0), roll(first[c], 6, 0))
            )
        up[x, 16:24] = jnp.where(sub >= 6, last[7], roll(last[6], -2, 0))
        down[x, 16:24] = jnp.where(sub < 2, first[7], roll(first[6], 2, 0))


def mat_vec(matrix, row):
    return lax.dot_general(
        jnp.broadcast_to(row, (8, LANES)),
        matrix,
        (((1,), (1,)), ((), ())),
        precision=HIGH,
        preferred_element_type=F32,
    )[0:1]


def vec_mat(row, matrix):
    return lax.dot_general(
        jnp.broadcast_to(row, (8, LANES)),
        matrix,
        (((1,), (0,)), ((), ())),
        precision=HIGH,
        preferred_element_type=F32,
    )[0:1]


def surface_row(q):
    return 4 * (q // 2) + q % 2


def contact_first(partner, active, rows, gap0, pressure, mortar, state):
    gx = lax.axis_index("gx")
    half = rows.shape[0] // 2
    for k in range(2):
        own = rows[pl.ds(4 * gx + k, 1), :]
        master = rows[pl.ds(half + surface_row(partner[k]), 1), :]
        matrix = mortar[k]
        press = pressure[k : k + 1, :]
        flag = jnp.full((1, LANES), active[k], jnp.int32).astype(F32)
        gap = gap0[k : k + 1, :] - own - mat_vec(matrix, master)
        radius = jnp.sqrt(gap * gap + press * press + 0.01)
        complement = gap + press - radius
        slope_gap = 1.0 - gap / radius
        slope_press = 1.0 - press / radius
        divisor = slope_press + 0.5
        stiffness = flag * slope_gap / divisor
        excess = flag * complement / divisor
        traction = flag * press - excess
        state[k : k + 1, :] = stiffness
        state[2 + k : 3 + k, :] = complement
        state[4 + k : 5 + k, :] = slope_gap
        state[6 + k : 7 + k, :] = divisor
        state[8 + k : 9 + k, :] = flag
        state[10 + k : 11 + k, :] = press
        state[12 + k : 13 + k, :] = traction
        state[14 + k : 15 + k, :] = vec_mat(traction, matrix)


def base(
    disp, force, kappa, sigma, low_x, high_x, low_y, high_y, state,
    res_out, image_out, strips, moments, package,
    fields, diag, res, image, second, smooth_a, smooth_b, smooth_k,
):
    body, gx, gy = lax.axis_index("body"), lax.axis_index("gx"), lax.axis_index("gy")
    lines = tile_lines(disp, force, kappa, sigma)
    places = ((0, 0, 0), (0, 3, -3), (1, 0, 0), (1, 3, -3), (0, 6, -6), (1, 6, -6), (2, 2, -2), (2, 0, 0))
    for field in range(8):
        group, before, after = places[field]
        for x in range(LINES):
            value = ext_line(lines[field], low_x, high_x, field, x)
            if value is None:
                continue
            part = slice(8 * group, 8 * group + 8)
            fields[field, x, 0:8] = roll(low_y[x, part], before, 0)
            fields[field, x, 8:40] = value
            fields[field, x, 40:48] = roll(high_y[x, part], after, 0)
    lane = iota((ROWS, LANES), 1)
    row = iota((ROWS, LANES), 0)
    keep_low = jnp.where(lane > 0, 0.5, 0.0).astype(F32)
    keep_high = jnp.where(lane < LANES - 1, 0.5, 0.0).astype(F32)
    row_low = jnp.where(gy == 0, 8, 0)
    row_high = jnp.where(gy == lax.axis_size("gy") - 1, 40, ROWS)
    inside_y = jnp.where((row >= row_low) & (row < row_high), 1.0, 0.0).astype(F32)
    line_low = jnp.where(gx == 0, 3, 0)
    line_high = jnp.where(gx == lax.axis_size("gx") - 1, 11, LINES)

    def in_plane(value):
        value = value + keep_low * roll(value, 1, 1) + keep_high * roll(value, -1, 1)
        return value + 0.5 * (roll(value, 1, 0) + roll(value, -1, 0))

    def along(ref, *at):
        *lead, x = at
        return ref[(*lead, x)] + 0.5 * (ref[(*lead, x - 1)] + ref[(*lead, x + 1)])

    def inside(x):
        return inside_y * jnp.where((x >= line_low) & (x < line_high), 1.0, 0.0).astype(F32)

    @pl.loop(0, LINES)
    def _(x):
        kap = fields[3, x]
        smooth_k[x] = in_plane(kap)
        for c in range(3):
            value = fields[c, x]
            smooth_a[c, x] = in_plane(value)
            smooth_b[c, x] = in_plane(kap * value)

    @pl.loop(1, LINES - 1)
    def _(x):
        kap = fields[3, x]
        dia = fields[7, x] + 8.0 * kap + along(smooth_k, x)
        diag[x] = dia
        mask = inside(x)
        for c in range(3):
            value = fields[4 + c, x] - (
                dia * fields[c, x] - kap * along(smooth_a, c, x) - along(smooth_b, c, x)
            )
            res[c, x] = mask * value

    @pl.loop(1, LINES - 1)
    def _(x):
        kap = fields[3, x]
        for c in range(3):
            value = res[c, x]
            smooth_a[c, x] = in_plane(value)
            smooth_b[c, x] = in_plane(kap * value)

    @pl.loop(2, LINES - 2)
    def _(x):
        kap = fields[3, x]
        dia = diag[x]
        mask = inside(x)
        for c in range(3):
            image[c, x] = mask * (
                dia * res[c, x] - kap * along(smooth_a, c, x) - along(smooth_b, c, x)
            )

    @pl.loop(2, LINES - 2)
    def _(x):
        kap = fields[3, x]
        for c in range(3):
            value = image[c, x]
            smooth_a[c, x] = in_plane(value)
            smooth_b[c, x] = in_plane(kap * value)

    def finish(k, sums):
        x = k + 3
        kap = fields[3, x]
        dia = diag[x]
        sums = list(sums)
        for c in range(3):
            r, p = res[c, x, 8:40], image[c, x, 8:40]
            q = (dia * image[c, x] - kap * along(smooth_a, c, x) - along(smooth_b, c, x))[8:40]
            if c == 2:
                second[k] = q
            res_out[c, k] = r
            image_out[c, k] = p
            for i, (a, b) in enumerate(((r, r), (r, p), (p, p), (p, q))):
                product = (a * b).reshape(4, 8, LANES)
                sums[i] = sums[i] + ((product[0] + product[1]) + (product[2] + product[3]))
        return tuple(sums)

    sums = lax.fori_loop(0, 8, finish, (jnp.zeros((8, LANES), F32),) * 4)
    for i in range(4):
        moments[i] = sums[i]
    strips[...] = jnp.zeros(strips.shape, F32)
    lanes = iota((LANES, LANES), 1)
    for group in range(4):
        near = [min(max(4 * group - 1 + k, 1), LINES - 2) for k in range(4)]
        wide = stack_rows([fields[3, x, 8:40] for x in near])
        wide = jnp.where(lanes < 2, wide, roll(stack_rows([diag[x, 8:40] for x in near]), 2, 1))
        count = 4
        if group in (1, 2):
            count = 10
            for at, piece in (
                (4, stack_rows([res[2, x, 8:40] for x in near])),
                (6, stack_rows([image[2, x, 8:40] for x in near])),
                (8, stack_rows([second[x - 3] for x in near])),
            ):
                wide = jnp.where(lanes < at, wide, roll(piece, at, 1))
        turned = wide.T
        for kind in range(count):
            strips[kind, group : group + 1, :] = turned[kind : kind + 1]
        if group in (1, 2):
            k = group - 1
            send = jnp.where(body == 1, state[14 + k : 15 + k, :], state[12 + k : 13 + k, :])
            if k == 0:
                sent, surface = [send], [turned[RES0 : RES0 + 1]]
            else:
                sent.append(send)
                surface.append(turned[RES0 : RES0 + 1])
    four = stack_rows(surface + sent)
    fill(package, stack_rows([four, four]))


def spread_row(select_rows, rows):
    half = rows.shape[0] // 2
    index = iota((half, LANES), 0) % 4
    select = jnp.where(index >= 2, select_rows[half:, :], 0.0)
    master = -lax.dot_general(
        select,
        rows[half:, :],
        (((0,), (0,)), ((), ())),
        precision=HIGH,
        preferred_element_type=F32,
    )[:half]
    slave = jnp.where(index < 2, -roll(rows[:half, :], -2, 0), 0.0)
    return slave, master


def own_extended(padded, gx):
    return stack_rows(
        [
            padded[pl.ds(4 * gx + 5, 1), :],
            padded[pl.ds(4 * gx + 8, 2), :],
            padded[pl.ds(4 * gx + 12, 1), :],
            jnp.zeros((4, LANES), F32),
        ]
    )


def put_padded(padded, value):
    half = value.shape[0]
    padded[0:8, :] = jnp.zeros((8, LANES), F32)
    padded[8 : 8 + half, :] = value
    padded[8 + half : 16 + half, :] = jnp.zeros((8, LANES), F32)


def contact_second(partner, select_rows, rows, state, mortar, strips, edges, out, padded, surf0, surf1):
    body, gx = lax.axis_index("body"), lax.axis_index("gx")
    half = rows.shape[0] // 2
    slave, master = spread_row(select_rows, rows)
    put_padded(padded, jnp.where(body == 0, slave, master))
    surf0[...] = rows[:half, :] + slave
    surf1[...] = rows[half:, :] + master
    first = own_extended(padded, gx)
    edges[0:8, :] = first
    edges[8:16, :] = strips[KAP0] * first
    for k in range(2):
        matrix = mortar[k]
        gap = -surf0[pl.ds(4 * gx + k, 1), :] - mat_vec(
            matrix, surf1[pl.ds(surface_row(partner[k]), 1), :]
        )
        push = state[k : k + 1, :] * gap
        pulled = vec_mat(push, matrix)
        out[k : k + 1, :] = gap
        out[2 + k : 3 + k, :] = push
        out[4 + k : 5 + k, :] = jnp.where(body == 1, pulled, push)
        out[6 + k : 7 + k, :] = strips[IM0, 1 + k : 2 + k, :]


def line_smooth(value):
    lane = iota(value.shape, 1)
    back, ahead = roll(value, 32, 1), roll(value, -32, 1)
    back = jnp.where(lane >= 32, back, roll(back, 1, 0))
    ahead = jnp.where(lane < 96, ahead, roll(ahead, -1, 0))
    return value + 0.5 * (back + ahead)


def row_smooth(value, low=None, high=None):
    y = iota(value.shape, 1) % 32
    before = 0.0 if low is None else roll(low, -31, 1)
    after = 0.0 if high is None else roll(high, 31, 1)
    before = jnp.where(y > 0, roll(value, 1, 1), before)
    after = jnp.where(y < 31, roll(value, -1, 1), after)
    return value + 0.5 * (before + after)


def couple(edges, low, high, strips, second, moved, package):
    gx = lax.axis_index("gx")
    first = edges[0:8, :]
    plain = line_smooth(row_smooth(first, low[0:8, :], high[0:8, :]))
    weighted = line_smooth(row_smooth(edges[8:16, :], low[8:16, :], high[8:16, :]))
    row = iota((8, LANES), 0)
    lowest = jnp.where(gx == 0, 1, 0)
    highest = jnp.where(gx == lax.axis_size("gx") - 1, 3, 4)
    mask = (row >= lowest) & (row < highest)
    kap0 = strips[KAP0]
    top = jnp.where(mask, strips[DIA0] * first - kap0 * plain - weighted, 0.0)
    below = jnp.where(mask, -0.5 * (strips[KAP1] * plain + weighted), 0.0)
    moved[0:8, :] = top
    moved[8:16, :] = below
    four = stack_rows([second[6:8, :] + top[1:3], second[4:6, :]])
    fill(package, stack_rows([four, four]))


def total(value):
    return jnp.sum(jnp.sum(value, axis=1, keepdims=True), axis=0, keepdims=True)


def measure_moments(
    partner, select_rows, rows, state, mortar, strips, edges, second, moved, moments,
    package, image_out, padded, surf0, surf1,
):
    body, gx = lax.axis_index("body"), lax.axis_index("gx")
    half = rows.shape[0] // 2
    slave, master = spread_row(select_rows, rows)
    put_padded(padded, jnp.where(body == 0, slave, master))
    surf0[...] = rows[:half, :] + slave
    surf1[...] = rows[half:, :] + master
    first = edges[0:8, :]
    k_first = moved[0:8, :]
    top = k_first + own_extended(padded, gx)
    below = moved[8:16, :]
    once = jnp.where(body == 0, 1.0, 0.0).astype(F32)
    push_sum = jnp.zeros((1, LANES), F32)
    gap_sum = jnp.zeros((1, LANES), F32)
    for k in range(2):
        gap = -surf0[pl.ds(4 * gx + k, 1), :] - mat_vec(
            mortar[k], surf1[pl.ds(surface_row(partner[k]), 1), :]
        )
        image_out[k : k + 1, :] = gap
        push_sum = push_sum + second[k : k + 1, :] * second[2 + k : 3 + k, :]
        gap_sum = gap_sum + state[k : k + 1, :] * gap * gap
    image_out[2:8, :] = jnp.zeros((6, LANES), F32)
    image_out[8:16, :] = top
    image_out[16:24, :] = below
    row = iota((8, LANES), 0)
    own = (row == 1) | (row == 2)
    kap0, kap1 = strips[KAP0], strips[KAP1]

    def surface_sum(value):
        return total(jnp.where(own, value, 0.0))

    im0, im1 = strips[IM0], strips[IM1]
    mu0 = total(moments[0]) + surface_sum(first * (2.0 * strips[RES0] + first))
    mu1 = total(moments[1]) + surface_sum(first * (2.0 * im0 + k_first)) + once * total(push_sum)
    mu2 = total(moments[2]) + surface_sum(top * (2.0 * im0 + top) + below * (2.0 * im1 + below))
    t_top = line_smooth(row_smooth(top + 0.5 * below))
    t_below = line_smooth(row_smooth(0.5 * top + below))
    mu3 = (
        total(moments[3])
        + surface_sum(
            top * (2.0 * strips[SEC0] + strips[DIA0] * top - 2.0 * kap0 * t_top)
            + below * (2.0 * strips[SEC1] + strips[DIA1] * below - 2.0 * kap1 * t_below)
        )
        + once * total(gap_sum)
    )
    lane = iota((8, LANES), 1)
    y = lane % 32
    send = jnp.zeros((8, LANES), F32)
    for k, value in enumerate((top, below, kap0 * top, kap1 * below)):
        send = send + jnp.where(y == 2 * k, roll(value, 2 * k, 1), 0.0)
        send = send + jnp.where(y == 2 * k + 1, roll(value, 2 * k + 1 - 31, 1), 0.0)
    for k, value in enumerate((mu0, mu1, mu2, mu3)):
        send = send + jnp.where((row == 0) & (lane == 16 + k), value, 0.0)
    send = send[0:4]
    fill(package, stack_rows([send, send]))


def reduce_column(rows, package):
    value = rows[...]
    count = value.shape[0]
    row, lane = iota(value.shape, 0), iota(value.shape, 1)
    place = row % 4
    following = roll(value, -4, 0)
    upper = [roll(value, -(2 * k + 1), 1) for k in range(4)]
    lower = [roll(following, -2 * k, 1) for k in range(4)]
    across = (
        upper[2] * line_smooth(lower[0] + 0.5 * lower[1])
        + upper[3] * line_smooth(0.5 * lower[0] + lower[1])
        + upper[0] * line_smooth(lower[2] + 0.5 * lower[3])
        + upper[1] * line_smooth(0.5 * lower[2] + lower[3])
    )
    counted = ((place == 1) | (place == 2)) & (lane % 32 == 0) & (row < count - 4)
    across = total(jnp.where(counted, across, 0.0))
    sums = jnp.sum(jnp.where(place == 0, value, 0.0), axis=0, keepdims=True)
    lane1 = iota((1, LANES), 1)
    sums = jnp.where((lane1 >= 16) & (lane1 < 20), sums, 0.0)
    sums = sums - jnp.where(lane1 == 19, across, 0.0)
    index = iota((8, LANES), 0)
    fill(package, jnp.where(index % 2 == 0, sums, 0.0))


def finish(rows, res, image, state, edges, second, last, increment, new_press):
    sums = jnp.sum(rows[...], axis=0, keepdims=True)
    lane = iota((1, LANES), 1)
    m0, m1, m2, m3 = [
        jnp.sum(jnp.where(lane == 16 + k, sums, 0.0), axis=1, keepdims=True) for k in range(4)
    ]
    alpha = m0 / m1
    left = alpha * alpha * m2 - m0
    beta = left / m0
    energy = (m1 - 2.0 * alpha * m2 + alpha * alpha * m3) - beta * left / alpha
    step = left / energy
    c_res = alpha + step * (1.0 + beta)
    c_im = -step * alpha
    for k in range(2):
        at = slice(k, k + 1)
        change = c_res * second[at, :] + c_im * last[at, :]
        press = state[10 + k : 11 + k, :]
        flag = state[8 + k : 9 + k, :]
        complement, slope = state[2 + k : 3 + k, :], state[4 + k : 5 + k, :]
        divisor = state[6 + k : 7 + k, :]
        new_press[at, :] = flag * (press - (complement + slope * change) / divisor)
    wide_res = jnp.broadcast_to(c_res, (8, LANES)).reshape(1, 8, LANES)
    wide_im = jnp.broadcast_to(c_im, (8, LANES)).reshape(1, 8, LANES)
    for c in range(3):
        for x in range(8):
            r = res[c, x].reshape(4, 8, LANES)
            p = image[c, x].reshape(4, 8, LANES)
            increment[0, c, x] = (wide_res * r + wide_im * p).reshape(32, LANES)
    for k in range(2):
        top = c_res * edges[1 + k : 2 + k, :] + c_im * last[9 + k : 10 + k, :]
        below = c_im * last[17 + k : 18 + k, :]
        wide = stack_rows([top, below, jnp.zeros((LANES - 2, LANES), F32)]).T
        for x in range(4):
            at = 4 * k + x
            increment[0, 2, at] = increment[0, 2, at] + wide[32 * x : 32 * x + 32]


def shifted(block, axis, step):
    count = lax.axis_size(axis)
    pairs = [(i, i + step) for i in range(count) if 0 <= i + step < count]
    return lax.ppermute(block, axis, pairs)


def on_device(disp, force, kappa, sigma, gap0, pressure, mortar, partner, active):
    nx, ny = lax.axis_size("gx"), lax.axis_size("gy")
    tile = (disp, force, kappa, sigma)
    whole = (8 * nx, LANES)
    row = ("body", "gx")

    def trade(package, axes):
        return lax.all_to_all(package, axes, 0, 0, tiled=True)

    slabs = (SLABS, 32, LANES)
    up, down, package = call(pack_x, [slabs, slabs, whole], (partner, *tile), smem=(0,))
    low_x, high_x = shifted(up, "gx", 1), shifted(down, "gx", -1)
    surfaces = trade(package, row)
    rims = (LINES, 24, LANES)
    up, down = call(pack_y, [rims, rims], (*tile, low_x, high_x))
    low_y, high_y = shifted(up, "gy", 1), shifted(down, "gy", -1)
    state = call(
        contact_first,
        (16, LANES),
        (partner, active, surfaces, gap0, pressure, mortar),
        smem=(0, 1),
    )
    lines = (LINES, ROWS, LANES)
    res, image, strips, moments, package = call(
        base,
        [(3, 8, 32, LANES), (3, 8, 32, LANES), (16, 8, LANES), (4, 8, LANES), whole],
        (*tile, low_x, high_x, low_y, high_y, state),
        scratch=[(8, *lines), lines, (3, *lines), (3, *lines), (8, 32, LANES), (3, *lines), (3, *lines), lines],
    )
    rows = trade(package, row)
    half = 4 * nx
    work = [(half + 16, LANES), (half, LANES), (half, LANES)]
    edges, second = call(
        contact_second,
        [(16, LANES), (8, LANES)],
        (partner, surfaces, rows, state, mortar, strips),
        smem=(0,),
        scratch=work,
    )
    low, high = shifted(edges, "gy", 1), shifted(edges, "gy", -1)
    moved, package = call(
        couple, [(16, LANES), whole], (edges, low, high, strips, second)
    )
    rows = trade(package, row)
    package, last = call(
        measure_moments,
        [(4 * ny, LANES), (24, LANES)],
        (partner, surfaces, rows, state, mortar, strips, edges, second, moved, moments),
        smem=(0,),
        scratch=work,
    )
    package = call(reduce_column, (4 * nx, LANES), (trade(package, "gy"),))
    sums = trade(package, row)
    increment, new_press = call(
        finish,
        [disp.shape, gap0.shape],
        (sums, res, image, state, edges, second, last),
    )
    return (increment, new_press)


def solution(mesh):
    placed = (
        P("body", None, "gx", "gy", None),
        P("body", None, "gx", "gy", None),
        P("body", "gx", "gy", None),
        P("body", "gx", "gy", None),
        P(("gx", "gy"), None),
        P(("gx", "gy"), None),
        P(("gx", "gy"), None, None),
        P(("gx", "gy")),
        P(("gx", "gy")),
    )
    return jax.shard_map(
        on_device,
        mesh=mesh,
        in_specs=placed,
        out_specs=(P("body", None, "gx", "gy", None), P(("gx", "gy"), None)),
        check_vma=False,
    )
```

```python
import jax
import jax.numpy as jnp
from jax import lax
from jax.experimental import pallas as pl
from jax.experimental.pallas import tpu as pltpu
from jax.sharding import PartitionSpec as P

HIGH = lax.Precision.HIGHEST
F32 = jnp.float32
LANES = 128
DEPTHS = (3, 3, 3, 3, 2, 2, 2, 2)
STARTS = (0, 3, 6, 9, 12, 14, 16, 18)
SLABS = 20
LINES = 14
ROWS = 48
KAP0, KAP1, DIA0, DIA1, RES0, IM0, IM1, SEC0, SEC1 = 0, 1, 2, 3, 4, 6, 7, 8, 9


def roll(value, step, axis):
    return pltpu.roll(value, step % value.shape[axis], axis)


def iota(shape, axis):
    return lax.broadcasted_iota(jnp.int32, shape, axis)


def call(body, outs, args, smem=(), away=(), scratch=(), more=(), limit=40, put=pltpu.VMEM):
    def space(i):
        return pltpu.SMEM if i in smem else pltpu.HBM if i in away else pltpu.VMEM

    specs = [pl.BlockSpec(memory_space=space(i)) for i in range(len(args))]
    many = isinstance(outs, list)
    shapes = [jax.ShapeDtypeStruct(s, F32) for s in (outs if many else [outs])]
    spec = pl.BlockSpec(memory_space=put)
    return pl.pallas_call(
        body,
        out_shape=shapes if many else shapes[0],
        in_specs=specs,
        out_specs=[spec] * len(shapes) if many else spec,
        scratch_shapes=[pltpu.VMEM(s, F32) for s in scratch] + list(more),
        compiler_params=pltpu.CompilerParams(vmem_limit_bytes=limit * 1024 * 1024),
    )(*args)


def fill(out, block):
    for at in range(0, out.shape[0], 8):
        out[at : at + 8, :] = block


def stack_rows(pieces):
    return jnp.concatenate(pieces, axis=0)


def tile_lines(disp, force, kappa, sigma):
    return (
        lambda x: disp[0, 0, x],
        lambda x: disp[0, 1, x],
        lambda x: disp[0, 2, x],
        lambda x: kappa[0, x],
        lambda x: force[0, 0, x],
        lambda x: force[0, 1, x],
        lambda x: force[0, 2, x],
        lambda x: sigma[0, x],
    )


def pack_surface(partner, disp, package, tile, sem):
    copy = pltpu.make_async_copy(disp.at[0, 2], tile, sem)
    copy.start()
    copy.wait()
    first = tile[0:4].reshape(LANES, LANES).T[0:1]
    second = tile[4:8].reshape(LANES, LANES).T[0:1]
    lane = iota((1, LANES), 1)
    hot = []
    for k in range(2):
        hot.append(jnp.where(lane == surface_row(partner[k]), 1.0, 0.0).astype(F32))
    four = stack_rows([first, second, hot[0], hot[1]])
    fill(package, stack_rows([four, four]))


def pack_x(disp, force, kappa, sigma, after, up, down, sems):
    sources = [disp.at[0, c] for c in range(3)] + [kappa.at[0]]
    sources += [force.at[0, c] for c in range(3)] + [sigma.at[0]]
    copies = []
    for k, (source, depth, start) in enumerate(zip(sources, DEPTHS, STARTS)):
        into = pl.ds(start, depth)
        copies.append(
            pltpu.make_async_copy(source.at[pl.ds(8 - depth, depth)], up.at[into], sems.at[2 * k])
        )
        copies.append(
            pltpu.make_async_copy(source.at[pl.ds(0, depth)], down.at[into], sems.at[2 * k + 1])
        )
    for copy in copies:
        copy.start()
    for copy in copies:
        copy.wait()


def ext_line(line, low, high, field, x):
    depth, start = DEPTHS[field], STARTS[field]
    if x < 3:
        k = x - (3 - depth)
        return None if k < 0 else low[start + k]
    if x < 11:
        return line(x - 3)
    k = x - 11
    return None if k >= depth else high[start + k]


def pack_y(disp, force, kappa, sigma, low, high, up, down):
    lines = tile_lines(disp, force, kappa, sigma)
    sub = iota((8, LANES), 0)
    zero = jnp.zeros((8, LANES), F32)
    for x in range(LINES):
        last, first = [], []
        for field in range(8):
            value = ext_line(lines[field], low, high, field, x)
            last.append(zero if value is None else value[24:32])
            first.append(zero if value is None else value[0:8])
        for k, (a, b, c) in enumerate(((0, 1, 4), (2, 3, 5))):
            up[x, 8 * k : 8 * k + 8] = jnp.where(
                sub >= 5, last[a], jnp.where(sub >= 2, roll(last[b], -3, 0), roll(last[c], -6, 0))
            )
            down[x, 8 * k : 8 * k + 8] = jnp.where(
                sub < 3, first[a], jnp.where(sub < 6, roll(first[b], 3, 0), roll(first[c], 6, 0))
            )
        up[x, 16:24] = jnp.where(sub >= 6, last[7], roll(last[6], -2, 0))
        down[x, 16:24] = jnp.where(sub < 2, first[7], roll(first[6], 2, 0))


def mat_vec(matrix, row):
    return lax.dot_general(
        jnp.broadcast_to(row, (8, LANES)),
        matrix,
        (((1,), (1,)), ((), ())),
        precision=HIGH,
        preferred_element_type=F32,
    )[0:1]


def vec_mat(row, matrix):
    return lax.dot_general(
        jnp.broadcast_to(row, (8, LANES)),
        matrix,
        (((1,), (0,)), ((), ())),
        precision=HIGH,
        preferred_element_type=F32,
    )[0:1]


def surface_row(q):
    return 4 * (q // 2) + q % 2


def contact_first(partner, active, rows, gap0, pressure, mortar, state):
    gx = lax.axis_index("gx")
    half = rows.shape[0] // 2
    for k in range(2):
        own = rows[pl.ds(4 * gx + k, 1), :]
        master = rows[pl.ds(half + surface_row(partner[k]), 1), :]
        matrix = mortar[k]
        press = pressure[k : k + 1, :]
        flag = jnp.full((1, LANES), active[k], jnp.int32).astype(F32)
        gap = gap0[k : k + 1, :] - own - mat_vec(matrix, master)
        radius = jnp.sqrt(gap * gap + press * press + 0.01)
        complement = gap + press - radius
        slope_gap = 1.0 - gap / radius
        slope_press = 1.0 - press / radius
        divisor = slope_press + 0.5
        stiffness = flag * slope_gap / divisor
        excess = flag * complement / divisor
        traction = flag * press - excess
        state[k : k + 1, :] = stiffness
        state[2 + k : 3 + k, :] = complement
        state[4 + k : 5 + k, :] = slope_gap
        state[6 + k : 7 + k, :] = divisor
        state[8 + k : 9 + k, :] = flag
        state[10 + k : 11 + k, :] = press
        state[12 + k : 13 + k, :] = traction
        state[14 + k : 15 + k, :] = vec_mat(traction, matrix)


PLACES = ((0, 0, 0), (0, 3, -3), (1, 0, 0), (1, 3, -3), (0, 6, -6), (1, 6, -6), (2, 2, -2), (2, 0, 0))


def put_line(target, value, low_y, high_y, field, x):
    group, before, after = PLACES[field]
    part = slice(8 * group, 8 * group + 8)
    target[x, 0:8] = roll(low_y[x, part], before, 0)
    target[x, 8:40] = value
    target[x, 40:48] = roll(high_y[x, part], after, 0)


def plane_smoother():
    lane = iota((ROWS, LANES), 1)
    keep_low = jnp.where(lane > 0, 0.5, 0.0).astype(F32)
    keep_high = jnp.where(lane < LANES - 1, 0.5, 0.0).astype(F32)

    def in_plane(value):
        value = value + keep_low * roll(value, 1, 1) + keep_high * roll(value, -1, 1)
        return value + 0.5 * (roll(value, 1, 0) + roll(value, -1, 0))

    return in_plane


def along(ref, *at):
    *lead, x = at
    return ref[(*lead, x)] + 0.5 * (ref[(*lead, x - 1)] + ref[(*lead, x + 1)])


def base_surface(
    disp, force, kappa, sigma, low_x, high_x, low_y, high_y, state, package,
    moved, kap_lines, smooth_a, smooth_b, smooth_k, res,
):
    body = lax.axis_index("body")
    lines = tile_lines(disp, force, kappa, sigma)
    for x in range(2, LINES - 2):
        put_line(moved, ext_line(lines[2], low_x, high_x, 2, x), low_y, high_y, 2, x)
        put_line(kap_lines, ext_line(lines[3], low_x, high_x, 3, x), low_y, high_y, 3, x)
    in_plane = plane_smoother()

    @pl.loop(2, LINES - 2)
    def _(x):
        kap, value = kap_lines[x], moved[x]
        smooth_k[x] = in_plane(kap)
        smooth_a[x] = in_plane(value)
        smooth_b[x] = in_plane(kap * value)

    @pl.loop(0, 8)
    def _(k):
        x = k + 3
        kap = kap_lines[x]
        part = (8.0 * kap + along(smooth_k, x)) * moved[x] - kap * along(smooth_a, x) - along(smooth_b, x)
        res[k] = force[0, 2, k] - sigma[0, k] * moved[x, 8:40] - part[8:40]

    pieces = []
    for k in range(2):
        pieces.append(res[4 * k : 4 * k + 4].reshape(LANES, LANES).T[0:1])
    for k in range(2):
        pieces.append(jnp.where(body == 1, state[14 + k : 15 + k, :], state[12 + k : 13 + k, :]))
    four = stack_rows(pieces)
    fill(package, stack_rows([four, four]))


def base(
    disp, force, kappa, sigma, low_x, high_x, low_y, high_y,
    res_out, image_out, strips, moments,
    fields, diag, res, image, second, smooth_a, smooth_b, smooth_k,
):
    gx, gy = lax.axis_index("gx"), lax.axis_index("gy")
    lines = tile_lines(disp, force, kappa, sigma)
    for field in range(8):
        for x in range(LINES):
            value = ext_line(lines[field], low_x, high_x, field, x)
            if value is not None:
                put_line(fields.at[field], value, low_y, high_y, field, x)
    row = iota((ROWS, LANES), 0)
    in_plane = plane_smoother()
    row_low = jnp.where(gy == 0, 8, 0)
    row_high = jnp.where(gy == lax.axis_size("gy") - 1, 40, ROWS)
    inside_y = jnp.where((row >= row_low) & (row < row_high), 1.0, 0.0).astype(F32)
    line_low = jnp.where(gx == 0, 3, 0)
    line_high = jnp.where(gx == lax.axis_size("gx") - 1, 11, LINES)

    def inside(x):
        return inside_y * jnp.where((x >= line_low) & (x < line_high), 1.0, 0.0).astype(F32)

    @pl.loop(0, LINES)
    def _(x):
        kap = fields[3, x]
        smooth_k[x] = in_plane(kap)
        for c in range(3):
            value = fields[c, x]
            smooth_a[c, x] = in_plane(value)
            smooth_b[c, x] = in_plane(kap * value)

    @pl.loop(1, LINES - 1)
    def _(x):
        kap = fields[3, x]
        dia = fields[7, x] + 8.0 * kap + along(smooth_k, x)
        diag[x] = dia
        mask = inside(x)
        for c in range(3):
            value = fields[4 + c, x] - (
                dia * fields[c, x] - kap * along(smooth_a, c, x) - along(smooth_b, c, x)
            )
            res[c, x] = mask * value

    @pl.loop(1, LINES - 1)
    def _(x):
        kap = fields[3, x]
        for c in range(3):
            value = res[c, x]
            smooth_a[c, x] = in_plane(value)
            smooth_b[c, x] = in_plane(kap * value)

    @pl.loop(2, LINES - 2)
    def _(x):
        kap = fields[3, x]
        dia = diag[x]
        mask = inside(x)
        for c in range(3):
            image[c, x] = mask * (
                dia * res[c, x] - kap * along(smooth_a, c, x) - along(smooth_b, c, x)
            )

    @pl.loop(2, LINES - 2)
    def _(x):
        kap = fields[3, x]
        for c in range(3):
            value = image[c, x]
            smooth_a[c, x] = in_plane(value)
            smooth_b[c, x] = in_plane(kap * value)

    def finish(k, sums):
        x = k + 3
        kap = fields[3, x]
        dia = diag[x]
        sums = list(sums)
        for c in range(3):
            r, p = res[c, x, 8:40], image[c, x, 8:40]
            q = (dia * image[c, x] - kap * along(smooth_a, c, x) - along(smooth_b, c, x))[8:40]
            if c == 2:
                second[k] = q
            res_out[c, k] = r
            image_out[c, k] = p
            for i, (a, b) in enumerate(((r, r), (r, p), (p, p), (p, q))):
                product = (a * b).reshape(4, 8, LANES)
                sums[i] = sums[i] + ((product[0] + product[1]) + (product[2] + product[3]))
        return tuple(sums)

    sums = lax.fori_loop(0, 8, finish, (jnp.zeros((8, LANES), F32),) * 4)
    for i in range(4):
        moments[i] = sums[i]
    strips[...] = jnp.zeros(strips.shape, F32)
    lanes = iota((LANES, LANES), 1)
    for group in range(4):
        near = [min(max(4 * group - 1 + k, 1), LINES - 2) for k in range(4)]
        wide = stack_rows([fields[3, x, 8:40] for x in near])
        wide = jnp.where(lanes < 2, wide, roll(stack_rows([diag[x, 8:40] for x in near]), 2, 1))
        count = 4
        if group in (1, 2):
            count = 10
            for at, piece in (
                (4, stack_rows([res[2, x, 8:40] for x in near])),
                (6, stack_rows([image[2, x, 8:40] for x in near])),
                (8, stack_rows([second[x - 3] for x in near])),
            ):
                wide = jnp.where(lanes < at, wide, roll(piece, at, 1))
        turned = wide.T
        for kind in range(count):
            strips[kind, group : group + 1, :] = turned[kind : kind + 1]


def spread_row(select_rows, rows):
    half = rows.shape[0] // 2
    index = iota((half, LANES), 0) % 4
    select = jnp.where(index >= 2, select_rows[half:, :], 0.0)
    master = -lax.dot_general(
        select,
        rows[half:, :],
        (((0,), (0,)), ((), ())),
        precision=HIGH,
        preferred_element_type=F32,
    )[:half]
    slave = jnp.where(index < 2, -roll(rows[:half, :], -2, 0), 0.0)
    return slave, master


def own_extended(padded, gx):
    return stack_rows(
        [
            padded[pl.ds(4 * gx + 5, 1), :],
            padded[pl.ds(4 * gx + 8, 2), :],
            padded[pl.ds(4 * gx + 12, 1), :],
            jnp.zeros((4, LANES), F32),
        ]
    )


def put_padded(padded, value):
    half = value.shape[0]
    padded[0:8, :] = jnp.zeros((8, LANES), F32)
    padded[8 : 8 + half, :] = value
    padded[8 + half : 16 + half, :] = jnp.zeros((8, LANES), F32)


def contact_second(partner, select_rows, rows, state, mortar, strips, edges, out, padded, surf0, surf1):
    body, gx = lax.axis_index("body"), lax.axis_index("gx")
    half = rows.shape[0] // 2
    slave, master = spread_row(select_rows, rows)
    put_padded(padded, jnp.where(body == 0, slave, master))
    surf0[...] = rows[:half, :] + slave
    surf1[...] = rows[half:, :] + master
    first = own_extended(padded, gx)
    edges[0:8, :] = first
    edges[8:16, :] = strips[KAP0] * first
    for k in range(2):
        matrix = mortar[k]
        gap = -surf0[pl.ds(4 * gx + k, 1), :] - mat_vec(
            matrix, surf1[pl.ds(surface_row(partner[k]), 1), :]
        )
        push = state[k : k + 1, :] * gap
        pulled = vec_mat(push, matrix)
        out[k : k + 1, :] = gap
        out[2 + k : 3 + k, :] = push
        out[4 + k : 5 + k, :] = jnp.where(body == 1, pulled, push)
        out[6 + k : 7 + k, :] = strips[IM0, 1 + k : 2 + k, :]


def line_smooth(value):
    lane = iota(value.shape, 1)
    back, ahead = roll(value, 32, 1), roll(value, -32, 1)
    back = jnp.where(lane >= 32, back, roll(back, 1, 0))
    ahead = jnp.where(lane < 96, ahead, roll(ahead, -1, 0))
    return value + 0.5 * (back + ahead)


def row_smooth(value, low=None, high=None):
    y = iota(value.shape, 1) % 32
    before = 0.0 if low is None else roll(low, -31, 1)
    after = 0.0 if high is None else roll(high, 31, 1)
    before = jnp.where(y > 0, roll(value, 1, 1), before)
    after = jnp.where(y < 31, roll(value, -1, 1), after)
    return value + 0.5 * (before + after)


def couple(edges, low, high, strips, second, moved, package):
    gx = lax.axis_index("gx")
    first = edges[0:8, :]
    plain = line_smooth(row_smooth(first, low[0:8, :], high[0:8, :]))
    weighted = line_smooth(row_smooth(edges[8:16, :], low[8:16, :], high[8:16, :]))
    row = iota((8, LANES), 0)
    lowest = jnp.where(gx == 0, 1, 0)
    highest = jnp.where(gx == lax.axis_size("gx") - 1, 3, 4)
    mask = (row >= lowest) & (row < highest)
    kap0 = strips[KAP0]
    top = jnp.where(mask, strips[DIA0] * first - kap0 * plain - weighted, 0.0)
    below = jnp.where(mask, -0.5 * (strips[KAP1] * plain + weighted), 0.0)
    moved[0:8, :] = top
    moved[8:16, :] = below
    four = stack_rows([second[6:8, :] + top[1:3], second[4:6, :]])
    fill(package, stack_rows([four, four]))


def total(value):
    return jnp.sum(jnp.sum(value, axis=1, keepdims=True), axis=0, keepdims=True)


def measure_moments(
    partner, select_rows, rows, state, mortar, strips, edges, second, moved, moments,
    package, image_out, padded, surf0, surf1,
):
    body, gx = lax.axis_index("body"), lax.axis_index("gx")
    half = rows.shape[0] // 2
    slave, master = spread_row(select_rows, rows)
    put_padded(padded, jnp.where(body == 0, slave, master))
    surf0[...] = rows[:half, :] + slave
    surf1[...] = rows[half:, :] + master
    first = edges[0:8, :]
    k_first = moved[0:8, :]
    top = k_first + own_extended(padded, gx)
    below = moved[8:16, :]
    once = jnp.where(body == 0, 1.0, 0.0).astype(F32)
    push_sum = jnp.zeros((1, LANES), F32)
    gap_sum = jnp.zeros((1, LANES), F32)
    for k in range(2):
        gap = -surf0[pl.ds(4 * gx + k, 1), :] - mat_vec(
            mortar[k], surf1[pl.ds(surface_row(partner[k]), 1), :]
        )
        image_out[k : k + 1, :] = gap
        push_sum = push_sum + second[k : k + 1, :] * second[2 + k : 3 + k, :]
        gap_sum = gap_sum + state[k : k + 1, :] * gap * gap
    image_out[2:8, :] = jnp.zeros((6, LANES), F32)
    image_out[8:16, :] = top
    image_out[16:24, :] = below
    row = iota((8, LANES), 0)
    own = (row == 1) | (row == 2)
    kap0, kap1 = strips[KAP0], strips[KAP1]

    def surface_sum(value):
        return total(jnp.where(own, value, 0.0))

    im0, im1 = strips[IM0], strips[IM1]
    mu0 = total(moments[0]) + surface_sum(first * (2.0 * strips[RES0] + first))
    mu1 = total(moments[1]) + surface_sum(first * (2.0 * im0 + k_first)) + once * total(push_sum)
    mu2 = total(moments[2]) + surface_sum(top * (2.0 * im0 + top) + below * (2.0 * im1 + below))
    t_top = line_smooth(row_smooth(top + 0.5 * below))
    t_below = line_smooth(row_smooth(0.5 * top + below))
    mu3 = (
        total(moments[3])
        + surface_sum(
            top * (2.0 * strips[SEC0] + strips[DIA0] * top - 2.0 * kap0 * t_top)
            + below * (2.0 * strips[SEC1] + strips[DIA1] * below - 2.0 * kap1 * t_below)
        )
        + once * total(gap_sum)
    )
    lane = iota((8, LANES), 1)
    y = lane % 32
    send = jnp.zeros((8, LANES), F32)
    for k, value in enumerate((top, below, kap0 * top, kap1 * below)):
        send = send + jnp.where(y == 2 * k, roll(value, 2 * k, 1), 0.0)
        send = send + jnp.where(y == 2 * k + 1, roll(value, 2 * k + 1 - 31, 1), 0.0)
    for k, value in enumerate((mu0, mu1, mu2, mu3)):
        send = send + jnp.where((row == 0) & (lane == 16 + k), value, 0.0)
    send = send[0:4]
    fill(package, stack_rows([send, send]))


def reduce_column(rows, package):
    value = rows[...]
    count = value.shape[0]
    row, lane = iota(value.shape, 0), iota(value.shape, 1)
    place = row % 4
    following = roll(value, -4, 0)
    upper = [roll(value, -(2 * k + 1), 1) for k in range(4)]
    lower = [roll(following, -2 * k, 1) for k in range(4)]
    across = (
        upper[2] * line_smooth(lower[0] + 0.5 * lower[1])
        + upper[3] * line_smooth(0.5 * lower[0] + lower[1])
        + upper[0] * line_smooth(lower[2] + 0.5 * lower[3])
        + upper[1] * line_smooth(0.5 * lower[2] + lower[3])
    )
    counted = ((place == 1) | (place == 2)) & (lane % 32 == 0) & (row < count - 4)
    across = total(jnp.where(counted, across, 0.0))
    sums = jnp.sum(jnp.where(place == 0, value, 0.0), axis=0, keepdims=True)
    lane1 = iota((1, LANES), 1)
    sums = jnp.where((lane1 >= 16) & (lane1 < 20), sums, 0.0)
    sums = sums - jnp.where(lane1 == 19, across, 0.0)
    index = iota((8, LANES), 0)
    fill(package, jnp.where(index % 2 == 0, sums, 0.0))


def finish(rows, res, image, state, edges, second, last, increment, new_press):
    sums = jnp.sum(rows[...], axis=0, keepdims=True)
    lane = iota((1, LANES), 1)
    m0, m1, m2, m3 = [
        jnp.sum(jnp.where(lane == 16 + k, sums, 0.0), axis=1, keepdims=True) for k in range(4)
    ]
    alpha = m0 / m1
    left = alpha * alpha * m2 - m0
    beta = left / m0
    energy = (m1 - 2.0 * alpha * m2 + alpha * alpha * m3) - beta * left / alpha
    step = left / energy
    c_res = alpha + step * (1.0 + beta)
    c_im = -step * alpha
    for k in range(2):
        at = slice(k, k + 1)
        change = c_res * second[at, :] + c_im * last[at, :]
        press = state[10 + k : 11 + k, :]
        flag = state[8 + k : 9 + k, :]
        complement, slope = state[2 + k : 3 + k, :], state[4 + k : 5 + k, :]
        divisor = state[6 + k : 7 + k, :]
        new_press[at, :] = flag * (press - (complement + slope * change) / divisor)
    wide_res = jnp.broadcast_to(c_res, (8, LANES)).reshape(1, 8, LANES)
    wide_im = jnp.broadcast_to(c_im, (8, LANES)).reshape(1, 8, LANES)
    for c in range(3):
        for x in range(8):
            r = res[c, x].reshape(4, 8, LANES)
            p = image[c, x].reshape(4, 8, LANES)
            increment[0, c, x] = (wide_res * r + wide_im * p).reshape(32, LANES)
    for k in range(2):
        top = c_res * edges[1 + k : 2 + k, :] + c_im * last[9 + k : 10 + k, :]
        below = c_im * last[17 + k : 18 + k, :]
        wide = stack_rows([top, below, jnp.zeros((LANES - 2, LANES), F32)]).T
        for x in range(4):
            at = 4 * k + x
            increment[0, 2, at] = increment[0, 2, at] + wide[32 * x : 32 * x + 32]


def shifted(block, axis, step):
    count = lax.axis_size(axis)
    pairs = [(i, i + step) for i in range(count) if 0 <= i + step < count]
    return lax.ppermute(block, axis, pairs)


def on_device(disp, force, kappa, sigma, gap0, pressure, mortar, partner, active):
    nx, ny = lax.axis_size("gx"), lax.axis_size("gy")
    tile = (disp, force, kappa, sigma)
    whole = (8 * nx, LANES)
    row = ("body", "gx")

    def trade(package, axes):
        return lax.all_to_all(package, axes, 0, 0, tiled=True)

    slabs = (SLABS, 32, LANES)
    package = call(
        pack_surface,
        whole,
        (partner, disp),
        smem=(0,),
        away=(1,),
        scratch=[(8, 32, LANES)],
        more=[pltpu.SemaphoreType.DMA],
        limit=60,
    )
    surfaces = trade(package, row)
    up, down = call(
        pack_x,
        [slabs, slabs],
        (*tile, package),
        away=range(5),
        more=[pltpu.SemaphoreType.DMA((16,))],
        put=pltpu.HBM,
        limit=60,
    )
    low_x, high_x = shifted(up, "gx", 1), shifted(down, "gx", -1)
    rims = (LINES, 24, LANES)
    up, down = call(pack_y, [rims, rims], (*tile, low_x, high_x))
    low_y, high_y = shifted(up, "gy", 1), shifted(down, "gy", -1)
    state = call(
        contact_first,
        (16, LANES),
        (partner, active, surfaces, gap0, pressure, mortar),
        smem=(0, 1),
    )
    lines = (LINES, ROWS, LANES)
    rims = (low_x, high_x, low_y, high_y)
    package = call(
        base_surface,
        whole,
        (*tile, *rims, state),
        scratch=[lines, lines, lines, lines, lines, (8, 32, LANES)],
    )
    rows = trade(package, row)
    res, image, strips, moments = call(
        base,
        [(3, 8, 32, LANES), (3, 8, 32, LANES), (16, 8, LANES), (4, 8, LANES)],
        (*tile, *rims),
        scratch=[(8, *lines), lines, (3, *lines), (3, *lines), (8, 32, LANES), (3, *lines), (3, *lines), lines],
    )
    half = 4 * nx
    work = [(half + 16, LANES), (half, LANES), (half, LANES)]
    edges, second = call(
        contact_second,
        [(16, LANES), (8, LANES)],
        (partner, surfaces, rows, state, mortar, strips),
        smem=(0,),
        scratch=work,
    )
    low, high = shifted(edges, "gy", 1), shifted(edges, "gy", -1)
    moved, package = call(
        couple, [(16, LANES), whole], (edges, low, high, strips, second)
    )
    rows = trade(package, row)
    package, last = call(
        measure_moments,
        [(4 * ny, LANES), (24, LANES)],
        (partner, surfaces, rows, state, mortar, strips, edges, second, moved, moments),
        smem=(0,),
        scratch=work,
    )
    package = call(reduce_column, (4 * nx, LANES), (trade(package, "gy"),))
    sums = trade(package, row)
    increment, new_press = call(
        finish,
        [disp.shape, gap0.shape],
        (sums, res, image, state, edges, second, last),
    )
    return (increment, new_press)


def solution(mesh):
    placed = (
        P("body", None, "gx", "gy", None),
        P("body", None, "gx", "gy", None),
        P("body", "gx", "gy", None),
        P("body", "gx", "gy", None),
        P(("gx", "gy"), None),
        P(("gx", "gy"), None),
        P(("gx", "gy"), None, None),
        P(("gx", "gy")),
        P(("gx", "gy")),
    )
    return jax.shard_map(
        on_device,
        mesh=mesh,
        in_specs=placed,
        out_specs=(P("body", None, "gx", "gy", None), P(("gx", "gy"), None)),
        check_vma=False,
    )
```

```python
import jax
import jax.numpy as jnp
from jax import lax
from jax.experimental import pallas as pl
from jax.experimental.pallas import tpu as pltpu
from jax.sharding import PartitionSpec as P

HIGH = lax.Precision.HIGHEST
F32 = jnp.float32
LANES = 128
DEPTHS = (3, 3, 3, 3, 2, 2, 2, 2)
STARTS = (0, 3, 6, 9, 12, 14, 16, 18)
SLABS = 20
LINES = 14
ROWS = 48
KAP0, KAP1, DIA0, DIA1, RES0, IM0, IM1 = 0, 1, 2, 3, 4, 6, 7


def roll(value, step, axis):
    return pltpu.roll(value, step % value.shape[axis], axis)


def iota(shape, axis):
    return lax.broadcasted_iota(jnp.int32, shape, axis)


def call(body, outs, args, smem=(), away=(), scratch=(), more=(), limit=16):
    def space(i):
        return pltpu.SMEM if i in smem else pltpu.HBM if i in away else pltpu.VMEM

    specs = [pl.BlockSpec(memory_space=space(i)) for i in range(len(args))]
    many = isinstance(outs, list)
    shapes = [jax.ShapeDtypeStruct(s, F32) for s in (outs if many else [outs])]
    spec = pl.BlockSpec(memory_space=pltpu.VMEM)
    return pl.pallas_call(
        body,
        out_shape=shapes if many else shapes[0],
        in_specs=specs,
        out_specs=[spec] * len(shapes) if many else spec,
        scratch_shapes=[pltpu.VMEM(s, F32) for s in scratch] + list(more),
        compiler_params=pltpu.CompilerParams(vmem_limit_bytes=limit * 1024 * 1024),
    )(*args)


def fill(out, block):
    for at in range(0, out.shape[0], 8):
        out[at : at + 8, :] = block


def stack_rows(pieces):
    return jnp.concatenate(pieces, axis=0)


def tile_lines(disp, force, kappa, sigma):
    return (
        lambda x: disp[0, 0, x],
        lambda x: disp[0, 1, x],
        lambda x: disp[0, 2, x],
        lambda x: kappa[0, x],
        lambda x: force[0, 0, x],
        lambda x: force[0, 1, x],
        lambda x: force[0, 2, x],
        lambda x: sigma[0, x],
    )


def pack_x(partner, disp, force, kappa, sigma, up, down, package, surface, sems):
    sources = [disp.at[0, c] for c in range(3)] + [kappa.at[0]]
    sources += [force.at[0, c] for c in range(3)] + [sigma.at[0]]
    copies = [
        pltpu.make_async_copy(disp.at[0, 2], surface.at[0], sems.at[0]),
        pltpu.make_async_copy(kappa.at[0], surface.at[1], sems.at[1]),
    ]
    for k, (source, depth, start) in enumerate(zip(sources, DEPTHS, STARTS)):
        into = pl.ds(start, depth)
        at = 2 + 2 * k
        copies.append(
            pltpu.make_async_copy(source.at[pl.ds(8 - depth, depth)], up.at[into], sems.at[at])
        )
        copies.append(
            pltpu.make_async_copy(source.at[pl.ds(0, depth)], down.at[into], sems.at[at + 1])
        )
    for copy in copies:
        copy.start()
    for copy in copies[:2]:
        copy.wait()
    lanes = iota((LANES, LANES), 1)
    lane = iota((1, LANES), 1)
    first, second = [], []
    for k in range(2):
        field = surface[0, 4 * k : 4 * k + 4].reshape(LANES, LANES)
        kap = surface[1, 4 * k : 4 * k + 4].reshape(LANES, LANES)
        turned = jnp.where(lanes < 1, field, roll(kap, 1, 1)).T
        first.append(turned[0:1])
        place = surface_row(partner[k])
        hot = jnp.where(lane == 32 * (place // 16) + 1 + place % 16, 1.0, 0.0).astype(F32)
        second.append(jnp.where(edge_lanes(lane), turned[1:2], hot))
    four = stack_rows(first + second)
    fill(package, stack_rows([four, four]))
    for copy in copies[2:]:
        copy.wait()


def edge_lanes(lane):
    return (lane % 32 == 0) | (lane % 32 == 31)


def ext_line(line, low, high, field, x):
    depth, start = DEPTHS[field], STARTS[field]
    if x < 3:
        k = x - (3 - depth)
        return None if k < 0 else low[start + k]
    if x < 11:
        return line(x - 3)
    k = x - 11
    return None if k >= depth else high[start + k]


def pack_y(disp, force, kappa, sigma, low, high, up, down):
    lines = tile_lines(disp, force, kappa, sigma)
    sub = iota((8, LANES), 0)
    zero = jnp.zeros((8, LANES), F32)
    for x in range(LINES):
        last, first = [], []
        for field in range(8):
            value = ext_line(lines[field], low, high, field, x)
            last.append(zero if value is None else value[24:32])
            first.append(zero if value is None else value[0:8])
        for k, (a, b, c) in enumerate(((0, 1, 4), (2, 3, 5))):
            up[x, 8 * k : 8 * k + 8] = jnp.where(
                sub >= 5, last[a], jnp.where(sub >= 2, roll(last[b], -3, 0), roll(last[c], -6, 0))
            )
            down[x, 8 * k : 8 * k + 8] = jnp.where(
                sub < 3, first[a], jnp.where(sub < 6, roll(first[b], 3, 0), roll(first[c], 6, 0))
            )
        up[x, 16:24] = jnp.where(sub >= 6, last[7], roll(last[6], -2, 0))
        down[x, 16:24] = jnp.where(sub < 2, first[7], roll(first[6], 2, 0))


def mat_vec(matrix, row):
    return lax.dot_general(
        jnp.broadcast_to(row, (8, LANES)),
        matrix,
        (((1,), (1,)), ((), ())),
        precision=HIGH,
        preferred_element_type=F32,
    )[0:1]


def vec_mat(row, matrix):
    return lax.dot_general(
        jnp.broadcast_to(row, (8, LANES)),
        matrix,
        (((1,), (0,)), ((), ())),
        precision=HIGH,
        preferred_element_type=F32,
    )[0:1]


def surface_row(q):
    return 4 * (q // 2) + q % 2


def contact_first(partner, active, rows, gap0, pressure, mortar, state):
    gx = lax.axis_index("gx")
    half = rows.shape[0] // 2
    for k in range(2):
        own = rows[pl.ds(4 * gx + k, 1), :]
        master = rows[pl.ds(half + surface_row(partner[k]), 1), :]
        matrix = mortar[k]
        press = pressure[k : k + 1, :]
        flag = jnp.full((1, LANES), active[k], jnp.int32).astype(F32)
        gap = gap0[k : k + 1, :] - own - mat_vec(matrix, master)
        radius = jnp.sqrt(gap * gap + press * press + 0.01)
        complement = gap + press - radius
        slope_gap = 1.0 - gap / radius
        slope_press = 1.0 - press / radius
        divisor = slope_press + 0.5
        stiffness = flag * slope_gap / divisor
        excess = flag * complement / divisor
        traction = flag * press - excess
        state[k : k + 1, :] = stiffness
        state[2 + k : 3 + k, :] = complement
        state[4 + k : 5 + k, :] = slope_gap
        state[6 + k : 7 + k, :] = divisor
        state[8 + k : 9 + k, :] = flag
        state[10 + k : 11 + k, :] = press
        state[12 + k : 13 + k, :] = traction
        state[14 + k : 15 + k, :] = vec_mat(traction, matrix)


PLACES = ((0, 0, 0), (0, 3, -3), (1, 0, 0), (1, 3, -3), (0, 6, -6), (1, 6, -6), (2, 2, -2), (2, 0, 0))


def put_line(target, value, low_y, high_y, field, x):
    group, before, after = PLACES[field]
    part = slice(8 * group, 8 * group + 8)
    target[x, 0:8] = roll(low_y[x, part], before, 0)
    target[x, 8:40] = value
    target[x, 40:48] = roll(high_y[x, part], after, 0)


def plane_smoother():
    lane = iota((ROWS, LANES), 1)
    keep_low = jnp.where(lane > 0, 0.5, 0.0).astype(F32)
    keep_high = jnp.where(lane < LANES - 1, 0.5, 0.0).astype(F32)

    def in_plane(value):
        value = value + keep_low * roll(value, 1, 1) + keep_high * roll(value, -1, 1)
        return value + 0.5 * (roll(value, 1, 0) + roll(value, -1, 0))

    return in_plane


def along(ref, *at):
    *lead, x = at
    return ref[(*lead, x)] + 0.5 * (ref[(*lead, x - 1)] + ref[(*lead, x + 1)])


def base_surface(
    disp, force, kappa, sigma, low_x, high_x, low_y, high_y, state, package,
    moved, kap_lines, smooth_a, smooth_b, smooth_k, res,
):
    body = lax.axis_index("body")
    lines = tile_lines(disp, force, kappa, sigma)
    for x in range(2, LINES - 2):
        put_line(moved, ext_line(lines[2], low_x, high_x, 2, x), low_y, high_y, 2, x)
        put_line(kap_lines, ext_line(lines[3], low_x, high_x, 3, x), low_y, high_y, 3, x)
    in_plane = plane_smoother()

    @pl.loop(2, LINES - 2)
    def _(x):
        kap, value = kap_lines[x], moved[x]
        smooth_k[x] = in_plane(kap)
        smooth_a[x] = in_plane(value)
        smooth_b[x] = in_plane(kap * value)

    @pl.loop(0, 8)
    def _(k):
        x = k + 3
        kap = kap_lines[x]
        part = (8.0 * kap + along(smooth_k, x)) * moved[x] - kap * along(smooth_a, x) - along(smooth_b, x)
        res[k] = force[0, 2, k] - sigma[0, k] * moved[x, 8:40] - part[8:40]

    pieces = []
    for k in range(2):
        pieces.append(res[4 * k : 4 * k + 4].reshape(LANES, LANES).T[0:1])
    for k in range(2):
        pieces.append(jnp.where(body == 1, state[14 + k : 15 + k, :], state[12 + k : 13 + k, :]))
    four = stack_rows(pieces)
    fill(package, stack_rows([four, four]))


def base(
    disp, force, kappa, sigma, low_x, high_x, low_y, high_y,
    res_out, strips, image_out, kap_out, diag_out,
    fields, diag, res, image, smooth_a, smooth_b, smooth_k,
):
    gx, gy = lax.axis_index("gx"), lax.axis_index("gy")
    lines = tile_lines(disp, force, kappa, sigma)
    for field in range(8):
        for x in range(LINES):
            value = ext_line(lines[field], low_x, high_x, field, x)
            if value is not None:
                put_line(fields.at[field], value, low_y, high_y, field, x)
    row = iota((ROWS, LANES), 0)
    in_plane = plane_smoother()
    row_low = jnp.where(gy == 0, 8, 0)
    row_high = jnp.where(gy == lax.axis_size("gy") - 1, 40, ROWS)
    inside_y = jnp.where((row >= row_low) & (row < row_high), 1.0, 0.0).astype(F32)
    line_low = jnp.where(gx == 0, 3, 0)
    line_high = jnp.where(gx == lax.axis_size("gx") - 1, 11, LINES)

    def inside(x):
        return inside_y * jnp.where((x >= line_low) & (x < line_high), 1.0, 0.0).astype(F32)

    @pl.loop(0, LINES)
    def _(x):
        kap = fields[3, x]
        smooth_k[x] = in_plane(kap)
        for c in range(3):
            value = fields[c, x]
            smooth_a[c, x] = in_plane(value)
            smooth_b[c, x] = in_plane(kap * value)

    @pl.loop(1, LINES - 1)
    def _(x):
        kap = fields[3, x]
        dia = fields[7, x] + 8.0 * kap + along(smooth_k, x)
        diag[x] = dia
        mask = inside(x)
        for c in range(3):
            value = fields[4 + c, x] - (
                dia * fields[c, x] - kap * along(smooth_a, c, x) - along(smooth_b, c, x)
            )
            res[c, x] = mask * value

    @pl.loop(1, LINES - 1)
    def _(x):
        kap = fields[3, x]
        for c in range(3):
            value = res[c, x]
            smooth_a[c, x] = in_plane(value)
            smooth_b[c, x] = in_plane(kap * value)

    @pl.loop(2, LINES - 2)
    def _(x):
        kap = fields[3, x]
        dia = diag[x]
        mask = inside(x)
        for c in range(3):
            image[c, x] = mask * (
                dia * res[c, x] - kap * along(smooth_a, c, x) - along(smooth_b, c, x)
            )

    for c in range(3):
        for k in range(8):
            res_out[c, k] = res[c, k + 3, 8:40]
    for k in range(8):
        diag_out[k] = diag[k + 3, 8:40]
    for k in range(10):
        kap_out[k] = fields[3, k + 2]
        for c in range(3):
            image_out[c, k] = image[c, k + 2]
    strips[...] = jnp.zeros(strips.shape, F32)
    lanes = iota((LANES, LANES), 1)
    for group in range(4):
        near = [min(max(4 * group - 1 + k, 1), LINES - 2) for k in range(4)]
        wide = stack_rows([fields[3, x, 8:40] for x in near])
        wide = jnp.where(lanes < 2, wide, roll(stack_rows([diag[x, 8:40] for x in near]), 2, 1))
        count = 4
        if group in (1, 2):
            count = 8
            for at, piece in (
                (4, stack_rows([res[2, x, 8:40] for x in near])),
                (6, stack_rows([image[2, x, 8:40] for x in near])),
            ):
                wide = jnp.where(lanes < at, wide, roll(piece, at, 1))
        turned = wide.T
        for kind in range(count):
            strips[kind, group : group + 1, :] = turned[kind : kind + 1]


def base_moments(after, image, kap_lines, diag, res_own, moments, strips, smooth_a, smooth_b, second):
    in_plane = plane_smoother()

    @pl.loop(0, 10)
    def _(x):
        kap = kap_lines[x]
        for c in range(3):
            value = image[c, x]
            smooth_a[c, x] = in_plane(value)
            smooth_b[c, x] = in_plane(kap * value)

    def finish_line(k, sums):
        x = k + 1
        kap, dia = kap_lines[x, 8:40], diag[k]
        sums = list(sums)
        for c in range(3):
            r, p = res_own[c, k], image[c, x, 8:40]
            q = dia * p - kap * along(smooth_a, c, x)[8:40] - along(smooth_b, c, x)[8:40]
            if c == 2:
                second[k] = q
            for i, (a, b) in enumerate(((r, r), (r, p), (p, p), (p, q))):
                product = (a * b).reshape(4, 8, LANES)
                sums[i] = sums[i] + ((product[0] + product[1]) + (product[2] + product[3]))
        return tuple(sums)

    sums = lax.fori_loop(0, 8, finish_line, (jnp.zeros((8, LANES), F32),) * 4)
    for i in range(4):
        moments[i] = sums[i]
    strips[...] = jnp.zeros(strips.shape, F32)
    for group in range(2):
        turned = second[4 * group : 4 * group + 4].reshape(LANES, LANES).T
        for kind in range(2):
            strips[kind, 1 + group : 2 + group, :] = turned[kind : kind + 1]


def spread_row(select_rows, rows):
    half = rows.shape[0] // 2
    shape = (half, LANES)
    index, lane = iota(shape, 0) % 4, iota(shape, 1) % 32
    hot = (index >= 2) & (lane >= 1) & (lane <= 16)
    select = jnp.where(hot, select_rows[half:, :], 0.0)
    spots = lax.dot_general(
        select,
        rows[half:, :],
        (((0,), (0,)), ((), ())),
        precision=HIGH,
        preferred_element_type=F32,
    )
    size = min(half, 16)
    master = -stack_rows([spots[32 * k + 1 : 32 * k + 1 + size] for k in range(half // size)])
    slave = jnp.where(index < 2, -roll(rows[:half, :], -2, 0), 0.0)
    return slave, master


def edge_kappa(select_rows):
    value = roll(select_rows[...], -2, 0)
    shape = value.shape
    return jnp.where((iota(shape, 0) % 4 < 2) & edge_lanes(iota(shape, 1)), value, 0.0)


def row_line_smooth(value):
    row, lane = iota(value.shape, 0), iota(value.shape, 1)
    place, spot = row % 4, row % (value.shape[0] // 2)
    back, ahead = roll(value, 32, 1), roll(value, -32, 1)
    before = jnp.where(place == 0, roll(back, 3, 0), roll(back, 1, 0))
    before = jnp.where(spot == 0, 0.0, before)
    after = jnp.where(place == 0, roll(ahead, -1, 0), roll(ahead, -3, 0))
    after = jnp.where(spot == value.shape[0] // 2 - 3, 0.0, after)
    back = jnp.where(lane >= 32, back, before)
    ahead = jnp.where(lane < 96, ahead, after)
    return jnp.where(place < 2, value + 0.5 * (back + ahead), 0.0)


def own_extended(padded, gx):
    return stack_rows(
        [
            padded[pl.ds(4 * gx + 5, 1), :],
            padded[pl.ds(4 * gx + 8, 2), :],
            padded[pl.ds(4 * gx + 12, 1), :],
            jnp.zeros((4, LANES), F32),
        ]
    )


def put_padded(padded, value):
    half = value.shape[0]
    padded[0:8, :] = jnp.zeros((8, LANES), F32)
    padded[8 : 8 + half, :] = value
    padded[8 + half : 16 + half, :] = jnp.zeros((8, LANES), F32)


def contact_second(
    partner, select_rows, rows, state, mortar, strips,
    edges, out, moved, message, package, padded, surf0, surf1,
):
    body, gx = lax.axis_index("body"), lax.axis_index("gx")
    half = rows.shape[0] // 2
    slave, master = spread_row(select_rows, rows)
    put_padded(padded, jnp.where(body == 0, slave, master))
    surf0[...] = rows[:half, :] + slave
    surf1[...] = rows[half:, :] + master
    first = own_extended(padded, gx)
    edges[...] = first
    both = stack_rows([slave, master])
    scaled = edge_kappa(select_rows) * both
    y = iota(both.shape, 1) % 32
    scaled = jnp.where(y == 1, roll(scaled, 1, 1), jnp.where(y == 30, roll(scaled, -1, 1), 0.0))
    message[...] = jnp.where((y == 0) | (y == 31), both, scaled)
    sent = []
    for k in range(2):
        matrix = mortar[k]
        gap = -surf0[pl.ds(4 * gx + k, 1), :] - mat_vec(
            matrix, surf1[pl.ds(surface_row(partner[k]), 1), :]
        )
        push = state[k : k + 1, :] * gap
        pulled = vec_mat(push, matrix)
        out[k : k + 1, :] = gap
        out[2 + k : 3 + k, :] = push
        sent.append(jnp.where(body == 1, pulled, push))
    out[4:8, :] = jnp.zeros((4, LANES), F32)
    plain = line_smooth(row_smooth(first))
    weighted = line_smooth(row_smooth(strips[KAP0] * first))
    mask = inside_rows()
    top = jnp.where(mask, strips[DIA0] * first - strips[KAP0] * plain - weighted, 0.0)
    moved[0:8, :] = top
    moved[8:16, :] = jnp.where(mask, -0.5 * (strips[KAP1] * plain + weighted), 0.0)
    four = stack_rows([(strips[IM0] + top)[1:3]] + sent)
    fill(package, stack_rows([four, four]))


def inside_rows():
    gx = lax.axis_index("gx")
    row = iota((8, LANES), 0)
    lowest = jnp.where(gx == 0, 1, 0)
    highest = jnp.where(gx == lax.axis_size("gx") - 1, 3, 4)
    return (row >= lowest) & (row < highest)


def line_smooth(value):
    lane = iota(value.shape, 1)
    back, ahead = roll(value, 32, 1), roll(value, -32, 1)
    back = jnp.where(lane >= 32, back, roll(back, 1, 0))
    ahead = jnp.where(lane < 96, ahead, roll(ahead, -1, 0))
    return value + 0.5 * (back + ahead)


def row_smooth(value):
    y = iota(value.shape, 1) % 32
    before = jnp.where(y > 0, roll(value, 1, 1), 0.0)
    after = jnp.where(y < 31, roll(value, -1, 1), 0.0)
    return value + 0.5 * (before + after)


def total(value):
    return jnp.sum(jnp.sum(value, axis=1, keepdims=True), axis=0, keepdims=True)


def measure_moments(
    partner, select_rows, rows, state, mortar, strips, edges, second, moved, low, high,
    more_strips, moments, package, image_out, padded, surf0, surf1,
):
    body, gx = lax.axis_index("body"), lax.axis_index("gx")
    half = rows.shape[0] // 2
    slave, master = spread_row(select_rows, rows)
    y = iota(rows.shape, 1) % 32
    below_row, above_row = low[...], high[...]
    plain = jnp.where(y == 0, roll(below_row, -31, 1), jnp.where(y == 31, roll(above_row, 31, 1), 0.0))
    scaled = jnp.where(y == 0, roll(below_row, -30, 1), jnp.where(y == 31, roll(above_row, 30, 1), 0.0))
    plain, scaled = row_line_smooth(plain), row_line_smooth(scaled)
    added = -0.5 * (edge_kappa(select_rows) * plain + scaled)
    surf0[...] = rows[:half, :] + slave + added[:half]
    surf1[...] = rows[half:, :] + master + added[half:]

    def own_rows(value):
        put_padded(padded, jnp.where(body == 0, value[:half], value[half:]))
        return own_extended(padded, gx)

    plain, scaled = own_rows(plain), own_rows(scaled)
    put_padded(padded, jnp.where(body == 0, slave, master))
    mask = inside_rows()
    kap0, kap1 = strips[KAP0], strips[KAP1]
    first = edges[...]
    k_first = moved[0:8, :] - jnp.where(mask, 0.5 * (kap0 * plain + scaled), 0.0)
    top = k_first + own_extended(padded, gx)
    below = moved[8:16, :] - jnp.where(mask, 0.25 * (kap1 * plain + scaled), 0.0)
    once = jnp.where(body == 0, 1.0, 0.0).astype(F32)
    push_sum = jnp.zeros((1, LANES), F32)
    gap_sum = jnp.zeros((1, LANES), F32)
    for k in range(2):
        gap = -surf0[pl.ds(4 * gx + k, 1), :] - mat_vec(
            mortar[k], surf1[pl.ds(surface_row(partner[k]), 1), :]
        )
        image_out[k : k + 1, :] = gap
        push_sum = push_sum + second[k : k + 1, :] * second[2 + k : 3 + k, :]
        gap_sum = gap_sum + state[k : k + 1, :] * gap * gap
    image_out[2:8, :] = jnp.zeros((6, LANES), F32)
    image_out[8:16, :] = top
    image_out[16:24, :] = below
    row = iota((8, LANES), 0)
    own = (row == 1) | (row == 2)

    def surface_sum(value):
        return total(jnp.where(own, value, 0.0))

    im0, im1 = strips[IM0], strips[IM1]
    mu0 = total(moments[0]) + surface_sum(first * (2.0 * strips[RES0] + first))
    mu1 = total(moments[1]) + surface_sum(first * (2.0 * im0 + k_first)) + once * total(push_sum)
    mu2 = total(moments[2]) + surface_sum(top * (2.0 * im0 + top) + below * (2.0 * im1 + below))
    t_top = line_smooth(row_smooth(top + 0.5 * below))
    t_below = line_smooth(row_smooth(0.5 * top + below))
    mu3 = (
        total(moments[3])
        + surface_sum(
            top * (2.0 * more_strips[0] + strips[DIA0] * top - 2.0 * kap0 * t_top)
            + below * (2.0 * more_strips[1] + strips[DIA1] * below - 2.0 * kap1 * t_below)
        )
        + once * total(gap_sum)
    )
    lane = iota((8, LANES), 1)
    y = lane % 32
    send = jnp.zeros((8, LANES), F32)
    for k, value in enumerate((top, below, kap0 * top, kap1 * below)):
        send = send + jnp.where(y == 2 * k, roll(value, 2 * k, 1), 0.0)
        send = send + jnp.where(y == 2 * k + 1, roll(value, 2 * k + 1 - 31, 1), 0.0)
    for k, value in enumerate((mu0, mu1, mu2, mu3)):
        send = send + jnp.where((row == 0) & (lane == 16 + k), value, 0.0)
    send = send[0:4]
    fill(package, stack_rows([send, send]))


def reduce_column(rows, package):
    value = rows[...]
    count = value.shape[0]
    row, lane = iota(value.shape, 0), iota(value.shape, 1)
    place = row % 4
    following = roll(value, -4, 0)
    upper = [roll(value, -(2 * k + 1), 1) for k in range(4)]
    lower = [roll(following, -2 * k, 1) for k in range(4)]
    across = (
        upper[2] * line_smooth(lower[0] + 0.5 * lower[1])
        + upper[3] * line_smooth(0.5 * lower[0] + lower[1])
        + upper[0] * line_smooth(lower[2] + 0.5 * lower[3])
        + upper[1] * line_smooth(0.5 * lower[2] + lower[3])
    )
    counted = ((place == 1) | (place == 2)) & (lane % 32 == 0) & (row < count - 4)
    across = total(jnp.where(counted, across, 0.0))
    sums = jnp.sum(jnp.where(place == 0, value, 0.0), axis=0, keepdims=True)
    lane1 = iota((1, LANES), 1)
    sums = jnp.where((lane1 >= 16) & (lane1 < 20), sums, 0.0)
    sums = sums - jnp.where(lane1 == 19, across, 0.0)
    index = iota((8, LANES), 0)
    fill(package, jnp.where(index % 2 == 0, sums, 0.0))


def finish(rows, res, image, state, edges, second, last, increment, new_press):
    sums = jnp.sum(rows[...], axis=0, keepdims=True)
    lane = iota((1, LANES), 1)
    m0, m1, m2, m3 = [
        jnp.sum(jnp.where(lane == 16 + k, sums, 0.0), axis=1, keepdims=True) for k in range(4)
    ]
    alpha = m0 / m1
    left = alpha * alpha * m2 - m0
    beta = left / m0
    energy = (m1 - 2.0 * alpha * m2 + alpha * alpha * m3) - beta * left / alpha
    step = left / energy
    c_res = alpha + step * (1.0 + beta)
    c_im = -step * alpha
    for k in range(2):
        at = slice(k, k + 1)
        change = c_res * second[at, :] + c_im * last[at, :]
        press = state[10 + k : 11 + k, :]
        flag = state[8 + k : 9 + k, :]
        complement, slope = state[2 + k : 3 + k, :], state[4 + k : 5 + k, :]
        divisor = state[6 + k : 7 + k, :]
        new_press[at, :] = flag * (press - (complement + slope * change) / divisor)
    wide_res = jnp.broadcast_to(c_res, (8, LANES)).reshape(1, 8, LANES)
    wide_im = jnp.broadcast_to(c_im, (8, LANES)).reshape(1, 8, LANES)
    for c in range(3):
        for x in range(8):
            r = res[c, x].reshape(4, 8, LANES)
            p = image[c, x + 1, 8:40].reshape(4, 8, LANES)
            increment[0, c, x] = (wide_res * r + wide_im * p).reshape(32, LANES)
    for k in range(2):
        top = c_res * edges[1 + k : 2 + k, :] + c_im * last[9 + k : 10 + k, :]
        below = c_im * last[17 + k : 18 + k, :]
        wide = stack_rows([top, below, jnp.zeros((LANES - 2, LANES), F32)]).T
        for x in range(4):
            at = 4 * k + x
            increment[0, 2, at] = increment[0, 2, at] + wide[32 * x : 32 * x + 32]


def shifted(block, axis, step):
    count = lax.axis_size(axis)
    pairs = [(i, i + step) for i in range(count) if 0 <= i + step < count]
    return lax.ppermute(block, axis, pairs)


def on_device(disp, force, kappa, sigma, gap0, pressure, mortar, partner, active):
    nx, ny = lax.axis_size("gx"), lax.axis_size("gy")
    tile = (disp, force, kappa, sigma)
    whole = (8 * nx, LANES)
    row = ("body", "gx")

    def trade(package, axes):
        return lax.all_to_all(package, axes, 0, 0, tiled=True)

    slabs = (SLABS, 32, LANES)
    up, down, package = call(
        pack_x,
        [slabs, slabs, whole],
        (partner, *tile),
        smem=(0,),
        away=range(1, 5),
        scratch=[(2, 8, 32, LANES)],
        more=[pltpu.SemaphoreType.DMA((18,))],
        limit=60,
    )
    surfaces = trade(package, row)
    low_x, high_x = shifted(up, "gx", 1), shifted(down, "gx", -1)
    rims = (LINES, 24, LANES)
    up, down = call(pack_y, [rims, rims], (*tile, low_x, high_x))
    low_y, high_y = shifted(up, "gy", 1), shifted(down, "gy", -1)
    state = call(
        contact_first,
        (16, LANES),
        (partner, active, surfaces, gap0, pressure, mortar),
        smem=(0, 1),
    )
    lines = (LINES, ROWS, LANES)
    rims = (low_x, high_x, low_y, high_y)
    package = call(
        base_surface,
        whole,
        (*tile, *rims, state),
        scratch=[lines, lines, lines, lines, lines, (8, 32, LANES)],
    )
    rows = trade(package, row)
    wide, near = (3, *lines), (10, ROWS, LANES)
    res, strips, image, ext_kappa, diag = call(
        base,
        [(3, 8, 32, LANES), (8, 8, LANES), (3, *near), near, (8, 32, LANES)],
        (*tile, *rims),
        scratch=[(8, *lines), lines, wide, wide, wide, wide, lines],
    )
    half = 4 * nx
    work = [(half + 16, LANES), (half, LANES), (half, LANES)]
    edges, second, moved, message, package = call(
        contact_second,
        [(8, LANES), (8, LANES), (16, LANES), whole, whole],
        (partner, surfaces, rows, state, mortar, strips),
        smem=(0,),
        scratch=work,
    )
    low, high = shifted(message, "gy", 1), shifted(message, "gy", -1)
    rows = trade(package, row)
    moments, more_strips = call(
        base_moments,
        [(4, 8, LANES), (2, 8, LANES)],
        (edges, image, ext_kappa, diag, res),
        scratch=[(3, *near), (3, *near), (8, 32, LANES)],
    )
    package, last = call(
        measure_moments,
        [(4 * ny, LANES), (24, LANES)],
        (partner, surfaces, rows, state, mortar, strips, edges, second, moved, low, high, more_strips, moments),
        smem=(0,),
        scratch=work,
    )
    package = call(reduce_column, (4 * nx, LANES), (trade(package, "gy"),))
    sums = trade(package, row)
    increment, new_press = call(
        finish,
        [disp.shape, gap0.shape],
        (sums, res, image, state, edges, second, last),
    )
    return (increment, new_press)


def solution(mesh):
    placed = (
        P("body", None, "gx", "gy", None),
        P("body", None, "gx", "gy", None),
        P("body", "gx", "gy", None),
        P("body", "gx", "gy", None),
        P(("gx", "gy"), None),
        P(("gx", "gy"), None),
        P(("gx", "gy"), None, None),
        P(("gx", "gy")),
        P(("gx", "gy")),
    )
    return jax.shard_map(
        on_device,
        mesh=mesh,
        in_specs=placed,
        out_specs=(P("body", None, "gx", "gy", None), P(("gx", "gy"), None)),
        check_vma=False,
    )
```

```python
import jax
import jax.numpy as jnp
from jax import lax
from jax.experimental import pallas as pl
from jax.experimental.pallas import tpu as pltpu
from jax.sharding import PartitionSpec as P

HIGH = lax.Precision.HIGHEST
F32 = jnp.float32
LANES = 128
DEPTHS = (3, 3, 3, 3, 2, 2, 2, 2)
STARTS = (0, 3, 6, 9, 12, 14, 16, 18)
SLABS = 20
LINES = 14
ROWS = 48
KAP0, KAP1, DIA0, DIA1, RES0, IM0, IM1 = 0, 1, 2, 3, 4, 6, 7


def roll(value, step, axis):
    return pltpu.roll(value, step % value.shape[axis], axis)


def iota(shape, axis):
    return lax.broadcasted_iota(jnp.int32, shape, axis)


def call(body, outs, args, smem=(), away=(), far=(), scratch=(), more=(), limit=16):
    def space(i):
        return pltpu.SMEM if i in smem else pltpu.HBM if i in away else pltpu.VMEM

    specs = [pl.BlockSpec(memory_space=space(i)) for i in range(len(args))]
    many = isinstance(outs, list)
    shapes = [jax.ShapeDtypeStruct(s, F32) for s in (outs if many else [outs])]
    kept = [
        pl.BlockSpec(memory_space=pltpu.HBM if i in far else pltpu.VMEM) for i in range(len(shapes))
    ]
    return pl.pallas_call(
        body,
        out_shape=shapes if many else shapes[0],
        in_specs=specs,
        out_specs=kept if many else kept[0],
        scratch_shapes=[pltpu.VMEM(s, F32) for s in scratch] + list(more),
        compiler_params=pltpu.CompilerParams(vmem_limit_bytes=limit * 1024 * 1024),
    )(*args)


def fill(out, block):
    for at in range(0, out.shape[0], 8):
        out[at : at + 8, :] = block


def stack_rows(pieces):
    return jnp.concatenate(pieces, axis=0)


def tile_lines(disp, force, kappa, sigma):
    return (
        lambda x: disp[0, 0, x],
        lambda x: disp[0, 1, x],
        lambda x: disp[0, 2, x],
        lambda x: kappa[0, x],
        lambda x: force[0, 0, x],
        lambda x: force[0, 1, x],
        lambda x: force[0, 2, x],
        lambda x: sigma[0, x],
    )


def pack_x(partner, disp, force, kappa, sigma, up, down, package, surface, sems):
    sources = [disp.at[0, c] for c in range(3)] + [kappa.at[0]]
    sources += [force.at[0, c] for c in range(3)] + [sigma.at[0]]
    copies = [
        pltpu.make_async_copy(disp.at[0, 2], surface.at[0], sems.at[0]),
        pltpu.make_async_copy(kappa.at[0], surface.at[1], sems.at[1]),
    ]
    for k, (source, depth, start) in enumerate(zip(sources, DEPTHS, STARTS)):
        into = pl.ds(start, depth)
        at = 2 + 2 * k
        copies.append(
            pltpu.make_async_copy(source.at[pl.ds(8 - depth, depth)], up.at[into], sems.at[at])
        )
        copies.append(
            pltpu.make_async_copy(source.at[pl.ds(0, depth)], down.at[into], sems.at[at + 1])
        )
    for copy in copies:
        copy.start()
    for copy in copies[:2]:
        copy.wait()
    lanes = iota((LANES, LANES), 1)
    lane = iota((1, LANES), 1)
    first, second = [], []
    for k in range(2):
        field = surface[0, 4 * k : 4 * k + 4].reshape(LANES, LANES)
        kap = surface[1, 4 * k : 4 * k + 4].reshape(LANES, LANES)
        turned = jnp.where(lanes < 1, field, roll(kap, 1, 1)).T
        first.append(turned[0:1])
        place = surface_row(partner[k])
        hot = jnp.where(lane == 32 * (place // 16) + 1 + place % 16, 1.0, 0.0).astype(F32)
        second.append(jnp.where(edge_lanes(lane), turned[1:2], hot))
    four = stack_rows(first + second)
    fill(package, stack_rows([four, four]))
    for copy in copies[2:]:
        copy.wait()


def edge_lanes(lane):
    return (lane % 32 == 0) | (lane % 32 == 31)


def ext_line(line, low, high, field, x):
    depth, start = DEPTHS[field], STARTS[field]
    if x < 3:
        k = x - (3 - depth)
        return None if k < 0 else low[start + k]
    if x < 11:
        return line(x - 3)
    k = x - 11
    return None if k >= depth else high[start + k]


def pack_y(disp, force, kappa, sigma, low, high, up, down):
    lines = tile_lines(disp, force, kappa, sigma)
    sub = iota((8, LANES), 0)
    zero = jnp.zeros((8, LANES), F32)
    for x in range(LINES):
        last, first = [], []
        for field in range(8):
            value = ext_line(lines[field], low, high, field, x)
            last.append(zero if value is None else value[24:32])
            first.append(zero if value is None else value[0:8])
        for k, (a, b, c) in enumerate(((0, 1, 4), (2, 3, 5))):
            up[x, 8 * k : 8 * k + 8] = jnp.where(
                sub >= 5, last[a], jnp.where(sub >= 2, roll(last[b], -3, 0), roll(last[c], -6, 0))
            )
            down[x, 8 * k : 8 * k + 8] = jnp.where(
                sub < 3, first[a], jnp.where(sub < 6, roll(first[b], 3, 0), roll(first[c], 6, 0))
            )
        up[x, 16:24] = jnp.where(sub >= 6, last[7], roll(last[6], -2, 0))
        down[x, 16:24] = jnp.where(sub < 2, first[7], roll(first[6], 2, 0))


def mat_vec(matrix, row):
    return lax.dot_general(
        jnp.broadcast_to(row, (8, LANES)),
        matrix,
        (((1,), (1,)), ((), ())),
        precision=HIGH,
        preferred_element_type=F32,
    )[0:1]


def vec_mat(row, matrix):
    return lax.dot_general(
        jnp.broadcast_to(row, (8, LANES)),
        matrix,
        (((1,), (0,)), ((), ())),
        precision=HIGH,
        preferred_element_type=F32,
    )[0:1]


def surface_row(q):
    return 4 * (q // 2) + q % 2


def contact_first(partner, active, rows, gap0, pressure, mortar, state):
    gx = lax.axis_index("gx")
    half = rows.shape[0] // 2
    for k in range(2):
        own = rows[pl.ds(4 * gx + k, 1), :]
        master = rows[pl.ds(half + surface_row(partner[k]), 1), :]
        matrix = mortar[k]
        press = pressure[k : k + 1, :]
        flag = jnp.full((1, LANES), active[k], jnp.int32).astype(F32)
        gap = gap0[k : k + 1, :] - own - mat_vec(matrix, master)
        radius = jnp.sqrt(gap * gap + press * press + 0.01)
        complement = gap + press - radius
        slope_gap = 1.0 - gap / radius
        slope_press = 1.0 - press / radius
        divisor = slope_press + 0.5
        stiffness = flag * slope_gap / divisor
        excess = flag * complement / divisor
        traction = flag * press - excess
        state[k : k + 1, :] = stiffness
        state[2 + k : 3 + k, :] = complement
        state[4 + k : 5 + k, :] = slope_gap
        state[6 + k : 7 + k, :] = divisor
        state[8 + k : 9 + k, :] = flag
        state[10 + k : 11 + k, :] = press
        state[12 + k : 13 + k, :] = traction
        state[14 + k : 15 + k, :] = vec_mat(traction, matrix)


PLACES = ((0, 0, 0), (0, 3, -3), (1, 0, 0), (1, 3, -3), (0, 6, -6), (1, 6, -6), (2, 2, -2), (2, 0, 0))


def put_line(target, value, low_y, high_y, field, x):
    group, before, after = PLACES[field]
    part = slice(8 * group, 8 * group + 8)
    target[x, 0:8] = roll(low_y[x, part], before, 0)
    target[x, 8:40] = value
    target[x, 40:48] = roll(high_y[x, part], after, 0)


def plane_smoother():
    lane = iota((ROWS, LANES), 1)
    keep_low = jnp.where(lane > 0, 0.5, 0.0).astype(F32)
    keep_high = jnp.where(lane < LANES - 1, 0.5, 0.0).astype(F32)

    def in_plane(value):
        value = value + keep_low * roll(value, 1, 1) + keep_high * roll(value, -1, 1)
        return value + 0.5 * (roll(value, 1, 0) + roll(value, -1, 0))

    return in_plane


def along(ref, *at):
    *lead, x = at
    return ref[(*lead, x)] + 0.5 * (ref[(*lead, x - 1)] + ref[(*lead, x + 1)])


def base_surface(
    disp, force, kappa, sigma, low_x, high_x, low_y, high_y, state, package,
    moved, kap_lines, smooth_a, smooth_b, smooth_k, res,
):
    body = lax.axis_index("body")
    lines = tile_lines(disp, force, kappa, sigma)
    for x in range(2, LINES - 2):
        put_line(moved, ext_line(lines[2], low_x, high_x, 2, x), low_y, high_y, 2, x)
        put_line(kap_lines, ext_line(lines[3], low_x, high_x, 3, x), low_y, high_y, 3, x)
    in_plane = plane_smoother()

    @pl.loop(2, LINES - 2)
    def _(x):
        kap, value = kap_lines[x], moved[x]
        smooth_k[x] = in_plane(kap)
        smooth_a[x] = in_plane(value)
        smooth_b[x] = in_plane(kap * value)

    @pl.loop(0, 8)
    def _(k):
        x = k + 3
        kap = kap_lines[x]
        part = (8.0 * kap + along(smooth_k, x)) * moved[x] - kap * along(smooth_a, x) - along(smooth_b, x)
        res[k] = force[0, 2, k] - sigma[0, k] * moved[x, 8:40] - part[8:40]

    pieces = []
    for k in range(2):
        pieces.append(res[4 * k : 4 * k + 4].reshape(LANES, LANES).T[0:1])
    for k in range(2):
        pieces.append(jnp.where(body == 1, state[14 + k : 15 + k, :], state[12 + k : 13 + k, :]))
    four = stack_rows(pieces)
    fill(package, stack_rows([four, four]))


def base(
    disp, force, kappa, sigma, low_x, high_x, low_y, high_y,
    res_out, strips, image_out, kap_out, diag_out,
    fields, diag, res, image, smooth_a, smooth_b, smooth_k, sems,
):
    gx, gy = lax.axis_index("gx"), lax.axis_index("gy")
    lines = tile_lines(disp, force, kappa, sigma)
    for field in range(8):
        for x in range(LINES):
            value = ext_line(lines[field], low_x, high_x, field, x)
            if value is not None:
                put_line(fields.at[field], value, low_y, high_y, field, x)
    row = iota((ROWS, LANES), 0)
    in_plane = plane_smoother()
    row_low = jnp.where(gy == 0, 8, 0)
    row_high = jnp.where(gy == lax.axis_size("gy") - 1, 40, ROWS)
    inside_y = jnp.where((row >= row_low) & (row < row_high), 1.0, 0.0).astype(F32)
    line_low = jnp.where(gx == 0, 3, 0)
    line_high = jnp.where(gx == lax.axis_size("gx") - 1, 11, LINES)

    def inside(x):
        return inside_y * jnp.where((x >= line_low) & (x < line_high), 1.0, 0.0).astype(F32)

    @pl.loop(0, LINES)
    def _(x):
        kap = fields[3, x]
        smooth_k[x] = in_plane(kap)
        for c in range(3):
            value = fields[c, x]
            smooth_a[c, x] = in_plane(value)
            smooth_b[c, x] = in_plane(kap * value)

    @pl.loop(1, LINES - 1)
    def _(x):
        kap = fields[3, x]
        dia = fields[7, x] + 8.0 * kap + along(smooth_k, x)
        diag[x] = dia
        mask = inside(x)
        for c in range(3):
            value = fields[4 + c, x] - (
                dia * fields[c, x] - kap * along(smooth_a, c, x) - along(smooth_b, c, x)
            )
            res[c, x] = mask * value

    copies = [
        pltpu.make_async_copy(
            res.at[c, pl.ds(3, 8), pl.ds(8, 32)], res_out.at[c], sems.at[c]
        )
        for c in range(3)
    ]
    for copy in copies:
        copy.start()

    @pl.loop(1, LINES - 1)
    def _(x):
        kap = fields[3, x]
        for c in range(3):
            value = res[c, x]
            smooth_a[c, x] = in_plane(value)
            smooth_b[c, x] = in_plane(kap * value)

    @pl.loop(2, LINES - 2)
    def _(x):
        kap = fields[3, x]
        dia = diag[x]
        mask = inside(x)
        for c in range(3):
            image[c, x] = mask * (
                dia * res[c, x] - kap * along(smooth_a, c, x) - along(smooth_b, c, x)
            )

    for k in range(8):
        diag_out[k] = diag[k + 3, 8:40]
    for k in range(10):
        kap_out[k] = fields[3, k + 2]
        for c in range(3):
            image_out[c, k] = image[c, k + 2]
    strips[...] = jnp.zeros(strips.shape, F32)
    lanes = iota((LANES, LANES), 1)
    for group in range(4):
        near = [min(max(4 * group - 1 + k, 1), LINES - 2) for k in range(4)]
        wide = stack_rows([fields[3, x, 8:40] for x in near])
        wide = jnp.where(lanes < 2, wide, roll(stack_rows([diag[x, 8:40] for x in near]), 2, 1))
        count = 4
        if group in (1, 2):
            count = 8
            for at, piece in (
                (4, stack_rows([res[2, x, 8:40] for x in near])),
                (6, stack_rows([image[2, x, 8:40] for x in near])),
            ):
                wide = jnp.where(lanes < at, wide, roll(piece, at, 1))
        turned = wide.T
        for kind in range(count):
            strips[kind, group : group + 1, :] = turned[kind : kind + 1]
    for copy in copies:
        copy.wait()


def base_moments(after, image, kap_lines, diag, res_own, moments, strips, smooth_a, smooth_b, second):
    in_plane = plane_smoother()

    @pl.loop(0, 10)
    def _(x):
        kap = kap_lines[x]
        for c in range(3):
            value = image[c, x]
            smooth_a[c, x] = in_plane(value)
            smooth_b[c, x] = in_plane(kap * value)

    def finish_line(k, sums):
        x = k + 1
        kap, dia = kap_lines[x, 8:40], diag[k]
        sums = list(sums)
        for c in range(3):
            r, p = res_own[c, k], image[c, x, 8:40]
            q = dia * p - kap * along(smooth_a, c, x)[8:40] - along(smooth_b, c, x)[8:40]
            if c == 2:
                second[k] = q
            for i, (a, b) in enumerate(((r, r), (r, p), (p, p), (p, q))):
                product = (a * b).reshape(4, 8, LANES)
                sums[i] = sums[i] + ((product[0] + product[1]) + (product[2] + product[3]))
        return tuple(sums)

    sums = lax.fori_loop(0, 8, finish_line, (jnp.zeros((8, LANES), F32),) * 4)
    for i in range(4):
        moments[i] = sums[i]
    strips[...] = jnp.zeros(strips.shape, F32)
    for group in range(2):
        turned = second[4 * group : 4 * group + 4].reshape(LANES, LANES).T
        for kind in range(2):
            strips[kind, 1 + group : 2 + group, :] = turned[kind : kind + 1]


def spread_row(select_rows, rows):
    half = rows.shape[0] // 2
    shape = (half, LANES)
    index, lane = iota(shape, 0) % 4, iota(shape, 1) % 32
    hot = (index >= 2) & (lane >= 1) & (lane <= 16)
    select = jnp.where(hot, select_rows[half:, :], 0.0)
    spots = lax.dot_general(
        select,
        rows[half:, :],
        (((0,), (0,)), ((), ())),
        precision=HIGH,
        preferred_element_type=F32,
    )
    size = min(half, 16)
    master = -stack_rows([spots[32 * k + 1 : 32 * k + 1 + size] for k in range(half // size)])
    slave = jnp.where(index < 2, -roll(rows[:half, :], -2, 0), 0.0)
    return slave, master


def edge_kappa(select_rows):
    value = roll(select_rows[...], -2, 0)
    shape = value.shape
    return jnp.where((iota(shape, 0) % 4 < 2) & edge_lanes(iota(shape, 1)), value, 0.0)


def row_line_smooth(value):
    row, lane = iota(value.shape, 0), iota(value.shape, 1)
    place, spot = row % 4, row % (value.shape[0] // 2)
    back, ahead = roll(value, 32, 1), roll(value, -32, 1)
    before = jnp.where(place == 0, roll(back, 3, 0), roll(back, 1, 0))
    before = jnp.where(spot == 0, 0.0, before)
    after = jnp.where(place == 0, roll(ahead, -1, 0), roll(ahead, -3, 0))
    after = jnp.where(spot == value.shape[0] // 2 - 3, 0.0, after)
    back = jnp.where(lane >= 32, back, before)
    ahead = jnp.where(lane < 96, ahead, after)
    return jnp.where(place < 2, value + 0.5 * (back + ahead), 0.0)


def own_extended(padded, gx):
    return stack_rows(
        [
            padded[pl.ds(4 * gx + 5, 1), :],
            padded[pl.ds(4 * gx + 8, 2), :],
            padded[pl.ds(4 * gx + 12, 1), :],
            jnp.zeros((4, LANES), F32),
        ]
    )


def put_padded(padded, value):
    half = value.shape[0]
    padded[0:8, :] = jnp.zeros((8, LANES), F32)
    padded[8 : 8 + half, :] = value
    padded[8 + half : 16 + half, :] = jnp.zeros((8, LANES), F32)


def contact_second(
    partner, select_rows, rows, state, mortar, strips,
    edges, out, moved, message, package, padded, surf0, surf1,
):
    body, gx = lax.axis_index("body"), lax.axis_index("gx")
    half = rows.shape[0] // 2
    slave, master = spread_row(select_rows, rows)
    put_padded(padded, jnp.where(body == 0, slave, master))
    surf0[...] = rows[:half, :] + slave
    surf1[...] = rows[half:, :] + master
    first = own_extended(padded, gx)
    edges[...] = first
    both = stack_rows([slave, master])
    scaled = edge_kappa(select_rows) * both
    y = iota(both.shape, 1) % 32
    scaled = jnp.where(y == 1, roll(scaled, 1, 1), jnp.where(y == 30, roll(scaled, -1, 1), 0.0))
    message[...] = jnp.where((y == 0) | (y == 31), both, scaled)
    sent = []
    for k in range(2):
        matrix = mortar[k]
        gap = -surf0[pl.ds(4 * gx + k, 1), :] - mat_vec(
            matrix, surf1[pl.ds(surface_row(partner[k]), 1), :]
        )
        push = state[k : k + 1, :] * gap
        pulled = vec_mat(push, matrix)
        out[k : k + 1, :] = gap
        out[2 + k : 3 + k, :] = push
        sent.append(jnp.where(body == 1, pulled, push))
    out[4:8, :] = jnp.zeros((4, LANES), F32)
    plain = line_smooth(row_smooth(first))
    weighted = line_smooth(row_smooth(strips[KAP0] * first))
    mask = inside_rows()
    top = jnp.where(mask, strips[DIA0] * first - strips[KAP0] * plain - weighted, 0.0)
    moved[0:8, :] = top
    moved[8:16, :] = jnp.where(mask, -0.5 * (strips[KAP1] * plain + weighted), 0.0)
    four = stack_rows([(strips[IM0] + top)[1:3]] + sent)
    fill(package, stack_rows([four, four]))


def inside_rows():
    gx = lax.axis_index("gx")
    row = iota((8, LANES), 0)
    lowest = jnp.where(gx == 0, 1, 0)
    highest = jnp.where(gx == lax.axis_size("gx") - 1, 3, 4)
    return (row >= lowest) & (row < highest)


def line_smooth(value):
    lane = iota(value.shape, 1)
    back, ahead = roll(value, 32, 1), roll(value, -32, 1)
    back = jnp.where(lane >= 32, back, roll(back, 1, 0))
    ahead = jnp.where(lane < 96, ahead, roll(ahead, -1, 0))
    return value + 0.5 * (back + ahead)


def row_smooth(value):
    y = iota(value.shape, 1) % 32
    before = jnp.where(y > 0, roll(value, 1, 1), 0.0)
    after = jnp.where(y < 31, roll(value, -1, 1), 0.0)
    return value + 0.5 * (before + after)


def total(value):
    return jnp.sum(jnp.sum(value, axis=1, keepdims=True), axis=0, keepdims=True)


def measure_moments(
    partner, select_rows, rows, state, mortar, strips, edges, second, moved, beside,
    more_strips, moments, package, image_out, padded, surf0, surf1,
):
    body, gx = lax.axis_index("body"), lax.axis_index("gx")
    half = rows.shape[0] // 2
    slave, master = spread_row(select_rows, rows)
    y = iota(rows.shape, 1) % 32
    below_row, above_row = beside[: 2 * half, :], beside[2 * half :, :]
    plain = jnp.where(y == 0, roll(below_row, -31, 1), jnp.where(y == 31, roll(above_row, 31, 1), 0.0))
    scaled = jnp.where(y == 0, roll(below_row, -30, 1), jnp.where(y == 31, roll(above_row, 30, 1), 0.0))
    plain, scaled = row_line_smooth(plain), row_line_smooth(scaled)
    added = -0.5 * (edge_kappa(select_rows) * plain + scaled)
    surf0[...] = rows[:half, :] + slave + added[:half]
    surf1[...] = rows[half:, :] + master + added[half:]

    def own_rows(value):
        put_padded(padded, jnp.where(body == 0, value[:half], value[half:]))
        return own_extended(padded, gx)

    plain, scaled = own_rows(plain), own_rows(scaled)
    put_padded(padded, jnp.where(body == 0, slave, master))
    mask = inside_rows()
    kap0, kap1 = strips[KAP0], strips[KAP1]
    first = edges[...]
    k_first = moved[0:8, :] - jnp.where(mask, 0.5 * (kap0 * plain + scaled), 0.0)
    top = k_first + own_extended(padded, gx)
    below = moved[8:16, :] - jnp.where(mask, 0.25 * (kap1 * plain + scaled), 0.0)
    once = jnp.where(body == 0, 1.0, 0.0).astype(F32)
    push_sum = jnp.zeros((1, LANES), F32)
    gap_sum = jnp.zeros((1, LANES), F32)
    for k in range(2):
        gap = -surf0[pl.ds(4 * gx + k, 1), :] - mat_vec(
            mortar[k], surf1[pl.ds(surface_row(partner[k]), 1), :]
        )
        image_out[k : k + 1, :] = gap
        push_sum = push_sum + second[k : k + 1, :] * second[2 + k : 3 + k, :]
        gap_sum = gap_sum + state[k : k + 1, :] * gap * gap
    image_out[2:8, :] = jnp.zeros((6, LANES), F32)
    image_out[8:16, :] = top
    image_out[16:24, :] = below
    row = iota((8, LANES), 0)
    own = (row == 1) | (row == 2)

    def surface_sum(value):
        return total(jnp.where(own, value, 0.0))

    im0, im1 = strips[IM0], strips[IM1]
    mu0 = total(moments[0]) + surface_sum(first * (2.0 * strips[RES0] + first))
    mu1 = total(moments[1]) + surface_sum(first * (2.0 * im0 + k_first)) + once * total(push_sum)
    mu2 = total(moments[2]) + surface_sum(top * (2.0 * im0 + top) + below * (2.0 * im1 + below))
    t_top = line_smooth(row_smooth(top + 0.5 * below))
    t_below = line_smooth(row_smooth(0.5 * top + below))
    mu3 = (
        total(moments[3])
        + surface_sum(
            top * (2.0 * more_strips[0] + strips[DIA0] * top - 2.0 * kap0 * t_top)
            + below * (2.0 * more_strips[1] + strips[DIA1] * below - 2.0 * kap1 * t_below)
        )
        + once * total(gap_sum)
    )
    lane = iota((8, LANES), 1)
    y = lane % 32
    send = jnp.zeros((8, LANES), F32)
    for k, value in enumerate((top, below, kap0 * top, kap1 * below)):
        send = send + jnp.where(y == 2 * k, roll(value, 2 * k, 1), 0.0)
        send = send + jnp.where(y == 2 * k + 1, roll(value, 2 * k + 1 - 31, 1), 0.0)
    for k, value in enumerate((mu0, mu1, mu2, mu3)):
        send = send + jnp.where((row == 0) & (lane == 16 + k), value, 0.0)
    send = send[0:4]
    fill(package, stack_rows([send, send]))


def reduce_column(rows, package):
    value = rows[...]
    count = value.shape[0]
    row, lane = iota(value.shape, 0), iota(value.shape, 1)
    place = row % 4
    following = roll(value, -4, 0)
    upper = [roll(value, -(2 * k + 1), 1) for k in range(4)]
    lower = [roll(following, -2 * k, 1) for k in range(4)]
    across = (
        upper[2] * line_smooth(lower[0] + 0.5 * lower[1])
        + upper[3] * line_smooth(0.5 * lower[0] + lower[1])
        + upper[0] * line_smooth(lower[2] + 0.5 * lower[3])
        + upper[1] * line_smooth(0.5 * lower[2] + lower[3])
    )
    counted = ((place == 1) | (place == 2)) & (lane % 32 == 0) & (row < count - 4)
    across = total(jnp.where(counted, across, 0.0))
    sums = jnp.sum(jnp.where(place == 0, value, 0.0), axis=0, keepdims=True)
    lane1 = iota((1, LANES), 1)
    sums = jnp.where((lane1 >= 16) & (lane1 < 20), sums, 0.0)
    sums = sums - jnp.where(lane1 == 19, across, 0.0)
    index = iota((8, LANES), 0)
    fill(package, jnp.where(index % 2 == 0, sums, 0.0))


def finish(rows, res, image, state, edges, second, last, increment, new_press):
    sums = jnp.sum(rows[...], axis=0, keepdims=True)
    lane = iota((1, LANES), 1)
    m0, m1, m2, m3 = [
        jnp.sum(jnp.where(lane == 16 + k, sums, 0.0), axis=1, keepdims=True) for k in range(4)
    ]
    alpha = m0 / m1
    left = alpha * alpha * m2 - m0
    beta = left / m0
    energy = (m1 - 2.0 * alpha * m2 + alpha * alpha * m3) - beta * left / alpha
    step = left / energy
    c_res = alpha + step * (1.0 + beta)
    c_im = -step * alpha
    for k in range(2):
        at = slice(k, k + 1)
        change = c_res * second[at, :] + c_im * last[at, :]
        press = state[10 + k : 11 + k, :]
        flag = state[8 + k : 9 + k, :]
        complement, slope = state[2 + k : 3 + k, :], state[4 + k : 5 + k, :]
        divisor = state[6 + k : 7 + k, :]
        new_press[at, :] = flag * (press - (complement + slope * change) / divisor)
    wide_res = jnp.broadcast_to(c_res, (8, LANES)).reshape(1, 8, LANES)
    wide_im = jnp.broadcast_to(c_im, (8, LANES)).reshape(1, 8, LANES)
    for c in range(3):
        for x in range(8):
            r = res[c, x].reshape(4, 8, LANES)
            p = image[c, x + 1, 8:40].reshape(4, 8, LANES)
            increment[0, c, x] = (wide_res * r + wide_im * p).reshape(32, LANES)
    for k in range(2):
        top = c_res * edges[1 + k : 2 + k, :] + c_im * last[9 + k : 10 + k, :]
        below = c_im * last[17 + k : 18 + k, :]
        wide = stack_rows([top, below, jnp.zeros((LANES - 2, LANES), F32)]).T
        for x in range(4):
            at = 4 * k + x
            increment[0, 2, at] = increment[0, 2, at] + wide[32 * x : 32 * x + 32]


def shifted(block, axis, step):
    count = lax.axis_size(axis)
    pairs = [(i, i + step) for i in range(count) if 0 <= i + step < count]
    return lax.ppermute(block, axis, pairs)


def on_device(disp, force, kappa, sigma, gap0, pressure, mortar, partner, active):
    nx, ny = lax.axis_size("gx"), lax.axis_size("gy")
    tile = (disp, force, kappa, sigma)
    whole = (8 * nx, LANES)
    row = ("body", "gx")

    def trade(package, axes):
        return lax.all_to_all(package, axes, 0, 0, tiled=True)

    slabs = (SLABS, 32, LANES)
    up, down, package = call(
        pack_x,
        [slabs, slabs, whole],
        (partner, *tile),
        smem=(0,),
        away=range(1, 5),
        scratch=[(2, 8, 32, LANES)],
        more=[pltpu.SemaphoreType.DMA((18,))],
        limit=60,
    )
    surfaces = trade(package, row)
    low_x, high_x = shifted(up, "gx", 1), shifted(down, "gx", -1)
    rims = (LINES, 24, LANES)
    up, down = call(pack_y, [rims, rims], (*tile, low_x, high_x))
    low_y, high_y = shifted(up, "gy", 1), shifted(down, "gy", -1)
    state = call(
        contact_first,
        (16, LANES),
        (partner, active, surfaces, gap0, pressure, mortar),
        smem=(0, 1),
    )
    lines = (LINES, ROWS, LANES)
    rims = (low_x, high_x, low_y, high_y)
    package = call(
        base_surface,
        whole,
        (*tile, *rims, state),
        scratch=[lines, lines, lines, lines, lines, (8, 32, LANES)],
    )
    rows = trade(package, row)
    wide, near = (3, *lines), (10, ROWS, LANES)
    res, strips, image, ext_kappa, diag = call(
        base,
        [(3, 8, 32, LANES), (8, 8, LANES), (3, *near), near, (8, 32, LANES)],
        (*tile, *rims),
        far=(0,),
        scratch=[(8, *lines), lines, wide, wide, wide, wide, lines],
        more=[pltpu.SemaphoreType.DMA((3,))],
    )
    half = 4 * nx
    work = [(half + 16, LANES), (half, LANES), (half, LANES)]
    edges, second, moved, message, package = call(
        contact_second,
        [(8, LANES), (8, LANES), (16, LANES), whole, whole],
        (partner, surfaces, rows, state, mortar, strips),
        smem=(0,),
        scratch=work,
    )
    pairs = [(j, j + 1) for j in range(ny - 1)] + [(ny + j + 1, ny + j) for j in range(ny - 1)]
    message = lax.ppermute(message, ("body", "gy"), pairs)
    beside = lax.all_gather(message, "body", axis=0, tiled=True)
    rows = trade(package, row)
    moments, more_strips = call(
        base_moments,
        [(4, 8, LANES), (2, 8, LANES)],
        (edges, image, ext_kappa, diag, res),
        scratch=[(3, *near), (3, *near), (8, 32, LANES)],
    )
    package, last = call(
        measure_moments,
        [(4 * ny, LANES), (24, LANES)],
        (partner, surfaces, rows, state, mortar, strips, edges, second, moved, beside, more_strips, moments),
        smem=(0,),
        scratch=work,
    )
    package = call(reduce_column, (4 * nx, LANES), (trade(package, "gy"),))
    sums = trade(package, row)
    increment, new_press = call(
        finish,
        [disp.shape, gap0.shape],
        (sums, res, image, state, edges, second, last),
    )
    return (increment, new_press)


def solution(mesh):
    placed = (
        P("body", None, "gx", "gy", None),
        P("body", None, "gx", "gy", None),
        P("body", "gx", "gy", None),
        P("body", "gx", "gy", None),
        P(("gx", "gy"), None),
        P(("gx", "gy"), None),
        P(("gx", "gy"), None, None),
        P(("gx", "gy")),
        P(("gx", "gy")),
    )
    return jax.shard_map(
        on_device,
        mesh=mesh,
        in_specs=placed,
        out_specs=(P("body", None, "gx", "gy", None), P(("gx", "gy"), None)),
        check_vma=False,
    )
```

```python
import jax
import jax.numpy as jnp
from jax import lax
from jax.experimental import pallas as pl
from jax.experimental.pallas import tpu as pltpu
from jax.sharding import PartitionSpec as P

HIGH = lax.Precision.HIGHEST
F32 = jnp.float32
LANES = 128
DEPTHS = (3, 3, 3, 3, 2, 2, 2, 2)
STARTS = (0, 3, 6, 9, 12, 14, 16, 18)
SLABS = 20
LINES = 14
ROWS = 48
KAP0, KAP1, DIA0, DIA1, RES0, IM0, IM1, SEC0, SEC1 = 0, 1, 2, 3, 4, 6, 7, 8, 9


def roll(value, step, axis):
    return pltpu.roll(value, step % value.shape[axis], axis)


def iota(shape, axis):
    return lax.broadcasted_iota(jnp.int32, shape, axis)


def call(body, outs, args, smem=(), away=(), far=(), scratch=(), more=(), limit=16):
    def space(i):
        return pltpu.SMEM if i in smem else pltpu.HBM if i in away else pltpu.VMEM

    specs = [pl.BlockSpec(memory_space=space(i)) for i in range(len(args))]
    many = isinstance(outs, list)
    shapes = [jax.ShapeDtypeStruct(s, F32) for s in (outs if many else [outs])]
    kept = [
        pl.BlockSpec(memory_space=pltpu.HBM if i in far else pltpu.VMEM) for i in range(len(shapes))
    ]
    return pl.pallas_call(
        body,
        out_shape=shapes if many else shapes[0],
        in_specs=specs,
        out_specs=kept if many else kept[0],
        scratch_shapes=[pltpu.VMEM(s, F32) for s in scratch] + list(more),
        compiler_params=pltpu.CompilerParams(vmem_limit_bytes=limit * 1024 * 1024),
    )(*args)


def fill(out, block):
    for at in range(0, out.shape[0], 8):
        out[at : at + 8, :] = block


def stack_rows(pieces):
    return jnp.concatenate(pieces, axis=0)


def tile_lines(disp, force, kappa, sigma):
    return (
        lambda x: disp[0, 0, x],
        lambda x: disp[0, 1, x],
        lambda x: disp[0, 2, x],
        lambda x: kappa[0, x],
        lambda x: force[0, 0, x],
        lambda x: force[0, 1, x],
        lambda x: force[0, 2, x],
        lambda x: sigma[0, x],
    )


def each(first, last):
    def run(body):
        for k in range(first, last):
            body(k)

    return run


def pack_x(partner, disp, force, kappa, sigma, up, down, package, surface, sems):
    sources = [disp.at[0, c] for c in range(3)] + [kappa.at[0]]
    sources += [force.at[0, c] for c in range(3)] + [sigma.at[0]]
    copies = [
        pltpu.make_async_copy(disp.at[0, 2], surface.at[0], sems.at[0]),
        pltpu.make_async_copy(kappa.at[0], surface.at[1], sems.at[1]),
    ]
    for k, (source, depth, start) in enumerate(zip(sources, DEPTHS, STARTS)):
        into = pl.ds(start, depth)
        at = 2 + 2 * k
        copies.append(
            pltpu.make_async_copy(source.at[pl.ds(8 - depth, depth)], up.at[into], sems.at[at])
        )
        copies.append(
            pltpu.make_async_copy(source.at[pl.ds(0, depth)], down.at[into], sems.at[at + 1])
        )
    for copy in copies:
        copy.start()
    for copy in copies[:2]:
        copy.wait()
    lanes = iota((LANES, LANES), 1)
    lane = iota((1, LANES), 1)
    first, second = [], []
    for k in range(2):
        field = surface[0, 4 * k : 4 * k + 4].reshape(LANES, LANES)
        kap = surface[1, 4 * k : 4 * k + 4].reshape(LANES, LANES)
        turned = jnp.where(lanes < 1, field, roll(kap, 1, 1)).T
        first.append(turned[0:1])
        place = surface_row(partner[k])
        hot = jnp.where(lane == 32 * (place // 16) + 1 + place % 16, 1.0, 0.0).astype(F32)
        second.append(jnp.where(edge_lanes(lane), turned[1:2], hot))
    four = stack_rows(first + second)
    fill(package, stack_rows([four, four]))
    for copy in copies[2:]:
        copy.wait()


def edge_lanes(lane):
    return (lane % 32 == 0) | (lane % 32 == 31)


def ext_line(line, low, high, field, x):
    depth, start = DEPTHS[field], STARTS[field]
    if x < 3:
        k = x - (3 - depth)
        return None if k < 0 else low[start + k]
    if x < 11:
        return line(x - 3)
    k = x - 11
    return None if k >= depth else high[start + k]


def pack_y(disp, force, kappa, sigma, low, high, up, down):
    lines = tile_lines(disp, force, kappa, sigma)
    sub = iota((8, LANES), 0)
    zero = jnp.zeros((8, LANES), F32)
    for x in range(LINES):
        last, first = [], []
        for field in range(8):
            value = ext_line(lines[field], low, high, field, x)
            last.append(zero if value is None else value[24:32])
            first.append(zero if value is None else value[0:8])
        for k, (a, b, c) in enumerate(((0, 1, 4), (2, 3, 5))):
            up[x, 8 * k : 8 * k + 8] = jnp.where(
                sub >= 5, last[a], jnp.where(sub >= 2, roll(last[b], -3, 0), roll(last[c], -6, 0))
            )
            down[x, 8 * k : 8 * k + 8] = jnp.where(
                sub < 3, first[a], jnp.where(sub < 6, roll(first[b], 3, 0), roll(first[c], 6, 0))
            )
        up[x, 16:24] = jnp.where(sub >= 6, last[7], roll(last[6], -2, 0))
        down[x, 16:24] = jnp.where(sub < 2, first[7], roll(first[6], 2, 0))


def mat_vec(matrix, row):
    return lax.dot_general(
        jnp.broadcast_to(row, (8, LANES)),
        matrix,
        (((1,), (1,)), ((), ())),
        precision=HIGH,
        preferred_element_type=F32,
    )[0:1]


def vec_mat(row, matrix):
    return lax.dot_general(
        jnp.broadcast_to(row, (8, LANES)),
        matrix,
        (((1,), (0,)), ((), ())),
        precision=HIGH,
        preferred_element_type=F32,
    )[0:1]


def surface_row(q):
    return 4 * (q // 2) + q % 2


def contact_first(partner, active, rows, gap0, pressure, mortar, state):
    gx = lax.axis_index("gx")
    half = rows.shape[0] // 2
    for k in range(2):
        own = rows[pl.ds(4 * gx + k, 1), :]
        master = rows[pl.ds(half + surface_row(partner[k]), 1), :]
        matrix = mortar[k]
        press = pressure[k : k + 1, :]
        flag = jnp.full((1, LANES), active[k], jnp.int32).astype(F32)
        gap = gap0[k : k + 1, :] - own - mat_vec(matrix, master)
        radius = jnp.sqrt(gap * gap + press * press + 0.01)
        complement = gap + press - radius
        slope_gap = 1.0 - gap / radius
        slope_press = 1.0 - press / radius
        divisor = slope_press + 0.5
        stiffness = flag * slope_gap / divisor
        excess = flag * complement / divisor
        traction = flag * press - excess
        state[k : k + 1, :] = stiffness
        state[2 + k : 3 + k, :] = complement
        state[4 + k : 5 + k, :] = slope_gap
        state[6 + k : 7 + k, :] = divisor
        state[8 + k : 9 + k, :] = flag
        state[10 + k : 11 + k, :] = press
        state[12 + k : 13 + k, :] = traction
        state[14 + k : 15 + k, :] = vec_mat(traction, matrix)


PLACES = ((0, 0, 0), (0, 3, -3), (1, 0, 0), (1, 3, -3), (0, 6, -6), (1, 6, -6), (2, 2, -2), (2, 0, 0))


def put_line(target, value, low_y, high_y, field, x):
    group, before, after = PLACES[field]
    part = slice(8 * group, 8 * group + 8)
    target[x, 0:8] = roll(low_y[x, part], before, 0)
    target[x, 8:40] = value
    target[x, 40:48] = roll(high_y[x, part], after, 0)


def plane_smoother():
    lane = iota((ROWS, LANES), 1)
    keep_low = jnp.where(lane > 0, 0.5, 0.0).astype(F32)
    keep_high = jnp.where(lane < LANES - 1, 0.5, 0.0).astype(F32)

    def in_plane(value):
        value = value + keep_low * roll(value, 1, 1) + keep_high * roll(value, -1, 1)
        return value + 0.5 * (roll(value, 1, 0) + roll(value, -1, 0))

    return in_plane


def along(ref, *at):
    *lead, x = at
    return ref[(*lead, x)] + 0.5 * (ref[(*lead, x - 1)] + ref[(*lead, x + 1)])


def base_surface(
    disp, force, kappa, sigma, low_x, high_x, low_y, high_y, state, package,
    moved, kap_lines, smooth_a, smooth_b, smooth_k, res,
):
    body = lax.axis_index("body")
    lines = tile_lines(disp, force, kappa, sigma)
    for x in range(2, LINES - 2):
        put_line(moved, ext_line(lines[2], low_x, high_x, 2, x), low_y, high_y, 2, x)
        put_line(kap_lines, ext_line(lines[3], low_x, high_x, 3, x), low_y, high_y, 3, x)
    in_plane = plane_smoother()

    @each(2, LINES - 2)
    def _(x):
        kap, value = kap_lines[x], moved[x]
        smooth_k[x] = in_plane(kap)
        smooth_a[x] = in_plane(value)
        smooth_b[x] = in_plane(kap * value)

    @each(0, 8)
    def _(k):
        x = k + 3
        kap = kap_lines[x]
        part = (8.0 * kap + along(smooth_k, x)) * moved[x] - kap * along(smooth_a, x) - along(smooth_b, x)
        res[k] = force[0, 2, k] - sigma[0, k] * moved[x, 8:40] - part[8:40]

    pieces = []
    for k in range(2):
        pieces.append(res[4 * k : 4 * k + 4].reshape(LANES, LANES).T[0:1])
    for k in range(2):
        pieces.append(jnp.where(body == 1, state[14 + k : 15 + k, :], state[12 + k : 13 + k, :]))
    four = stack_rows(pieces)
    fill(package, stack_rows([four, four]))


def base(comps, surface):
    count = len(comps)

    def kernel(disp, force, kappa, sigma, low_x, high_x, low_y, high_y, after, *rest):
        res_out, image_out, moments, *rest = rest
        if surface:
            strips, *rest = rest
        inputs, pushes, kap_lines, sig_lines, diag, res, image, smooth_a, smooth_b, smooth_k, second = rest
        gx, gy = lax.axis_index("gx"), lax.axis_index("gy")
        lines = tile_lines(disp, force, kappa, sigma)
        targets = [(c, inputs.at[k]) for k, c in enumerate(comps)]
        targets += [(4 + c, pushes.at[k]) for k, c in enumerate(comps)]
        targets += [(3, kap_lines), (7, sig_lines)]
        for field, target in targets:
            for x in range(LINES):
                value = ext_line(lines[field], low_x, high_x, field, x)
                if value is not None:
                    put_line(target, value, low_y, high_y, field, x)
        row = iota((ROWS, LANES), 0)
        in_plane = plane_smoother()
        row_low = jnp.where(gy == 0, 8, 0)
        row_high = jnp.where(gy == lax.axis_size("gy") - 1, 40, ROWS)
        inside_y = jnp.where((row >= row_low) & (row < row_high), 1.0, 0.0).astype(F32)
        line_low = jnp.where(gx == 0, 3, 0)
        line_high = jnp.where(gx == lax.axis_size("gx") - 1, 11, LINES)

        def inside(x):
            return inside_y * jnp.where((x >= line_low) & (x < line_high), 1.0, 0.0).astype(F32)

        def smooth_all(source, first):
            @each(first, LINES - first)
            def _(x):
                kap = kap_lines[x]
                if first == 0:
                    smooth_k[x] = in_plane(kap)
                for c in range(count):
                    value = source[c, x]
                    smooth_a[c, x] = in_plane(value)
                    smooth_b[c, x] = in_plane(kap * value)

        smooth_all(inputs, 0)

        @each(1, LINES - 1)
        def _(x):
            kap = kap_lines[x]
            dia = sig_lines[x] + 8.0 * kap + along(smooth_k, x)
            diag[x] = dia
            mask = inside(x)
            for c in range(count):
                value = pushes[c, x] - (
                    dia * inputs[c, x] - kap * along(smooth_a, c, x) - along(smooth_b, c, x)
                )
                res[c, x] = mask * value

        smooth_all(res, 1)

        @each(2, LINES - 2)
        def _(x):
            kap, dia = kap_lines[x], diag[x]
            mask = inside(x)
            for c in range(count):
                image[c, x] = mask * (
                    dia * res[c, x] - kap * along(smooth_a, c, x) - along(smooth_b, c, x)
                )

        smooth_all(image, 2)

        def finish_line(k, sums):
            x = k + 3
            kap, dia = kap_lines[x, 8:40], diag[x, 8:40]
            sums = list(sums)
            for c in range(count):
                r, p = res[c, x, 8:40], image[c, x, 8:40]
                q = dia * p - kap * along(smooth_a, c, x)[8:40] - along(smooth_b, c, x)[8:40]
                if surface:
                    second[k] = q
                res_out[c, k] = r
                image_out[c, k] = p
                for i, (a, b) in enumerate(((r, r), (r, p), (p, p), (p, q))):
                    product = (a * b).reshape(4, 8, LANES)
                    sums[i] = sums[i] + ((product[0] + product[1]) + (product[2] + product[3]))
            return tuple(sums)

        sums = (jnp.zeros((8, LANES), F32),) * 4
        for k in range(8):
            sums = finish_line(k, sums)
        for i in range(4):
            moments[i] = sums[i]
        if not surface:
            return
        strips[...] = jnp.zeros(strips.shape, F32)
        lanes = iota((LANES, LANES), 1)
        for group in range(4):
            near = [min(max(4 * group - 1 + k, 1), LINES - 2) for k in range(4)]
            wide = stack_rows([kap_lines[x, 8:40] for x in near])
            wide = jnp.where(lanes < 2, wide, roll(stack_rows([diag[x, 8:40] for x in near]), 2, 1))
            total_kinds = 4
            if group in (1, 2):
                total_kinds = 10
                for at, piece in (
                    (4, stack_rows([res[0, x, 8:40] for x in near])),
                    (6, stack_rows([image[0, x, 8:40] for x in near])),
                    (8, stack_rows([second[x - 3] for x in near])),
                ):
                    wide = jnp.where(lanes < at, wide, roll(piece, at, 1))
            turned = wide.T
            for kind in range(total_kinds):
                strips[kind, group : group + 1, :] = turned[kind : kind + 1]

    def run(args):
        lines, wide = (LINES, ROWS, LANES), (count, LINES, ROWS, LANES)
        own = (count, 8, 32, LANES)
        outs = [own, own, (4, 8, LANES)] + ([(16, 8, LANES)] if surface else [])
        return call(
            kernel,
            outs,
            args,
            scratch=[wide, wide, lines, lines, lines, wide, wide, wide, wide, lines, (8, 32, LANES)],
        )

    return run


def spread_row(select_rows, rows):
    half = rows.shape[0] // 2
    shape = (half, LANES)
    index, lane = iota(shape, 0) % 4, iota(shape, 1) % 32
    hot = (index >= 2) & (lane >= 1) & (lane <= 16)
    select = jnp.where(hot, select_rows[half:, :], 0.0)
    spots = lax.dot_general(
        select,
        rows[half:, :],
        (((0,), (0,)), ((), ())),
        precision=HIGH,
        preferred_element_type=F32,
    )
    size = min(half, 16)
    master = -stack_rows([spots[32 * k + 1 : 32 * k + 1 + size] for k in range(half // size)])
    slave = jnp.where(index < 2, -roll(rows[:half, :], -2, 0), 0.0)
    return slave, master


def edge_kappa(select_rows):
    value = roll(select_rows[...], -2, 0)
    shape = value.shape
    return jnp.where((iota(shape, 0) % 4 < 2) & edge_lanes(iota(shape, 1)), value, 0.0)


def row_line_smooth(value):
    row, lane = iota(value.shape, 0), iota(value.shape, 1)
    place, spot = row % 4, row % (value.shape[0] // 2)
    back, ahead = roll(value, 32, 1), roll(value, -32, 1)
    before = jnp.where(place == 0, roll(back, 3, 0), roll(back, 1, 0))
    before = jnp.where(spot == 0, 0.0, before)
    after = jnp.where(place == 0, roll(ahead, -1, 0), roll(ahead, -3, 0))
    after = jnp.where(spot == value.shape[0] // 2 - 3, 0.0, after)
    back = jnp.where(lane >= 32, back, before)
    ahead = jnp.where(lane < 96, ahead, after)
    return jnp.where(place < 2, value + 0.5 * (back + ahead), 0.0)


def own_extended(padded, gx):
    return stack_rows(
        [
            padded[pl.ds(4 * gx + 5, 1), :],
            padded[pl.ds(4 * gx + 8, 2), :],
            padded[pl.ds(4 * gx + 12, 1), :],
            jnp.zeros((4, LANES), F32),
        ]
    )


def put_padded(padded, value):
    half = value.shape[0]
    padded[0:8, :] = jnp.zeros((8, LANES), F32)
    padded[8 : 8 + half, :] = value
    padded[8 + half : 16 + half, :] = jnp.zeros((8, LANES), F32)


def contact_second(
    partner, select_rows, rows, state, mortar, strips,
    edges, out, moved, message, package, padded, surf0, surf1,
):
    body, gx = lax.axis_index("body"), lax.axis_index("gx")
    half = rows.shape[0] // 2
    slave, master = spread_row(select_rows, rows)
    put_padded(padded, jnp.where(body == 0, slave, master))
    surf0[...] = rows[:half, :] + slave
    surf1[...] = rows[half:, :] + master
    first = own_extended(padded, gx)
    edges[...] = first
    both = stack_rows([slave, master])
    scaled = edge_kappa(select_rows) * both
    y = iota(both.shape, 1) % 32
    scaled = jnp.where(y == 1, roll(scaled, 1, 1), jnp.where(y == 30, roll(scaled, -1, 1), 0.0))
    message[...] = jnp.where((y == 0) | (y == 31), both, scaled)
    sent = []
    for k in range(2):
        matrix = mortar[k]
        gap = -surf0[pl.ds(4 * gx + k, 1), :] - mat_vec(
            matrix, surf1[pl.ds(surface_row(partner[k]), 1), :]
        )
        push = state[k : k + 1, :] * gap
        pulled = vec_mat(push, matrix)
        out[k : k + 1, :] = gap
        out[2 + k : 3 + k, :] = push
        sent.append(jnp.where(body == 1, pulled, push))
    out[4:8, :] = jnp.zeros((4, LANES), F32)
    plain = line_smooth(row_smooth(first))
    weighted = line_smooth(row_smooth(strips[KAP0] * first))
    mask = inside_rows()
    top = jnp.where(mask, strips[DIA0] * first - strips[KAP0] * plain - weighted, 0.0)
    moved[0:8, :] = top
    moved[8:16, :] = jnp.where(mask, -0.5 * (strips[KAP1] * plain + weighted), 0.0)
    four = stack_rows([(strips[IM0] + top)[1:3]] + sent)
    fill(package, stack_rows([four, four]))


def inside_rows():
    gx = lax.axis_index("gx")
    row = iota((8, LANES), 0)
    lowest = jnp.where(gx == 0, 1, 0)
    highest = jnp.where(gx == lax.axis_size("gx") - 1, 3, 4)
    return (row >= lowest) & (row < highest)


def line_smooth(value):
    lane = iota(value.shape, 1)
    back, ahead = roll(value, 32, 1), roll(value, -32, 1)
    back = jnp.where(lane >= 32, back, roll(back, 1, 0))
    ahead = jnp.where(lane < 96, ahead, roll(ahead, -1, 0))
    return value + 0.5 * (back + ahead)


def row_smooth(value):
    y = iota(value.shape, 1) % 32
    before = jnp.where(y > 0, roll(value, 1, 1), 0.0)
    after = jnp.where(y < 31, roll(value, -1, 1), 0.0)
    return value + 0.5 * (before + after)


def total(value):
    return jnp.sum(jnp.sum(value, axis=1, keepdims=True), axis=0, keepdims=True)


def measure_moments(
    partner, select_rows, rows, state, mortar, strips, edges, second, moved, beside,
    moments, more_moments, package, image_out, padded, surf0, surf1,
):
    body, gx = lax.axis_index("body"), lax.axis_index("gx")
    half = rows.shape[0] // 2
    slave, master = spread_row(select_rows, rows)
    y = iota(rows.shape, 1) % 32
    below_row, above_row = beside[: 2 * half, :], beside[2 * half :, :]
    plain = jnp.where(y == 0, roll(below_row, -31, 1), jnp.where(y == 31, roll(above_row, 31, 1), 0.0))
    scaled = jnp.where(y == 0, roll(below_row, -30, 1), jnp.where(y == 31, roll(above_row, 30, 1), 0.0))
    plain, scaled = row_line_smooth(plain), row_line_smooth(scaled)
    added = -0.5 * (edge_kappa(select_rows) * plain + scaled)
    surf0[...] = rows[:half, :] + slave + added[:half]
    surf1[...] = rows[half:, :] + master + added[half:]

    def own_rows(value):
        put_padded(padded, jnp.where(body == 0, value[:half], value[half:]))
        return own_extended(padded, gx)

    plain, scaled = own_rows(plain), own_rows(scaled)
    put_padded(padded, jnp.where(body == 0, slave, master))
    mask = inside_rows()
    kap0, kap1 = strips[KAP0], strips[KAP1]
    first = edges[...]
    k_first = moved[0:8, :] - jnp.where(mask, 0.5 * (kap0 * plain + scaled), 0.0)
    top = k_first + own_extended(padded, gx)
    below = moved[8:16, :] - jnp.where(mask, 0.25 * (kap1 * plain + scaled), 0.0)
    once = jnp.where(body == 0, 1.0, 0.0).astype(F32)
    push_sum = jnp.zeros((1, LANES), F32)
    gap_sum = jnp.zeros((1, LANES), F32)
    for k in range(2):
        gap = -surf0[pl.ds(4 * gx + k, 1), :] - mat_vec(
            mortar[k], surf1[pl.ds(surface_row(partner[k]), 1), :]
        )
        image_out[k : k + 1, :] = gap
        push_sum = push_sum + second[k : k + 1, :] * second[2 + k : 3 + k, :]
        gap_sum = gap_sum + state[k : k + 1, :] * gap * gap
    image_out[2:8, :] = jnp.zeros((6, LANES), F32)
    image_out[8:16, :] = top
    image_out[16:24, :] = below
    row = iota((8, LANES), 0)
    own = (row == 1) | (row == 2)

    def surface_sum(value):
        return total(jnp.where(own, value, 0.0))

    im0, im1 = strips[IM0], strips[IM1]
    mu0 = total(moments[0] + more_moments[0]) + surface_sum(first * (2.0 * strips[RES0] + first))
    mu1 = total(moments[1] + more_moments[1]) + surface_sum(first * (2.0 * im0 + k_first)) + once * total(push_sum)
    mu2 = total(moments[2] + more_moments[2]) + surface_sum(top * (2.0 * im0 + top) + below * (2.0 * im1 + below))
    t_top = line_smooth(row_smooth(top + 0.5 * below))
    t_below = line_smooth(row_smooth(0.5 * top + below))
    mu3 = (
        total(moments[3] + more_moments[3])
        + surface_sum(
            top * (2.0 * strips[SEC0] + strips[DIA0] * top - 2.0 * kap0 * t_top)
            + below * (2.0 * strips[SEC1] + strips[DIA1] * below - 2.0 * kap1 * t_below)
        )
        + once * total(gap_sum)
    )
    lane = iota((8, LANES), 1)
    y = lane % 32
    send = jnp.zeros((8, LANES), F32)
    for k, value in enumerate((top, below, kap0 * top, kap1 * below)):
        send = send + jnp.where(y == 2 * k, roll(value, 2 * k, 1), 0.0)
        send = send + jnp.where(y == 2 * k + 1, roll(value, 2 * k + 1 - 31, 1), 0.0)
    for k, value in enumerate((mu0, mu1, mu2, mu3)):
        send = send + jnp.where((row == 0) & (lane == 16 + k), value, 0.0)
    send = send[0:4]
    fill(package, stack_rows([send, send]))


def reduce_column(rows, package):
    value = rows[...]
    count = value.shape[0]
    row, lane = iota(value.shape, 0), iota(value.shape, 1)
    place = row % 4
    following = roll(value, -4, 0)
    upper = [roll(value, -(2 * k + 1), 1) for k in range(4)]
    lower = [roll(following, -2 * k, 1) for k in range(4)]
    across = (
        upper[2] * line_smooth(lower[0] + 0.5 * lower[1])
        + upper[3] * line_smooth(0.5 * lower[0] + lower[1])
        + upper[0] * line_smooth(lower[2] + 0.5 * lower[3])
        + upper[1] * line_smooth(0.5 * lower[2] + lower[3])
    )
    counted = ((place == 1) | (place == 2)) & (lane % 32 == 0) & (row < count - 4)
    across = total(jnp.where(counted, across, 0.0))
    sums = jnp.sum(jnp.where(place == 0, value, 0.0), axis=0, keepdims=True)
    lane1 = iota((1, LANES), 1)
    sums = jnp.where((lane1 >= 16) & (lane1 < 20), sums, 0.0)
    sums = sums - jnp.where(lane1 == 19, across, 0.0)
    index = iota((8, LANES), 0)
    fill(package, jnp.where(index % 2 == 0, sums, 0.0))


def finish(rows, res, image, res_2, image_2, state, edges, second, last, increment, new_press):
    sums = jnp.sum(rows[...], axis=0, keepdims=True)
    lane = iota((1, LANES), 1)
    m0, m1, m2, m3 = [
        jnp.sum(jnp.where(lane == 16 + k, sums, 0.0), axis=1, keepdims=True) for k in range(4)
    ]
    alpha = m0 / m1
    left = alpha * alpha * m2 - m0
    beta = left / m0
    energy = (m1 - 2.0 * alpha * m2 + alpha * alpha * m3) - beta * left / alpha
    step = left / energy
    c_res = alpha + step * (1.0 + beta)
    c_im = -step * alpha
    for k in range(2):
        at = slice(k, k + 1)
        change = c_res * second[at, :] + c_im * last[at, :]
        press = state[10 + k : 11 + k, :]
        flag = state[8 + k : 9 + k, :]
        complement, slope = state[2 + k : 3 + k, :], state[4 + k : 5 + k, :]
        divisor = state[6 + k : 7 + k, :]
        new_press[at, :] = flag * (press - (complement + slope * change) / divisor)
    wide_res = jnp.broadcast_to(c_res, (8, LANES)).reshape(1, 8, LANES)
    wide_im = jnp.broadcast_to(c_im, (8, LANES)).reshape(1, 8, LANES)
    for c in range(3):
        for x in range(8):
            r = (res_2[0, x] if c == 2 else res[c, x]).reshape(4, 8, LANES)
            p = (image_2[0, x] if c == 2 else image[c, x]).reshape(4, 8, LANES)
            increment[0, c, x] = (wide_res * r + wide_im * p).reshape(32, LANES)
    for k in range(2):
        top = c_res * edges[1 + k : 2 + k, :] + c_im * last[9 + k : 10 + k, :]
        below = c_im * last[17 + k : 18 + k, :]
        wide = stack_rows([top, below, jnp.zeros((LANES - 2, LANES), F32)]).T
        for x in range(4):
            at = 4 * k + x
            increment[0, 2, at] = increment[0, 2, at] + wide[32 * x : 32 * x + 32]


def shifted(block, axis, step):
    count = lax.axis_size(axis)
    pairs = [(i, i + step) for i in range(count) if 0 <= i + step < count]
    return lax.ppermute(block, axis, pairs)


def on_device(disp, force, kappa, sigma, gap0, pressure, mortar, partner, active):
    nx, ny = lax.axis_size("gx"), lax.axis_size("gy")
    tile = (disp, force, kappa, sigma)
    whole = (8 * nx, LANES)
    row = ("body", "gx")

    def trade(package, axes):
        return lax.all_to_all(package, axes, 0, 0, tiled=True)

    slabs = (SLABS, 32, LANES)
    up, down, package = call(
        pack_x,
        [slabs, slabs, whole],
        (partner, *tile),
        smem=(0,),
        away=range(1, 5),
        scratch=[(2, 8, 32, LANES)],
        more=[pltpu.SemaphoreType.DMA((18,))],
        limit=60,
    )
    surfaces = trade(package, row)
    low_x, high_x = shifted(up, "gx", 1), shifted(down, "gx", -1)
    rims = (LINES, 24, LANES)
    up, down = call(pack_y, [rims, rims], (*tile, low_x, high_x))
    low_y, high_y = shifted(up, "gy", 1), shifted(down, "gy", -1)
    state = call(
        contact_first,
        (16, LANES),
        (partner, active, surfaces, gap0, pressure, mortar),
        smem=(0, 1),
    )
    lines = (LINES, ROWS, LANES)
    rims = (low_x, high_x, low_y, high_y)
    package = call(
        base_surface,
        whole,
        (*tile, *rims, state),
        scratch=[lines, lines, lines, lines, lines, (8, 32, LANES)],
    )
    rows = trade(package, row)
    res_2, image_2, moments, strips = base((2,), True)((*tile, *rims, package))
    half = 4 * nx
    work = [(half + 16, LANES), (half, LANES), (half, LANES)]
    edges, second, moved, message, package = call(
        contact_second,
        [(8, LANES), (8, LANES), (16, LANES), whole, whole],
        (partner, surfaces, rows, state, mortar, strips),
        smem=(0,),
        scratch=work,
    )
    pairs = [(j, j + 1) for j in range(ny - 1)] + [(ny + j + 1, ny + j) for j in range(ny - 1)]
    message = lax.ppermute(message, ("body", "gy"), pairs)
    beside = lax.all_gather(message, "body", axis=0, tiled=True)
    rows = trade(package, row)
    res, image, more_moments = base((0, 1), False)((*tile, *rims, edges))
    package, last = call(
        measure_moments,
        [(4 * ny, LANES), (24, LANES)],
        (partner, surfaces, rows, state, mortar, strips, edges, second, moved, beside, moments, more_moments),
        smem=(0,),
        scratch=work,
    )
    package = call(reduce_column, (4 * nx, LANES), (trade(package, "gy"),))
    sums = trade(package, row)
    increment, new_press = call(
        finish,
        [disp.shape, gap0.shape],
        (sums, res, image, res_2, image_2, state, edges, second, last),
    )
    return (increment, new_press)


def solution(mesh):
    placed = (
        P("body", None, "gx", "gy", None),
        P("body", None, "gx", "gy", None),
        P("body", "gx", "gy", None),
        P("body", "gx", "gy", None),
        P(("gx", "gy"), None),
        P(("gx", "gy"), None),
        P(("gx", "gy"), None, None),
        P(("gx", "gy")),
        P(("gx", "gy")),
    )
    return jax.shard_map(
        on_device,
        mesh=mesh,
        in_specs=placed,
        out_specs=(P("body", None, "gx", "gy", None), P(("gx", "gy"), None)),
        check_vma=False,
    )
```

```python
import jax
import jax.numpy as jnp
from jax import lax
from jax.experimental import pallas as pl
from jax.experimental.pallas import tpu as pltpu
from jax.sharding import PartitionSpec as P

HIGH = lax.Precision.HIGHEST
F32 = jnp.float32
LANES = 128
DEPTHS = (3, 3, 3, 3, 2, 2, 2, 2)
STARTS = (0, 3, 6, 9, 12, 14, 16, 18)
SLABS = 20
LINES = 14
ROWS = 48
KAP0, KAP1, DIA0, DIA1, RES0, IM0, IM1, SEC0, SEC1 = 0, 1, 2, 3, 4, 6, 7, 8, 9


def roll(value, step, axis):
    return pltpu.roll(value, step % value.shape[axis], axis)


def iota(shape, axis):
    return lax.broadcasted_iota(jnp.int32, shape, axis)


def call(body, outs, args, smem=(), away=(), far=(), scratch=(), more=(), limit=16):
    def space(i):
        return pltpu.SMEM if i in smem else pltpu.HBM if i in away else pltpu.VMEM

    specs = [pl.BlockSpec(memory_space=space(i)) for i in range(len(args))]
    many = isinstance(outs, list)
    shapes = [jax.ShapeDtypeStruct(s, F32) for s in (outs if many else [outs])]
    kept = [
        pl.BlockSpec(memory_space=pltpu.HBM if i in far else pltpu.VMEM) for i in range(len(shapes))
    ]
    return pl.pallas_call(
        body,
        out_shape=shapes if many else shapes[0],
        in_specs=specs,
        out_specs=kept if many else kept[0],
        scratch_shapes=[pltpu.VMEM(s, F32) for s in scratch] + list(more),
        compiler_params=pltpu.CompilerParams(vmem_limit_bytes=limit * 1024 * 1024),
    )(*args)


def fill(out, block):
    for at in range(0, out.shape[0], 8):
        out[at : at + 8, :] = block


def stack_rows(pieces):
    return jnp.concatenate(pieces, axis=0)


def tile_lines(disp, force, kappa, sigma):
    return (
        lambda x: disp[0, 0, x],
        lambda x: disp[0, 1, x],
        lambda x: disp[0, 2, x],
        lambda x: kappa[0, x],
        lambda x: force[0, 0, x],
        lambda x: force[0, 1, x],
        lambda x: force[0, 2, x],
        lambda x: sigma[0, x],
    )


def each(first, last):
    def run(body):
        for k in range(first, last):
            body(k)

    return run


def pack_x(partner, disp, force, kappa, sigma, up, down, package, surface, sems):
    sources = [disp.at[0, c] for c in range(3)] + [kappa.at[0]]
    sources += [force.at[0, c] for c in range(3)] + [sigma.at[0]]
    copies = [
        pltpu.make_async_copy(disp.at[0, 2], surface.at[0], sems.at[0]),
        pltpu.make_async_copy(kappa.at[0], surface.at[1], sems.at[1]),
    ]
    for k, (source, depth, start) in enumerate(zip(sources, DEPTHS, STARTS)):
        into = pl.ds(start, depth)
        at = 2 + 2 * k
        copies.append(
            pltpu.make_async_copy(source.at[pl.ds(8 - depth, depth)], up.at[into], sems.at[at])
        )
        copies.append(
            pltpu.make_async_copy(source.at[pl.ds(0, depth)], down.at[into], sems.at[at + 1])
        )
    for copy in copies:
        copy.start()
    for copy in copies[:2]:
        copy.wait()
    lanes = iota((LANES, LANES), 1)
    lane = iota((1, LANES), 1)
    first, second = [], []
    for k in range(2):
        field = surface[0, 4 * k : 4 * k + 4].reshape(LANES, LANES)
        kap = surface[1, 4 * k : 4 * k + 4].reshape(LANES, LANES)
        turned = jnp.where(lanes < 1, field, roll(kap, 1, 1)).T
        first.append(turned[0:1])
        place = surface_row(partner[k])
        hot = jnp.where(lane == 32 * (place // 16) + 1 + place % 16, 1.0, 0.0).astype(F32)
        second.append(jnp.where(edge_lanes(lane), turned[1:2], hot))
    four = stack_rows(first + second)
    fill(package, stack_rows([four, four]))
    for copy in copies[2:]:
        copy.wait()


def edge_lanes(lane):
    return (lane % 32 == 0) | (lane % 32 == 31)


def ext_line(line, low, high, field, x):
    depth, start = DEPTHS[field], STARTS[field]
    if x < 3:
        k = x - (3 - depth)
        return None if k < 0 else low[start + k]
    if x < 11:
        return line(x - 3)
    k = x - 11
    return None if k >= depth else high[start + k]


def pack_y(disp, force, kappa, sigma, low, high, up, down):
    lines = tile_lines(disp, force, kappa, sigma)
    sub = iota((8, LANES), 0)
    zero = jnp.zeros((8, LANES), F32)
    for x in range(LINES):
        last, first = [], []
        for field in range(8):
            value = ext_line(lines[field], low, high, field, x)
            last.append(zero if value is None else value[24:32])
            first.append(zero if value is None else value[0:8])
        for k, (a, b, c) in enumerate(((0, 1, 4), (2, 3, 5))):
            up[x, 8 * k : 8 * k + 8] = jnp.where(
                sub >= 5, last[a], jnp.where(sub >= 2, roll(last[b], -3, 0), roll(last[c], -6, 0))
            )
            down[x, 8 * k : 8 * k + 8] = jnp.where(
                sub < 3, first[a], jnp.where(sub < 6, roll(first[b], 3, 0), roll(first[c], 6, 0))
            )
        up[x, 16:24] = jnp.where(sub >= 6, last[7], roll(last[6], -2, 0))
        down[x, 16:24] = jnp.where(sub < 2, first[7], roll(first[6], 2, 0))


def mat_vec(matrix, row):
    return lax.dot_general(
        jnp.broadcast_to(row, (8, LANES)),
        matrix,
        (((1,), (1,)), ((), ())),
        precision=HIGH,
        preferred_element_type=F32,
    )[0:1]


def vec_mat(row, matrix):
    return lax.dot_general(
        jnp.broadcast_to(row, (8, LANES)),
        matrix,
        (((1,), (0,)), ((), ())),
        precision=HIGH,
        preferred_element_type=F32,
    )[0:1]


def surface_row(q):
    return 4 * (q // 2) + q % 2


def contact_first(partner, active, rows, gap0, pressure, mortar, state):
    gx = lax.axis_index("gx")
    half = rows.shape[0] // 2
    for k in range(2):
        own = rows[pl.ds(4 * gx + k, 1), :]
        master = rows[pl.ds(half + surface_row(partner[k]), 1), :]
        matrix = mortar[k]
        press = pressure[k : k + 1, :]
        flag = jnp.full((1, LANES), active[k], jnp.int32).astype(F32)
        gap = gap0[k : k + 1, :] - own - mat_vec(matrix, master)
        radius = jnp.sqrt(gap * gap + press * press + 0.01)
        complement = gap + press - radius
        slope_gap = 1.0 - gap / radius
        slope_press = 1.0 - press / radius
        divisor = slope_press + 0.5
        stiffness = flag * slope_gap / divisor
        excess = flag * complement / divisor
        traction = flag * press - excess
        state[k : k + 1, :] = stiffness
        state[2 + k : 3 + k, :] = complement
        state[4 + k : 5 + k, :] = slope_gap
        state[6 + k : 7 + k, :] = divisor
        state[8 + k : 9 + k, :] = flag
        state[10 + k : 11 + k, :] = press
        state[12 + k : 13 + k, :] = traction
        state[14 + k : 15 + k, :] = vec_mat(traction, matrix)


PLACES = ((0, 0, 0), (0, 3, -3), (1, 0, 0), (1, 3, -3), (0, 6, -6), (1, 6, -6), (2, 2, -2), (2, 0, 0))


def put_line(target, value, low_y, high_y, field, x):
    group, before, after = PLACES[field]
    part = slice(8 * group, 8 * group + 8)
    target[x, 0:8] = roll(low_y[x, part], before, 0)
    target[x, 8:40] = value
    target[x, 40:48] = roll(high_y[x, part], after, 0)


def plane_smoother():
    lane = iota((ROWS, LANES), 1)
    keep_low = jnp.where(lane > 0, 0.5, 0.0).astype(F32)
    keep_high = jnp.where(lane < LANES - 1, 0.5, 0.0).astype(F32)

    def in_plane(value):
        value = value + keep_low * roll(value, 1, 1) + keep_high * roll(value, -1, 1)
        return value + 0.5 * (roll(value, 1, 0) + roll(value, -1, 0))

    return in_plane


def along(ref, *at):
    *lead, x = at
    return ref[(*lead, x)] + 0.5 * (ref[(*lead, x - 1)] + ref[(*lead, x + 1)])


def base_surface(
    disp, force, kappa, sigma, low_x, high_x, low_y, high_y, state, package,
    moved, kap_lines, smooth_a, smooth_b, smooth_k, res,
):
    body = lax.axis_index("body")
    lines = tile_lines(disp, force, kappa, sigma)
    for x in range(2, LINES - 2):
        put_line(moved, ext_line(lines[2], low_x, high_x, 2, x), low_y, high_y, 2, x)
        put_line(kap_lines, ext_line(lines[3], low_x, high_x, 3, x), low_y, high_y, 3, x)
    in_plane = plane_smoother()

    @each(2, LINES - 2)
    def _(x):
        kap, value = kap_lines[x], moved[x]
        smooth_k[x] = in_plane(kap)
        smooth_a[x] = in_plane(value)
        smooth_b[x] = in_plane(kap * value)

    @each(0, 8)
    def _(k):
        x = k + 3
        kap = kap_lines[x]
        part = (8.0 * kap + along(smooth_k, x)) * moved[x] - kap * along(smooth_a, x) - along(smooth_b, x)
        res[k] = force[0, 2, k] - sigma[0, k] * moved[x, 8:40] - part[8:40]

    pieces = []
    for k in range(2):
        pieces.append(res[4 * k : 4 * k + 4].reshape(LANES, LANES).T[0:1])
    for k in range(2):
        pieces.append(jnp.where(body == 1, state[14 + k : 15 + k, :], state[12 + k : 13 + k, :]))
    four = stack_rows(pieces)
    fill(package, stack_rows([four, four]))


def base(comps, surface):
    count = len(comps)

    def kernel(disp, force, kappa, sigma, low_x, high_x, low_y, high_y, after, *rest):
        res_out, image_out, moments, *rest = rest
        if surface:
            strips, *rest = rest
        inputs, pushes, kap_lines, sig_lines, diag, res, image, smooth_a, smooth_b, smooth_k, second = rest
        gx, gy = lax.axis_index("gx"), lax.axis_index("gy")
        lines = tile_lines(disp, force, kappa, sigma)
        targets = [(c, inputs.at[k]) for k, c in enumerate(comps)]
        targets += [(4 + c, pushes.at[k]) for k, c in enumerate(comps)]
        targets += [(3, kap_lines), (7, sig_lines)]
        for field, target in targets:
            for x in range(LINES):
                value = ext_line(lines[field], low_x, high_x, field, x)
                if value is not None:
                    put_line(target, value, low_y, high_y, field, x)
        row = iota((ROWS, LANES), 0)
        in_plane = plane_smoother()
        row_low = jnp.where(gy == 0, 8, 0)
        row_high = jnp.where(gy == lax.axis_size("gy") - 1, 40, ROWS)
        inside_y = jnp.where((row >= row_low) & (row < row_high), 1.0, 0.0).astype(F32)
        line_low = jnp.where(gx == 0, 3, 0)
        line_high = jnp.where(gx == lax.axis_size("gx") - 1, 11, LINES)

        def inside(x):
            return inside_y * jnp.where((x >= line_low) & (x < line_high), 1.0, 0.0).astype(F32)

        def smooth_all(source, first):
            @each(first, LINES - first)
            def _(x):
                kap = kap_lines[x]
                if first == 0:
                    smooth_k[x] = in_plane(kap)
                for c in range(count):
                    value = source[c, x]
                    smooth_a[c, x] = in_plane(value)
                    smooth_b[c, x] = in_plane(kap * value)

        smooth_all(inputs, 0)

        @each(1, LINES - 1)
        def _(x):
            kap = kap_lines[x]
            dia = sig_lines[x] + 8.0 * kap + along(smooth_k, x)
            diag[x] = dia
            mask = inside(x)
            for c in range(count):
                value = pushes[c, x] - (
                    dia * inputs[c, x] - kap * along(smooth_a, c, x) - along(smooth_b, c, x)
                )
                res[c, x] = mask * value

        smooth_all(res, 1)

        @each(2, LINES - 2)
        def _(x):
            kap, dia = kap_lines[x], diag[x]
            mask = inside(x)
            for c in range(count):
                image[c, x] = mask * (
                    dia * res[c, x] - kap * along(smooth_a, c, x) - along(smooth_b, c, x)
                )

        smooth_all(image, 2)

        def finish_line(k, sums):
            x = k + 3
            kap, dia = kap_lines[x, 8:40], diag[x, 8:40]
            sums = list(sums)
            for c in range(count):
                r, p = res[c, x, 8:40], image[c, x, 8:40]
                q = dia * p - kap * along(smooth_a, c, x)[8:40] - along(smooth_b, c, x)[8:40]
                if surface:
                    second[k] = q
                res_out[c, k] = r
                image_out[c, k] = p
                for i, (a, b) in enumerate(((r, r), (r, p), (p, p), (p, q))):
                    product = (a * b).reshape(4, 8, LANES)
                    sums[i] = sums[i] + ((product[0] + product[1]) + (product[2] + product[3]))
            return tuple(sums)

        sums = (jnp.zeros((8, LANES), F32),) * 4
        for k in range(8):
            sums = finish_line(k, sums)
        for i in range(4):
            moments[i] = sums[i]
        if not surface:
            return
        strips[...] = jnp.zeros(strips.shape, F32)
        lanes = iota((LANES, LANES), 1)
        for group in range(4):
            near = [min(max(4 * group - 1 + k, 1), LINES - 2) for k in range(4)]
            wide = stack_rows([kap_lines[x, 8:40] for x in near])
            wide = jnp.where(lanes < 2, wide, roll(stack_rows([diag[x, 8:40] for x in near]), 2, 1))
            total_kinds = 4
            if group in (1, 2):
                total_kinds = 10
                for at, piece in (
                    (4, stack_rows([res[0, x, 8:40] for x in near])),
                    (6, stack_rows([image[0, x, 8:40] for x in near])),
                    (8, stack_rows([second[x - 3] for x in near])),
                ):
                    wide = jnp.where(lanes < at, wide, roll(piece, at, 1))
            turned = wide.T
            for kind in range(total_kinds):
                strips[kind, group : group + 1, :] = turned[kind : kind + 1]

    def run(args):
        lines, wide = (LINES, ROWS, LANES), (count, LINES, ROWS, LANES)
        own = (count, 8, 32, LANES)
        outs = [own, own, (4, 8, LANES)] + ([(16, 8, LANES)] if surface else [])
        return call(
            kernel,
            outs,
            args,
            scratch=[wide, wide, lines, lines, lines, wide, wide, wide, wide, lines, (8, 32, LANES)],
        )

    return run


def spread_row(select_rows, rows):
    half = rows.shape[0] // 2
    shape = (half, LANES)
    index, lane = iota(shape, 0) % 4, iota(shape, 1) % 32
    hot = (index >= 2) & (lane >= 1) & (lane <= 16)
    select = jnp.where(hot, select_rows[half:, :], 0.0)
    spots = lax.dot_general(
        select,
        rows[half:, :],
        (((0,), (0,)), ((), ())),
        precision=HIGH,
        preferred_element_type=F32,
    )
    size = min(half, 16)
    master = -stack_rows([spots[32 * k + 1 : 32 * k + 1 + size] for k in range(half // size)])
    slave = jnp.where(index < 2, -roll(rows[:half, :], -2, 0), 0.0)
    return slave, master


def edge_kappa(select_rows):
    value = roll(select_rows[...], -2, 0)
    shape = value.shape
    return jnp.where((iota(shape, 0) % 4 < 2) & edge_lanes(iota(shape, 1)), value, 0.0)


def row_line_smooth(value):
    row, lane = iota(value.shape, 0), iota(value.shape, 1)
    place, spot = row % 4, row % (value.shape[0] // 2)
    back, ahead = roll(value, 32, 1), roll(value, -32, 1)
    before = jnp.where(place == 0, roll(back, 3, 0), roll(back, 1, 0))
    before = jnp.where(spot == 0, 0.0, before)
    after = jnp.where(place == 0, roll(ahead, -1, 0), roll(ahead, -3, 0))
    after = jnp.where(spot == value.shape[0] // 2 - 3, 0.0, after)
    back = jnp.where(lane >= 32, back, before)
    ahead = jnp.where(lane < 96, ahead, after)
    return jnp.where(place < 2, value + 0.5 * (back + ahead), 0.0)


def own_extended(padded, gx):
    return stack_rows(
        [
            padded[pl.ds(4 * gx + 5, 1), :],
            padded[pl.ds(4 * gx + 8, 2), :],
            padded[pl.ds(4 * gx + 12, 1), :],
            jnp.zeros((4, LANES), F32),
        ]
    )


def put_padded(padded, value):
    half = value.shape[0]
    padded[0:8, :] = jnp.zeros((8, LANES), F32)
    padded[8 : 8 + half, :] = value
    padded[8 + half : 16 + half, :] = jnp.zeros((8, LANES), F32)


def contact_second(
    partner, select_rows, rows, state, mortar, strips,
    edges, out, moved, message, package, padded, surf0, surf1,
):
    body, gx = lax.axis_index("body"), lax.axis_index("gx")
    half = rows.shape[0] // 2
    slave, master = spread_row(select_rows, rows)
    put_padded(padded, jnp.where(body == 0, slave, master))
    surf0[...] = rows[:half, :] + slave
    surf1[...] = rows[half:, :] + master
    first = own_extended(padded, gx)
    edges[...] = first
    both = stack_rows([slave, master])
    scaled = edge_kappa(select_rows) * both
    y = iota(both.shape, 1) % 32
    scaled = jnp.where(y == 1, roll(scaled, 1, 1), jnp.where(y == 30, roll(scaled, -1, 1), 0.0))
    message[...] = jnp.where((y == 0) | (y == 31), both, scaled)
    sent = []
    for k in range(2):
        matrix = mortar[k]
        gap = -surf0[pl.ds(4 * gx + k, 1), :] - mat_vec(
            matrix, surf1[pl.ds(surface_row(partner[k]), 1), :]
        )
        push = state[k : k + 1, :] * gap
        pulled = vec_mat(push, matrix)
        out[k : k + 1, :] = gap
        out[2 + k : 3 + k, :] = push
        sent.append(jnp.where(body == 1, pulled, push))
    out[4:8, :] = jnp.zeros((4, LANES), F32)
    plain = line_smooth(row_smooth(first))
    weighted = line_smooth(row_smooth(strips[KAP0] * first))
    mask = inside_rows()
    top = jnp.where(mask, strips[DIA0] * first - strips[KAP0] * plain - weighted, 0.0)
    moved[0:8, :] = top
    moved[8:16, :] = jnp.where(mask, -0.5 * (strips[KAP1] * plain + weighted), 0.0)
    four = stack_rows([(strips[IM0] + top)[1:3]] + sent)
    fill(package, stack_rows([four, four]))


def inside_rows():
    gx = lax.axis_index("gx")
    row = iota((8, LANES), 0)
    lowest = jnp.where(gx == 0, 1, 0)
    highest = jnp.where(gx == lax.axis_size("gx") - 1, 3, 4)
    return (row >= lowest) & (row < highest)


def line_smooth(value):
    lane = iota(value.shape, 1)
    back, ahead = roll(value, 32, 1), roll(value, -32, 1)
    back = jnp.where(lane >= 32, back, roll(back, 1, 0))
    ahead = jnp.where(lane < 96, ahead, roll(ahead, -1, 0))
    return value + 0.5 * (back + ahead)


def row_smooth(value):
    y = iota(value.shape, 1) % 32
    before = jnp.where(y > 0, roll(value, 1, 1), 0.0)
    after = jnp.where(y < 31, roll(value, -1, 1), 0.0)
    return value + 0.5 * (before + after)


def total(value):
    return jnp.sum(jnp.sum(value, axis=1, keepdims=True), axis=0, keepdims=True)


def measure_moments(
    partner, select_rows, rows, state, mortar, strips, edges, second, moved, beside,
    moments, more_moments, package, image_out, padded, surf0, surf1,
):
    body, gx = lax.axis_index("body"), lax.axis_index("gx")
    half = rows.shape[0] // 2
    slave, master = spread_row(select_rows, rows)
    y = iota(rows.shape, 1) % 32
    below_row, above_row = beside[: 2 * half, :], beside[2 * half :, :]
    plain = jnp.where(y == 0, roll(below_row, -31, 1), jnp.where(y == 31, roll(above_row, 31, 1), 0.0))
    scaled = jnp.where(y == 0, roll(below_row, -30, 1), jnp.where(y == 31, roll(above_row, 30, 1), 0.0))
    plain, scaled = row_line_smooth(plain), row_line_smooth(scaled)
    added = -0.5 * (edge_kappa(select_rows) * plain + scaled)
    surf0[...] = rows[:half, :] + slave + added[:half]
    surf1[...] = rows[half:, :] + master + added[half:]

    def own_rows(value):
        put_padded(padded, jnp.where(body == 0, value[:half], value[half:]))
        return own_extended(padded, gx)

    plain, scaled = own_rows(plain), own_rows(scaled)
    put_padded(padded, jnp.where(body == 0, slave, master))
    mask = inside_rows()
    kap0, kap1 = strips[KAP0], strips[KAP1]
    first = edges[...]
    k_first = moved[0:8, :] - jnp.where(mask, 0.5 * (kap0 * plain + scaled), 0.0)
    top = k_first + own_extended(padded, gx)
    below = moved[8:16, :] - jnp.where(mask, 0.25 * (kap1 * plain + scaled), 0.0)
    once = jnp.where(body == 0, 1.0, 0.0).astype(F32)
    push_sum = jnp.zeros((1, LANES), F32)
    gap_sum = jnp.zeros((1, LANES), F32)
    for k in range(2):
        gap = -surf0[pl.ds(4 * gx + k, 1), :] - mat_vec(
            mortar[k], surf1[pl.ds(surface_row(partner[k]), 1), :]
        )
        image_out[k : k + 1, :] = gap
        push_sum = push_sum + second[k : k + 1, :] * second[2 + k : 3 + k, :]
        gap_sum = gap_sum + state[k : k + 1, :] * gap * gap
    image_out[2:8, :] = jnp.zeros((6, LANES), F32)
    image_out[8:16, :] = top
    image_out[16:24, :] = below
    row = iota((8, LANES), 0)
    own = (row == 1) | (row == 2)

    def surface_sum(value):
        return total(jnp.where(own, value, 0.0))

    im0, im1 = strips[IM0], strips[IM1]
    mu0 = total(moments[0] + more_moments[0]) + surface_sum(first * (2.0 * strips[RES0] + first))
    mu1 = total(moments[1] + more_moments[1]) + surface_sum(first * (2.0 * im0 + k_first)) + once * total(push_sum)
    mu2 = total(moments[2] + more_moments[2]) + surface_sum(top * (2.0 * im0 + top) + below * (2.0 * im1 + below))
    t_top = line_smooth(row_smooth(top + 0.5 * below))
    t_below = line_smooth(row_smooth(0.5 * top + below))
    mu3 = (
        total(moments[3] + more_moments[3])
        + surface_sum(
            top * (2.0 * strips[SEC0] + strips[DIA0] * top - 2.0 * kap0 * t_top)
            + below * (2.0 * strips[SEC1] + strips[DIA1] * below - 2.0 * kap1 * t_below)
        )
        + once * total(gap_sum)
    )
    lane = iota((8, LANES), 1)
    y = lane % 32
    send = jnp.zeros((8, LANES), F32)
    for k, value in enumerate((top, below, kap0 * top, kap1 * below)):
        send = send + jnp.where(y == 2 * k, roll(value, 2 * k, 1), 0.0)
        send = send + jnp.where(y == 2 * k + 1, roll(value, 2 * k + 1 - 31, 1), 0.0)
    for k, value in enumerate((mu0, mu1, mu2, mu3)):
        send = send + jnp.where((row == 0) & (lane == 16 + k), value, 0.0)
    send = send[0:4]
    fill(package, stack_rows([send, send]))


def two_sum(a, b):
    total_of = a + b
    shift = total_of - a
    return total_of, (a - (total_of - shift)) + (b - shift)


def halves(a):
    big = 4097.0 * a
    high = big - (big - a)
    return high, a - high


def pair_add(x, y):
    high, low = two_sum(x[0], y[0])
    return two_sum(high, low + (x[1] + y[1]))


def pair_mul(x, y):
    product = x[0] * y[0]
    a, b = halves(x[0])
    c, d = halves(y[0])
    error = ((a * c - product) + a * d + b * c) + b * d
    return two_sum(product, error + (x[0] * y[1] + x[1] * y[0]))


def pair_scale(x, factor):
    return x[0] * factor, x[1] * factor


def pair_div(x, y):
    first = x[0] / y[0]
    zero = jnp.zeros_like(first)
    rest = pair_add(x, pair_scale(pair_mul(y, (first, zero)), -1.0))
    return two_sum(first, rest[0] / y[0])


def pair_rows(high, low):
    while high.shape[0] > 8:
        half = high.shape[0] // 2
        sums, error = two_sum(high[:half], high[half:])
        low = (low[:half] + low[half:]) + error
        high = sums
    for step in (4, 2, 1):
        sums, error = two_sum(high, roll(high, step, 0))
        low = (low + roll(low, step, 0)) + error
        high = sums
    return high, low


def reduce_column(rows, package):
    value = rows[...]
    count = value.shape[0]
    row, lane = iota(value.shape, 0), iota(value.shape, 1)
    place = row % 4
    following = roll(value, -4, 0)
    upper = [roll(value, -(2 * k + 1), 1) for k in range(4)]
    lower = [roll(following, -2 * k, 1) for k in range(4)]
    across = (
        upper[2] * line_smooth(lower[0] + 0.5 * lower[1])
        + upper[3] * line_smooth(0.5 * lower[0] + lower[1])
        + upper[0] * line_smooth(lower[2] + 0.5 * lower[3])
        + upper[1] * line_smooth(0.5 * lower[2] + lower[3])
    )
    counted = ((place == 1) | (place == 2)) & (lane % 32 == 0) & (row < count - 4)
    across = total(jnp.where(counted, across, 0.0))
    kept = jnp.where((place == 0) & (lane >= 16) & (lane < 20), value, 0.0)
    high, low = pair_rows(kept, jnp.zeros_like(kept))
    row, lane = iota((8, LANES), 0), iota((8, LANES), 1)
    high, error = two_sum(high, jnp.where(lane == 19, -across, 0.0))
    low = roll(low + error, 4, 1)
    fill(package, jnp.where(row % 2 == 0, high + low, 0.0))


def finish(rows, res, image, res_2, image_2, state, edges, second, last, increment, new_press):
    value = rows[...]
    lane = iota(value.shape, 1)
    high = jnp.where((lane >= 16) & (lane < 20), value, 0.0)
    low = roll(jnp.where((lane >= 20) & (lane < 24), value, 0.0), -4, 1)
    high, low = pair_rows(high, low)
    lane = iota((1, LANES), 1)

    def at_lane(part, k):
        return jnp.sum(jnp.where(lane == 16 + k, part[0:1], 0.0), axis=1, keepdims=True)

    m0, m1, m2, m3 = [two_sum(at_lane(high, k), at_lane(low, k)) for k in range(4)]
    alpha = pair_div(m0, m1)
    square = pair_mul(alpha, alpha)
    left = pair_add(pair_mul(square, m2), pair_scale(m0, -1.0))
    energy = pair_add(m1, pair_scale(pair_mul(alpha, m2), -2.0))
    energy = pair_add(energy, pair_mul(square, m3))
    left, alpha = left[0], alpha[0]
    beta = left / m0[0]
    energy = energy[0] - beta * left / alpha
    step = left / energy
    c_res = alpha + step * (1.0 + beta)
    c_im = -step * alpha
    for k in range(2):
        at = slice(k, k + 1)
        change = c_res * second[at, :] + c_im * last[at, :]
        press = state[10 + k : 11 + k, :]
        flag = state[8 + k : 9 + k, :]
        complement, slope = state[2 + k : 3 + k, :], state[4 + k : 5 + k, :]
        divisor = state[6 + k : 7 + k, :]
        new_press[at, :] = flag * (press - (complement + slope * change) / divisor)
    wide_res = jnp.broadcast_to(c_res, (8, LANES)).reshape(1, 8, LANES)
    wide_im = jnp.broadcast_to(c_im, (8, LANES)).reshape(1, 8, LANES)
    for c in range(3):
        for x in range(8):
            r = (res_2[0, x] if c == 2 else res[c, x]).reshape(4, 8, LANES)
            p = (image_2[0, x] if c == 2 else image[c, x]).reshape(4, 8, LANES)
            increment[0, c, x] = (wide_res * r + wide_im * p).reshape(32, LANES)
    for k in range(2):
        top = c_res * edges[1 + k : 2 + k, :] + c_im * last[9 + k : 10 + k, :]
        below = c_im * last[17 + k : 18 + k, :]
        wide = stack_rows([top, below, jnp.zeros((LANES - 2, LANES), F32)]).T
        for x in range(4):
            at = 4 * k + x
            increment[0, 2, at] = increment[0, 2, at] + wide[32 * x : 32 * x + 32]


def shifted(block, axis, step):
    count = lax.axis_size(axis)
    pairs = [(i, i + step) for i in range(count) if 0 <= i + step < count]
    return lax.ppermute(block, axis, pairs)


def on_device(disp, force, kappa, sigma, gap0, pressure, mortar, partner, active):
    nx, ny = lax.axis_size("gx"), lax.axis_size("gy")
    tile = (disp, force, kappa, sigma)
    whole = (8 * nx, LANES)
    row = ("body", "gx")

    def trade(package, axes):
        return lax.all_to_all(package, axes, 0, 0, tiled=True)

    slabs = (SLABS, 32, LANES)
    up, down, package = call(
        pack_x,
        [slabs, slabs, whole],
        tuple(pltpu.with_memory_space_constraint(a, pltpu.HBM) for a in (partner, *tile)),
        smem=(0,),
        away=range(1, 5),
        scratch=[(2, 8, 32, LANES)],
        more=[pltpu.SemaphoreType.DMA((18,))],
    )
    surfaces = trade(package, row)
    low_x, high_x = shifted(up, "gx", 1), shifted(down, "gx", -1)
    rims = (LINES, 24, LANES)
    up, down = call(pack_y, [rims, rims], (*tile, low_x, high_x))
    low_y, high_y = shifted(up, "gy", 1), shifted(down, "gy", -1)
    state = call(
        contact_first,
        (16, LANES),
        (partner, active, surfaces, gap0, pressure, mortar),
        smem=(0, 1),
    )
    lines = (LINES, ROWS, LANES)
    rims = (low_x, high_x, low_y, high_y)
    package = call(
        base_surface,
        whole,
        (*tile, *rims, state),
        scratch=[lines, lines, lines, lines, lines, (8, 32, LANES)],
    )
    rows = trade(package, row)
    res_2, image_2, moments, strips = base((2,), True)((*tile, *rims, package))
    half = 4 * nx
    work = [(half + 16, LANES), (half, LANES), (half, LANES)]
    edges, second, moved, message, package = call(
        contact_second,
        [(8, LANES), (8, LANES), (16, LANES), whole, whole],
        (partner, surfaces, rows, state, mortar, strips),
        smem=(0,),
        scratch=work,
    )
    pairs = [(j, j + 1) for j in range(ny - 1)] + [(ny + j + 1, ny + j) for j in range(ny - 1)]
    message = lax.ppermute(message, ("body", "gy"), pairs)
    beside = lax.all_gather(message, "body", axis=0, tiled=True)
    rows = trade(package, row)
    res, image, more_moments = base((0, 1), False)((*tile, *rims, edges))
    package, last = call(
        measure_moments,
        [(4 * ny, LANES), (24, LANES)],
        (partner, surfaces, rows, state, mortar, strips, edges, second, moved, beside, moments, more_moments),
        smem=(0,),
        scratch=work,
    )
    package = call(reduce_column, (4 * nx, LANES), (trade(package, "gy"),))
    sums = trade(package, row)
    increment, new_press = call(
        finish,
        [disp.shape, gap0.shape],
        (sums, res, image, res_2, image_2, state, edges, second, last),
    )
    return (increment, new_press)


def solution(mesh):
    placed = (
        P("body", None, "gx", "gy", None),
        P("body", None, "gx", "gy", None),
        P("body", "gx", "gy", None),
        P("body", "gx", "gy", None),
        P(("gx", "gy"), None),
        P(("gx", "gy"), None),
        P(("gx", "gy"), None, None),
        P(("gx", "gy")),
        P(("gx", "gy")),
    )
    return jax.shard_map(
        on_device,
        mesh=mesh,
        in_specs=placed,
        out_specs=(P("body", None, "gx", "gy", None), P(("gx", "gy"), None)),
        check_vma=False,
    )
```

```python
import jax
import jax.numpy as jnp
from jax import lax
from jax.experimental import pallas as pl
from jax.experimental.pallas import tpu as pltpu
from jax.sharding import PartitionSpec as P

HIGH = lax.Precision.HIGHEST
F32 = jnp.float32
LANES = 128
DEPTHS = (3, 3, 3, 3, 2, 2, 2, 2)
STARTS = (0, 3, 6, 9, 12, 14, 16, 18)
SLABS = 20
LINES = 14
ROWS = 48
KAP0, KAP1, DIA0, DIA1, RES0, IM0, IM1, SEC0, SEC1 = 0, 1, 2, 3, 4, 6, 7, 8, 9


def roll(value, step, axis):
    return pltpu.roll(value, step % value.shape[axis], axis)


def iota(shape, axis):
    return lax.broadcasted_iota(jnp.int32, shape, axis)


def call(body, outs, args, smem=(), away=(), far=(), scratch=(), more=(), limit=16):
    def space(i):
        return pltpu.SMEM if i in smem else pltpu.HBM if i in away else pltpu.VMEM

    specs = [pl.BlockSpec(memory_space=space(i)) for i in range(len(args))]
    many = isinstance(outs, list)
    shapes = [jax.ShapeDtypeStruct(s, F32) for s in (outs if many else [outs])]
    kept = [
        pl.BlockSpec(memory_space=pltpu.HBM if i in far else pltpu.VMEM) for i in range(len(shapes))
    ]
    return pl.pallas_call(
        body,
        out_shape=shapes if many else shapes[0],
        in_specs=specs,
        out_specs=kept if many else kept[0],
        scratch_shapes=[pltpu.VMEM(s, F32) for s in scratch] + list(more),
        compiler_params=pltpu.CompilerParams(vmem_limit_bytes=limit * 1024 * 1024),
    )(*args)


def fill(out, block):
    for at in range(0, out.shape[0], 8):
        out[at : at + 8, :] = block


def stack_rows(pieces):
    return jnp.concatenate(pieces, axis=0)


def tile_lines(disp, force, kappa, sigma):
    return (
        lambda x: disp[0, 0, x],
        lambda x: disp[0, 1, x],
        lambda x: disp[0, 2, x],
        lambda x: kappa[0, x],
        lambda x: force[0, 0, x],
        lambda x: force[0, 1, x],
        lambda x: force[0, 2, x],
        lambda x: sigma[0, x],
    )


def each(first, last):
    def run(body):
        for k in range(first, last):
            body(k)

    return run


def pack_x(partner, disp, force, kappa, sigma, up, down, package, surface, sems):
    sources = [disp.at[0, c] for c in range(3)] + [kappa.at[0]]
    sources += [force.at[0, c] for c in range(3)] + [sigma.at[0]]
    copies = [
        pltpu.make_async_copy(disp.at[0, 2], surface.at[0], sems.at[0]),
        pltpu.make_async_copy(kappa.at[0], surface.at[1], sems.at[1]),
    ]
    for k, (source, depth, start) in enumerate(zip(sources, DEPTHS, STARTS)):
        into = pl.ds(start, depth)
        at = 2 + 2 * k
        copies.append(
            pltpu.make_async_copy(source.at[pl.ds(8 - depth, depth)], up.at[into], sems.at[at])
        )
        copies.append(
            pltpu.make_async_copy(source.at[pl.ds(0, depth)], down.at[into], sems.at[at + 1])
        )
    for copy in copies:
        copy.start()
    for copy in copies[:2]:
        copy.wait()
    lanes = iota((LANES, LANES), 1)
    lane = iota((1, LANES), 1)
    first, second = [], []
    for k in range(2):
        field = surface[0, 4 * k : 4 * k + 4].reshape(LANES, LANES)
        kap = surface[1, 4 * k : 4 * k + 4].reshape(LANES, LANES)
        turned = jnp.where(lanes < 1, field, roll(kap, 1, 1)).T
        first.append(turned[0:1])
        place = surface_row(partner[k])
        hot = jnp.where(lane == 32 * (place // 16) + 1 + place % 16, 1.0, 0.0).astype(F32)
        second.append(jnp.where(edge_lanes(lane), turned[1:2], hot))
    four = stack_rows(first + second)
    fill(package, stack_rows([four, four]))
    for copy in copies[2:]:
        copy.wait()


def edge_lanes(lane):
    return (lane % 32 == 0) | (lane % 32 == 31)


def ext_line(line, low, high, field, x):
    depth, start = DEPTHS[field], STARTS[field]
    if x < 3:
        k = x - (3 - depth)
        return None if k < 0 else low[start + k]
    if x < 11:
        return line(x - 3)
    k = x - 11
    return None if k >= depth else high[start + k]


def pack_y(disp, force, kappa, sigma, low, high, up, down):
    lines = tile_lines(disp, force, kappa, sigma)
    sub = iota((8, LANES), 0)
    zero = jnp.zeros((8, LANES), F32)
    for x in range(LINES):
        last, first = [], []
        for field in range(8):
            value = ext_line(lines[field], low, high, field, x)
            last.append(zero if value is None else value[24:32])
            first.append(zero if value is None else value[0:8])
        for k, (a, b, c) in enumerate(((0, 1, 4), (2, 3, 5))):
            up[x, 8 * k : 8 * k + 8] = jnp.where(
                sub >= 5, last[a], jnp.where(sub >= 2, roll(last[b], -3, 0), roll(last[c], -6, 0))
            )
            down[x, 8 * k : 8 * k + 8] = jnp.where(
                sub < 3, first[a], jnp.where(sub < 6, roll(first[b], 3, 0), roll(first[c], 6, 0))
            )
        up[x, 16:24] = jnp.where(sub >= 6, last[7], roll(last[6], -2, 0))
        down[x, 16:24] = jnp.where(sub < 2, first[7], roll(first[6], 2, 0))


def turn(mortar, turned):
    for k in range(2):
        turned[k] = mortar[k].T


def vec_mat(row, matrix):
    column = jnp.broadcast_to(row, (LANES, LANES)).T
    return jnp.sum(column * matrix, axis=0, keepdims=True)


def surface_row(q):
    return 4 * (q // 2) + q % 2


def contact_first(partner, active, rows, gap0, pressure, mortar, turned, state):
    gx = lax.axis_index("gx")
    half = rows.shape[0] // 2
    for k in range(2):
        own = rows[pl.ds(4 * gx + k, 1), :]
        master = rows[pl.ds(half + surface_row(partner[k]), 1), :]
        matrix = mortar[k]
        press = pressure[k : k + 1, :]
        flag = jnp.full((1, LANES), active[k], jnp.int32).astype(F32)
        gap = gap0[k : k + 1, :] - own - vec_mat(master, turned[k])
        radius = jnp.sqrt(gap * gap + press * press + 0.01)
        complement = gap + press - radius
        slope_gap = 1.0 - gap / radius
        slope_press = 1.0 - press / radius
        divisor = slope_press + 0.5
        stiffness = flag * slope_gap / divisor
        excess = flag * complement / divisor
        traction = flag * press - excess
        state[k : k + 1, :] = stiffness
        state[2 + k : 3 + k, :] = complement
        state[4 + k : 5 + k, :] = slope_gap
        state[6 + k : 7 + k, :] = divisor
        state[8 + k : 9 + k, :] = flag
        state[10 + k : 11 + k, :] = press
        state[12 + k : 13 + k, :] = traction
        state[14 + k : 15 + k, :] = vec_mat(traction, matrix)


PLACES = ((0, 0, 0), (0, 3, -3), (1, 0, 0), (1, 3, -3), (0, 6, -6), (1, 6, -6), (2, 2, -2), (2, 0, 0))


def put_line(target, value, low_y, high_y, field, x):
    group, before, after = PLACES[field]
    part = slice(8 * group, 8 * group + 8)
    target[x, 0:8] = roll(low_y[x, part], before, 0)
    target[x, 8:40] = value
    target[x, 40:48] = roll(high_y[x, part], after, 0)


def plane_smoother():
    lane = iota((ROWS, LANES), 1)
    keep_low = jnp.where(lane > 0, 0.5, 0.0).astype(F32)
    keep_high = jnp.where(lane < LANES - 1, 0.5, 0.0).astype(F32)

    def in_plane(value):
        value = value + keep_low * roll(value, 1, 1) + keep_high * roll(value, -1, 1)
        return value + 0.5 * (roll(value, 1, 0) + roll(value, -1, 0))

    return in_plane


def along(ref, *at):
    *lead, x = at
    return ref[(*lead, x)] + 0.5 * (ref[(*lead, x - 1)] + ref[(*lead, x + 1)])


def base_surface(
    disp, force, kappa, sigma, low_x, high_x, low_y, high_y, state, package,
    moved, kap_lines, smooth_a, smooth_b, smooth_k, res,
):
    body = lax.axis_index("body")
    lines = tile_lines(disp, force, kappa, sigma)
    for x in range(2, LINES - 2):
        put_line(moved, ext_line(lines[2], low_x, high_x, 2, x), low_y, high_y, 2, x)
        put_line(kap_lines, ext_line(lines[3], low_x, high_x, 3, x), low_y, high_y, 3, x)
    in_plane = plane_smoother()

    @each(2, LINES - 2)
    def _(x):
        kap, value = kap_lines[x], moved[x]
        smooth_k[x] = in_plane(kap)
        smooth_a[x] = in_plane(value)
        smooth_b[x] = in_plane(kap * value)

    @each(0, 8)
    def _(k):
        x = k + 3
        kap = kap_lines[x]
        part = (8.0 * kap + along(smooth_k, x)) * moved[x] - kap * along(smooth_a, x) - along(smooth_b, x)
        res[k] = force[0, 2, k] - sigma[0, k] * moved[x, 8:40] - part[8:40]

    pieces = []
    for k in range(2):
        pieces.append(res[4 * k : 4 * k + 4].reshape(LANES, LANES).T[0:1])
    for k in range(2):
        pieces.append(jnp.where(body == 1, state[14 + k : 15 + k, :], state[12 + k : 13 + k, :]))
    four = stack_rows(pieces)
    fill(package, stack_rows([four, four]))


def base(comps, surface):
    count = len(comps)

    def kernel(disp, force, kappa, sigma, low_x, high_x, low_y, high_y, after, *rest):
        res_out, image_out, moments, *rest = rest
        if surface:
            strips, *rest = rest
        inputs, pushes, kap_lines, sig_lines, diag, res, image, smooth_a, smooth_b, smooth_k, second = rest
        gx, gy = lax.axis_index("gx"), lax.axis_index("gy")
        lines = tile_lines(disp, force, kappa, sigma)
        targets = [(c, inputs.at[k]) for k, c in enumerate(comps)]
        targets += [(4 + c, pushes.at[k]) for k, c in enumerate(comps)]
        targets += [(3, kap_lines), (7, sig_lines)]
        for field, target in targets:
            for x in range(LINES):
                value = ext_line(lines[field], low_x, high_x, field, x)
                if value is not None:
                    put_line(target, value, low_y, high_y, field, x)
        row = iota((ROWS, LANES), 0)
        in_plane = plane_smoother()
        row_low = jnp.where(gy == 0, 8, 0)
        row_high = jnp.where(gy == lax.axis_size("gy") - 1, 40, ROWS)
        inside_y = jnp.where((row >= row_low) & (row < row_high), 1.0, 0.0).astype(F32)
        line_low = jnp.where(gx == 0, 3, 0)
        line_high = jnp.where(gx == lax.axis_size("gx") - 1, 11, LINES)

        def inside(x):
            return inside_y * jnp.where((x >= line_low) & (x < line_high), 1.0, 0.0).astype(F32)

        def smooth_all(source, first):
            @each(first, LINES - first)
            def _(x):
                kap = kap_lines[x]
                if first == 0:
                    smooth_k[x] = in_plane(kap)
                for c in range(count):
                    value = source[c, x]
                    smooth_a[c, x] = in_plane(value)
                    smooth_b[c, x] = in_plane(kap * value)

        smooth_all(inputs, 0)

        @each(1, LINES - 1)
        def _(x):
            kap = kap_lines[x]
            dia = sig_lines[x] + 8.0 * kap + along(smooth_k, x)
            diag[x] = dia
            mask = inside(x)
            for c in range(count):
                value = pushes[c, x] - (
                    dia * inputs[c, x] - kap * along(smooth_a, c, x) - along(smooth_b, c, x)
                )
                res[c, x] = mask * value

        smooth_all(res, 1)

        @each(2, LINES - 2)
        def _(x):
            kap, dia = kap_lines[x], diag[x]
            mask = inside(x)
            for c in range(count):
                image[c, x] = mask * (
                    dia * res[c, x] - kap * along(smooth_a, c, x) - along(smooth_b, c, x)
                )

        smooth_all(image, 2)

        def finish_line(k, sums):
            x = k + 3
            kap, dia = kap_lines[x, 8:40], diag[x, 8:40]
            sums = list(sums)
            for c in range(count):
                r, p = res[c, x, 8:40], image[c, x, 8:40]
                q = dia * p - kap * along(smooth_a, c, x)[8:40] - along(smooth_b, c, x)[8:40]
                if surface:
                    second[k] = q
                res_out[c, k] = r
                image_out[c, k] = p
                for i, (a, b) in enumerate(((r, r), (r, p), (p, p), (p, q))):
                    product = (a * b).reshape(4, 8, LANES)
                    sums[i] = sums[i] + ((product[0] + product[1]) + (product[2] + product[3]))
            return tuple(sums)

        sums = (jnp.zeros((8, LANES), F32),) * 4
        for k in range(8):
            sums = finish_line(k, sums)
        for i in range(4):
            moments[i] = sums[i]
        if not surface:
            return
        strips[...] = jnp.zeros(strips.shape, F32)
        lanes = iota((LANES, LANES), 1)
        for group in range(4):
            near = [min(max(4 * group - 1 + k, 1), LINES - 2) for k in range(4)]
            wide = stack_rows([kap_lines[x, 8:40] for x in near])
            wide = jnp.where(lanes < 2, wide, roll(stack_rows([diag[x, 8:40] for x in near]), 2, 1))
            total_kinds = 4
            if group in (1, 2):
                total_kinds = 10
                for at, piece in (
                    (4, stack_rows([res[0, x, 8:40] for x in near])),
                    (6, stack_rows([image[0, x, 8:40] for x in near])),
                    (8, stack_rows([second[x - 3] for x in near])),
                ):
                    wide = jnp.where(lanes < at, wide, roll(piece, at, 1))
            turned = wide.T
            for kind in range(total_kinds):
                strips[kind, group : group + 1, :] = turned[kind : kind + 1]

    def run(args):
        lines, wide = (LINES, ROWS, LANES), (count, LINES, ROWS, LANES)
        own = (count, 8, 32, LANES)
        outs = [own, own, (4, 8, LANES)] + ([(16, 8, LANES)] if surface else [])
        return call(
            kernel,
            outs,
            args,
            scratch=[wide, wide, lines, lines, lines, wide, wide, wide, wide, lines, (8, 32, LANES)],
        )

    return run


def spread_row(select_rows, rows):
    half = rows.shape[0] // 2
    shape = (half, LANES)
    index, lane = iota(shape, 0) % 4, iota(shape, 1) % 32
    hot = (index >= 2) & (lane >= 1) & (lane <= 16)
    select = jnp.where(hot, select_rows[half:, :], 0.0)
    spots = lax.dot_general(
        select,
        rows[half:, :],
        (((0,), (0,)), ((), ())),
        precision=HIGH,
        preferred_element_type=F32,
    )
    size = min(half, 16)
    master = -stack_rows([spots[32 * k + 1 : 32 * k + 1 + size] for k in range(half // size)])
    slave = jnp.where(index < 2, -roll(rows[:half, :], -2, 0), 0.0)
    return slave, master


def edge_kappa(select_rows):
    value = roll(select_rows[...], -2, 0)
    shape = value.shape
    return jnp.where((iota(shape, 0) % 4 < 2) & edge_lanes(iota(shape, 1)), value, 0.0)


def row_line_smooth(value):
    row, lane = iota(value.shape, 0), iota(value.shape, 1)
    place, spot = row % 4, row % (value.shape[0] // 2)
    back, ahead = roll(value, 32, 1), roll(value, -32, 1)
    before = jnp.where(place == 0, roll(back, 3, 0), roll(back, 1, 0))
    before = jnp.where(spot == 0, 0.0, before)
    after = jnp.where(place == 0, roll(ahead, -1, 0), roll(ahead, -3, 0))
    after = jnp.where(spot == value.shape[0] // 2 - 3, 0.0, after)
    back = jnp.where(lane >= 32, back, before)
    ahead = jnp.where(lane < 96, ahead, after)
    return jnp.where(place < 2, value + 0.5 * (back + ahead), 0.0)


def own_extended(padded, gx):
    return stack_rows(
        [
            padded[pl.ds(4 * gx + 5, 1), :],
            padded[pl.ds(4 * gx + 8, 2), :],
            padded[pl.ds(4 * gx + 12, 1), :],
            jnp.zeros((4, LANES), F32),
        ]
    )


def put_padded(padded, value):
    half = value.shape[0]
    padded[0:8, :] = jnp.zeros((8, LANES), F32)
    padded[8 : 8 + half, :] = value
    padded[8 + half : 16 + half, :] = jnp.zeros((8, LANES), F32)


def contact_second(
    partner, select_rows, rows, state, mortar, turned, strips,
    edges, out, moved, message, package, padded, surf0, surf1,
):
    body, gx = lax.axis_index("body"), lax.axis_index("gx")
    half = rows.shape[0] // 2
    slave, master = spread_row(select_rows, rows)
    put_padded(padded, jnp.where(body == 0, slave, master))
    surf0[...] = rows[:half, :] + slave
    surf1[...] = rows[half:, :] + master
    first = own_extended(padded, gx)
    edges[...] = first
    both = stack_rows([slave, master])
    scaled = edge_kappa(select_rows) * both
    y = iota(both.shape, 1) % 32
    scaled = jnp.where(y == 1, roll(scaled, 1, 1), jnp.where(y == 30, roll(scaled, -1, 1), 0.0))
    message[...] = jnp.where((y == 0) | (y == 31), both, scaled)
    sent = []
    for k in range(2):
        matrix = mortar[k]
        gap = -surf0[pl.ds(4 * gx + k, 1), :] - vec_mat(
            surf1[pl.ds(surface_row(partner[k]), 1), :], turned[k]
        )
        push = state[k : k + 1, :] * gap
        pulled = vec_mat(push, matrix)
        out[k : k + 1, :] = gap
        out[2 + k : 3 + k, :] = push
        sent.append(jnp.where(body == 1, pulled, push))
    out[4:8, :] = jnp.zeros((4, LANES), F32)
    plain = line_smooth(row_smooth(first))
    weighted = line_smooth(row_smooth(strips[KAP0] * first))
    mask = inside_rows()
    top = jnp.where(mask, strips[DIA0] * first - strips[KAP0] * plain - weighted, 0.0)
    moved[0:8, :] = top
    moved[8:16, :] = jnp.where(mask, -0.5 * (strips[KAP1] * plain + weighted), 0.0)
    four = stack_rows([(strips[IM0] + top)[1:3]] + sent)
    fill(package, stack_rows([four, four]))


def inside_rows():
    gx = lax.axis_index("gx")
    row = iota((8, LANES), 0)
    lowest = jnp.where(gx == 0, 1, 0)
    highest = jnp.where(gx == lax.axis_size("gx") - 1, 3, 4)
    return (row >= lowest) & (row < highest)


def line_smooth(value):
    lane = iota(value.shape, 1)
    back, ahead = roll(value, 32, 1), roll(value, -32, 1)
    back = jnp.where(lane >= 32, back, roll(back, 1, 0))
    ahead = jnp.where(lane < 96, ahead, roll(ahead, -1, 0))
    return value + 0.5 * (back + ahead)


def row_smooth(value):
    y = iota(value.shape, 1) % 32
    before = jnp.where(y > 0, roll(value, 1, 1), 0.0)
    after = jnp.where(y < 31, roll(value, -1, 1), 0.0)
    return value + 0.5 * (before + after)


def total(value):
    return jnp.sum(jnp.sum(value, axis=1, keepdims=True), axis=0, keepdims=True)


def measure_moments(
    partner, select_rows, rows, state, turned, strips, edges, second, moved, beside,
    moments, more_moments, package, image_out, padded, surf0, surf1,
):
    body, gx = lax.axis_index("body"), lax.axis_index("gx")
    half = rows.shape[0] // 2
    slave, master = spread_row(select_rows, rows)
    y = iota(rows.shape, 1) % 32
    below_row, above_row = beside[: 2 * half, :], beside[2 * half :, :]
    plain = jnp.where(y == 0, roll(below_row, -31, 1), jnp.where(y == 31, roll(above_row, 31, 1), 0.0))
    scaled = jnp.where(y == 0, roll(below_row, -30, 1), jnp.where(y == 31, roll(above_row, 30, 1), 0.0))
    plain, scaled = row_line_smooth(plain), row_line_smooth(scaled)
    added = -0.5 * (edge_kappa(select_rows) * plain + scaled)
    surf0[...] = rows[:half, :] + slave + added[:half]
    surf1[...] = rows[half:, :] + master + added[half:]

    def own_rows(value):
        put_padded(padded, jnp.where(body == 0, value[:half], value[half:]))
        return own_extended(padded, gx)

    plain, scaled = own_rows(plain), own_rows(scaled)
    put_padded(padded, jnp.where(body == 0, slave, master))
    mask = inside_rows()
    kap0, kap1 = strips[KAP0], strips[KAP1]
    first = edges[...]
    k_first = moved[0:8, :] - jnp.where(mask, 0.5 * (kap0 * plain + scaled), 0.0)
    top = k_first + own_extended(padded, gx)
    below = moved[8:16, :] - jnp.where(mask, 0.25 * (kap1 * plain + scaled), 0.0)
    once = jnp.where(body == 0, 1.0, 0.0).astype(F32)
    push_sum = jnp.zeros((1, LANES), F32)
    gap_sum = jnp.zeros((1, LANES), F32)
    for k in range(2):
        gap = -surf0[pl.ds(4 * gx + k, 1), :] - vec_mat(
            surf1[pl.ds(surface_row(partner[k]), 1), :], turned[k]
        )
        image_out[k : k + 1, :] = gap
        push_sum = push_sum + second[k : k + 1, :] * second[2 + k : 3 + k, :]
        gap_sum = gap_sum + state[k : k + 1, :] * gap * gap
    image_out[2:8, :] = jnp.zeros((6, LANES), F32)
    image_out[8:16, :] = top
    image_out[16:24, :] = below
    row = iota((8, LANES), 0)
    own = (row == 1) | (row == 2)

    def surface_sum(value):
        return total(jnp.where(own, value, 0.0))

    im0, im1 = strips[IM0], strips[IM1]
    mu0 = total(moments[0] + more_moments[0]) + surface_sum(first * (2.0 * strips[RES0] + first))
    mu1 = total(moments[1] + more_moments[1]) + surface_sum(first * (2.0 * im0 + k_first)) + once * total(push_sum)
    mu2 = total(moments[2] + more_moments[2]) + surface_sum(top * (2.0 * im0 + top) + below * (2.0 * im1 + below))
    t_top = line_smooth(row_smooth(top + 0.5 * below))
    t_below = line_smooth(row_smooth(0.5 * top + below))
    mu3 = (
        total(moments[3] + more_moments[3])
        + surface_sum(
            top * (2.0 * strips[SEC0] + strips[DIA0] * top - 2.0 * kap0 * t_top)
            + below * (2.0 * strips[SEC1] + strips[DIA1] * below - 2.0 * kap1 * t_below)
        )
        + once * total(gap_sum)
    )
    lane = iota((8, LANES), 1)
    y = lane % 32
    send = jnp.zeros((8, LANES), F32)
    for k, value in enumerate((top, below, kap0 * top, kap1 * below)):
        send = send + jnp.where(y == 2 * k, roll(value, 2 * k, 1), 0.0)
        send = send + jnp.where(y == 2 * k + 1, roll(value, 2 * k + 1 - 31, 1), 0.0)
    for k, value in enumerate((mu0, mu1, mu2, mu3)):
        send = send + jnp.where((row == 0) & (lane == 16 + k), value, 0.0)
    send = send[0:4]
    fill(package, stack_rows([send, send]))


def two_sum(a, b):
    total_of = a + b
    shift = total_of - a
    return total_of, (a - (total_of - shift)) + (b - shift)


def halves(a):
    big = 4097.0 * a
    high = big - (big - a)
    return high, a - high


def pair_add(x, y):
    high, low = two_sum(x[0], y[0])
    return two_sum(high, low + (x[1] + y[1]))


def pair_mul(x, y):
    product = x[0] * y[0]
    a, b = halves(x[0])
    c, d = halves(y[0])
    error = ((a * c - product) + a * d + b * c) + b * d
    return two_sum(product, error + (x[0] * y[1] + x[1] * y[0]))


def pair_scale(x, factor):
    return x[0] * factor, x[1] * factor


def pair_div(x, y):
    first = x[0] / y[0]
    zero = jnp.zeros_like(first)
    rest = pair_add(x, pair_scale(pair_mul(y, (first, zero)), -1.0))
    return two_sum(first, rest[0] / y[0])


def pair_rows(high, low):
    while high.shape[0] > 8:
        half = high.shape[0] // 2
        sums, error = two_sum(high[:half], high[half:])
        low = (low[:half] + low[half:]) + error
        high = sums
    for step in (4, 2, 1):
        sums, error = two_sum(high, roll(high, step, 0))
        low = (low + roll(low, step, 0)) + error
        high = sums
    return high, low


def reduce_column(rows, package):
    value = rows[...]
    count = value.shape[0]
    row, lane = iota(value.shape, 0), iota(value.shape, 1)
    place = row % 4
    following = roll(value, -4, 0)
    upper = [roll(value, -(2 * k + 1), 1) for k in range(4)]
    lower = [roll(following, -2 * k, 1) for k in range(4)]
    across = (
        upper[2] * line_smooth(lower[0] + 0.5 * lower[1])
        + upper[3] * line_smooth(0.5 * lower[0] + lower[1])
        + upper[0] * line_smooth(lower[2] + 0.5 * lower[3])
        + upper[1] * line_smooth(0.5 * lower[2] + lower[3])
    )
    counted = ((place == 1) | (place == 2)) & (lane % 32 == 0) & (row < count - 4)
    across = total(jnp.where(counted, across, 0.0))
    kept = jnp.where((place == 0) & (lane >= 16) & (lane < 20), value, 0.0)
    high, low = pair_rows(kept, jnp.zeros_like(kept))
    row, lane = iota((8, LANES), 0), iota((8, LANES), 1)
    high, error = two_sum(high, jnp.where(lane == 19, -across, 0.0))
    low = roll(low + error, 4, 1)
    fill(package, jnp.where(row % 2 == 0, high + low, 0.0))


def finish(rows, res, image, res_2, image_2, state, edges, second, last, increment, new_press):
    value = rows[...]
    lane = iota(value.shape, 1)
    high = jnp.where((lane >= 16) & (lane < 20), value, 0.0)
    low = roll(jnp.where((lane >= 20) & (lane < 24), value, 0.0), -4, 1)
    high, low = pair_rows(high, low)
    lane = iota((1, LANES), 1)

    def at_lane(part, k):
        return jnp.sum(jnp.where(lane == 16 + k, part[0:1], 0.0), axis=1, keepdims=True)

    m0, m1, m2, m3 = [two_sum(at_lane(high, k), at_lane(low, k)) for k in range(4)]
    alpha = pair_div(m0, m1)
    square = pair_mul(alpha, alpha)
    left = pair_add(pair_mul(square, m2), pair_scale(m0, -1.0))
    energy = pair_add(m1, pair_scale(pair_mul(alpha, m2), -2.0))
    energy = pair_add(energy, pair_mul(square, m3))
    left, alpha = left[0], alpha[0]
    beta = left / m0[0]
    energy = energy[0] - beta * left / alpha
    step = left / energy
    c_res = alpha + step * (1.0 + beta)
    c_im = -step * alpha
    for k in range(2):
        at = slice(k, k + 1)
        change = c_res * second[at, :] + c_im * last[at, :]
        press = state[10 + k : 11 + k, :]
        flag = state[8 + k : 9 + k, :]
        complement, slope = state[2 + k : 3 + k, :], state[4 + k : 5 + k, :]
        divisor = state[6 + k : 7 + k, :]
        new_press[at, :] = flag * (press - (complement + slope * change) / divisor)
    wide_res = jnp.broadcast_to(c_res, (8, LANES)).reshape(1, 8, LANES)
    wide_im = jnp.broadcast_to(c_im, (8, LANES)).reshape(1, 8, LANES)
    for c in range(3):
        for x in range(8):
            r = (res_2[0, x] if c == 2 else res[c, x]).reshape(4, 8, LANES)
            p = (image_2[0, x] if c == 2 else image[c, x]).reshape(4, 8, LANES)
            increment[0, c, x] = (wide_res * r + wide_im * p).reshape(32, LANES)
    for k in range(2):
        top = c_res * edges[1 + k : 2 + k, :] + c_im * last[9 + k : 10 + k, :]
        below = c_im * last[17 + k : 18 + k, :]
        wide = stack_rows([top, below, jnp.zeros((LANES - 2, LANES), F32)]).T
        for x in range(4):
            at = 4 * k + x
            increment[0, 2, at] = increment[0, 2, at] + wide[32 * x : 32 * x + 32]


def shifted(block, axis, step):
    count = lax.axis_size(axis)
    pairs = [(i, i + step) for i in range(count) if 0 <= i + step < count]
    return lax.ppermute(block, axis, pairs)


def on_device(disp, force, kappa, sigma, gap0, pressure, mortar, partner, active):
    nx, ny = lax.axis_size("gx"), lax.axis_size("gy")
    tile = (disp, force, kappa, sigma)
    whole = (8 * nx, LANES)
    row = ("body", "gx")

    def trade(package, axes):
        return lax.all_to_all(package, axes, 0, 0, tiled=True)

    slabs = (SLABS, 32, LANES)
    up, down, package = call(
        pack_x,
        [slabs, slabs, whole],
        tuple(pltpu.with_memory_space_constraint(a, pltpu.HBM) for a in (partner, *tile)),
        smem=(0,),
        away=range(1, 5),
        scratch=[(2, 8, 32, LANES)],
        more=[pltpu.SemaphoreType.DMA((18,))],
    )
    surfaces = trade(package, row)
    low_x, high_x = shifted(up, "gx", 1), shifted(down, "gx", -1)
    rims = (LINES, 24, LANES)
    up, down = call(pack_y, [rims, rims], (*tile, low_x, high_x))
    low_y, high_y = shifted(up, "gy", 1), shifted(down, "gy", -1)
    turned = call(turn, mortar.shape, (mortar,))
    state = call(
        contact_first,
        (16, LANES),
        (partner, active, surfaces, gap0, pressure, mortar, turned),
        smem=(0, 1),
    )
    lines = (LINES, ROWS, LANES)
    rims = (low_x, high_x, low_y, high_y)
    package = call(
        base_surface,
        whole,
        (*tile, *rims, state),
        scratch=[lines, lines, lines, lines, lines, (8, 32, LANES)],
    )
    rows = trade(package, row)
    res_2, image_2, moments, strips = base((2,), True)((*tile, *rims, package))
    half = 4 * nx
    work = [(half + 16, LANES), (half, LANES), (half, LANES)]
    edges, second, moved, message, package = call(
        contact_second,
        [(8, LANES), (8, LANES), (16, LANES), whole, whole],
        (partner, surfaces, rows, state, mortar, turned, strips),
        smem=(0,),
        scratch=work,
    )
    pairs = [(j, j + 1) for j in range(ny - 1)] + [(ny + j + 1, ny + j) for j in range(ny - 1)]
    message = lax.ppermute(message, ("body", "gy"), pairs)
    beside = lax.all_gather(message, "body", axis=0, tiled=True)
    rows = trade(package, row)
    res, image, more_moments = base((0, 1), False)((*tile, *rims, edges))
    package, last = call(
        measure_moments,
        [(4 * ny, LANES), (24, LANES)],
        (partner, surfaces, rows, state, turned, strips, edges, second, moved, beside, moments, more_moments),
        smem=(0,),
        scratch=work,
    )
    package = call(reduce_column, (4 * nx, LANES), (trade(package, "gy"),))
    sums = trade(package, row)
    increment, new_press = call(
        finish,
        [disp.shape, gap0.shape],
        (sums, res, image, res_2, image_2, state, edges, second, last),
    )
    return (increment, new_press)


def solution(mesh):
    placed = (
        P("body", None, "gx", "gy", None),
        P("body", None, "gx", "gy", None),
        P("body", "gx", "gy", None),
        P("body", "gx", "gy", None),
        P(("gx", "gy"), None),
        P(("gx", "gy"), None),
        P(("gx", "gy"), None, None),
        P(("gx", "gy")),
        P(("gx", "gy")),
    )
    return jax.shard_map(
        on_device,
        mesh=mesh,
        in_specs=placed,
        out_specs=(P("body", None, "gx", "gy", None), P(("gx", "gy"), None)),
        check_vma=False,
    )
```
